128 devices in a mesh: seq: 4 (over x), head: 8 (over y_hi, z), rows: 4 (over y_lo, core).
Axes of the slice: x: 4, y: 4 (y_hi: 2, y_lo: 2; y = y_hi * 2 + y_lo), z: 4, core: 2. Of those that a mesh axis runs over, the one named last changes fastest.
Arguments:
- tokens: bfloat16 [16384, 1024], P(('seq', 'head', 'rows')), may hold values from -6 to 6
- lengths: int32 [4, 2], P('seq'), may hold values from 512 to 3584, as said below
- w_query: bfloat16 [1024, 2048], P('rows', 'head'), may hold values from -0.1875 to 0.1875
- w_key: bfloat16 [1024, 1024], P('rows'), may hold values from -0.1875 to 0.1875
- w_value: bfloat16 [1024, 1024], P('rows'), may hold values from -0.1875 to 0.1875
- w_output: bfloat16 [1024, 2048], P('rows', 'head'), may hold values from -0.125 to 0.125
- w_gate: bfloat16 [1024, 3072], P('rows', 'head'), may hold values from -0.1875 to 0.1875
- w_up: bfloat16 [1024, 3072], P('rows', 'head'), may hold values from -0.1875 to 0.1875
- w_down: bfloat16 [1024, 3072], P('rows', 'head'), may hold values from -0.109375 to 0.109375
- gain_attn_in: float32 [1024], replicated, may hold values from 0.5 to 1.5
- gain_attn_out: float32 [1024], replicated, may hold values from 0.5 to 1.5
- gain_mlp_in: float32 [1024], replicated, may hold values from 0.5 to 1.5
- gain_mlp_out: float32 [1024], replicated, may hold values from 0.5 to 1.5
- out_grad: bfloat16 [16384, 1024], P(('seq', 'head', 'rows')), may hold values from -6 to 6
Outputs:
- mixed: bfloat16 [16384, 1024], P(('seq', 'head', 'rows'))
- tokens_grad: bfloat16 [16384, 1024], P(('seq', 'head', 'rows'))
- w_query_grad: float32 [1024, 2048], P(('seq', 'rows'), 'head')
- w_key_grad: float32 [1024, 1024], P(('seq', 'head', 'rows'))
- w_value_grad: float32 [1024, 1024], P(('seq', 'head', 'rows'))
- w_output_grad: float32 [1024, 2048], P(('seq', 'rows'), 'head')
- w_gate_grad: float32 [1024, 3072], P(('seq', 'rows'), 'head')
- w_up_grad: float32 [1024, 3072], P(('seq', 'rows'), 'head')
- w_down_grad: float32 [1024, 3072], P(('seq', 'rows'), 'head')
- gain_attn_in_grad: float32 [1024], P(('seq', 'head', 'rows'))
- gain_attn_out_grad: float32 [1024], P(('seq', 'head', 'rows'))
- gain_mlp_in_grad: float32 [1024], P(('seq', 'head', 'rows'))
- gain_mlp_out_grad: float32 [1024], P(('seq', 'head', 'rows'))
The draws below stay inside these ranges and needn't reach their ends.
Inputs may be any that keep to these rules, and one draw needn't show every extreme that they name: Row t lists the lengths of the 2 documents of bucket t in order; they add up to 4096, and one of them is longer than 3072.
All inputs are finite; a program needn't handle non-finite values.
Results may differ from the reference program's by a relative error of at most 0.034.
Values may be sent and summed in bfloat16 or wider, within the bound.
A program may use at most 256 MiB of HBM per device.

```python
import math
import jax
import jax.numpy as jnp
from jax import lax

D = 1024
H = 16
KV = 8
DH = 128
FF = 3072
BUCKET = 4096
QEXP_MODEL = 10
QEXP_HIDDEN = 11
BUCKETS = 4
TOKENS = 16384


def draw_lengths(key, part):
    key = jax.random.fold_in(key, 7)
    key_short, key_flip, key_chosen = jax.random.split(key, 3)
    short_len = jax.random.randint(key_short, (BUCKETS,), BUCKET // 8, BUCKET // 4)
    chosen = jax.random.randint(key_chosen, (), 0, BUCKETS)
    short_len = jnp.where(jnp.arange(BUCKETS) == chosen, BUCKET // 8, short_len)
    flipped = jax.random.randint(key_flip, (BUCKETS,), 0, 2)
    first_len = jnp.where(flipped == 1, short_len, BUCKET - short_len)
    second_len = BUCKET - first_len
    return jnp.stack([first_len, second_len], axis=1).astype(jnp.int32)


def level_of(stream_key, extent, cuts, low, top_value):
    gain = 1.0
    for axis_at, shards_of in cuts:
        steps = jax.random.uniform(jax.random.fold_in(jax.random.fold_in(stream_key, 6), axis_at), (shards_of,), jnp.float32, low / len(cuts), top_value / len(cuts))
        gain = gain * jnp.repeat(jnp.exp(steps), extent[axis_at] // shards_of).reshape((-1,) + (1,) * (len(extent) - 1 - axis_at))
    return gain


def centred(stream_key, shape, width, bound, shards=(), kind=jnp.bfloat16):
    loudness = level_of(stream_key, shape, shards, -0.22, 0.18) if shards else 1.0
    drawn = jax.random.normal(stream_key, shape, jnp.float32) * width * loudness
    return jnp.minimum(jnp.maximum(drawn, -bound), bound).astype(kind)


def setup_inputs(seed: int = 0) -> dict:
    splits = jax.random.split(jax.random.key(seed), 15)
    return {
        "tokens": centred(splits[0], (TOKENS, D), 1.0, 6.0, ((0, 128),)),
        "lengths": draw_lengths(jax.random.fold_in(splits[14], 71), 0),
        "w_query": centred(splits[2], (D, H * DH), D ** -0.5, 0.1875, ((0, 4), (1, 8))),
        "w_key": centred(splits[3], (D, KV * DH), D ** -0.5, 0.1875, ((0, 4),)),
        "w_value": centred(splits[4], (D, KV * DH), D ** -0.5, 0.1875, ((0, 4),)),
        "w_output": centred(splits[5], (D, H * DH), (H * DH) ** -0.5, 0.125, ((0, 4), (1, 8))),
        "w_gate": centred(splits[6], (D, FF), D ** -0.5, 0.1875, ((0, 4), (1, 8))),
        "w_up": centred(splits[7], (D, FF), D ** -0.5, 0.1875, ((0, 4), (1, 8))),
        "w_down": centred(splits[8], (D, FF), FF ** -0.5, 0.109375, ((0, 4), (1, 8))),
        "gain_attn_in": jnp.clip(1.0 + 0.1 * jax.random.normal(splits[9], (D,), jnp.float32), 0.5, 1.5),
        "gain_attn_out": jnp.clip(1.0 + 0.1 * jax.random.normal(splits[10], (D,), jnp.float32), 0.5, 1.5),
        "gain_mlp_in": jnp.clip(1.0 + 0.1 * jax.random.normal(splits[11], (D,), jnp.float32), 0.5, 1.5),
        "gain_mlp_out": jnp.clip(1.0 + 0.1 * jax.random.normal(splits[12], (D,), jnp.float32), 0.5, 1.5),
        "out_grad": centred(splits[13], (TOKENS, D), 1.0, 6.0, ((0, 128),)),
    }


CAP = 50.0
EPSILON = 1e-06
THETA = 10000.0
HIGH = lax.Precision.HIGHEST

@jax.custom_vjp
def low(v):
    return lax.optimization_barrier(v.astype(jnp.bfloat16)).astype(jnp.float32)

@jax.custom_vjp
def low_back(v):
    return v

def low_keep(v):
    return (low(v), None)

def low_pass(kept, grad):
    return (grad,)

def back_keep(v):
    return (v, None)

def back_low(kept, grad):
    return (low(grad),)
low.defvjp(low_keep, low_pass)
low_back.defvjp(back_keep, back_low)

def quantize(weight, exponent, bit_count):
    bit_shift = 8 - bit_count
    scaled = jnp.floor(weight.astype(jnp.float32) * 2.0 ** exponent)
    int_codes = jnp.clip(scaled.astype(jnp.int32) + 128, 0, 255)
    if bit_shift > 0:
        levels = jnp.minimum((int_codes + 2 ** (bit_shift - 1)) // 2 ** bit_shift, 2 ** bit_count - 1) * 2 ** bit_shift
    else:
        levels = int_codes
    return (levels - 128).astype(jnp.float32) * 2.0 ** (-exponent)

def rms_norm(values, gain_vec):
    return values * lax.rsqrt(lax.optimization_barrier(jnp.mean(values * values, axis=-1, keepdims=True)) + EPSILON) * gain_vec

def rope_tables(positions, head_size):
    half_size = head_size // 2
    freqs = jnp.exp(jnp.arange(half_size, dtype=jnp.float32) * (-2.0 * math.log(THETA) / head_size))
    angles = positions.astype(jnp.float32)[:, None] * freqs[None, :]
    return (jnp.cos(angles), jnp.sin(angles))

def rotate(values, cosine, sine):
    half_size = values.shape[-1] // 2
    first_half = values[..., :half_size]
    second_half = values[..., half_size:]
    cos_b = cosine[:, None, :]
    sin_b = sine[:, None, :]
    return jnp.concatenate([first_half * cos_b - second_half * sin_b, second_half * cos_b + first_half * sin_b], axis=-1)

def token_docs(token_ids, length_row):
    seq_ends = jnp.cumsum(length_row)
    passed = token_ids[:, None] >= seq_ends[None, :]
    doc_ids = lax.optimization_barrier(jnp.sum(passed.astype(jnp.int32), axis=1))
    starts = lax.optimization_barrier(jnp.sum(jnp.where(passed, length_row[None, :], 0), axis=1))
    return (doc_ids, token_ids - starts)

def layer(inputs, w_query, w_key, w_value, w_output, w_gate, w_up, w_down, gain_attn_in, gain_attn_out, gain_mlp_in, gain_mlp_out, visible, positions):
    count_tok = inputs.shape[0]
    normed = low(rms_norm(inputs, gain_attn_in))
    cosine, sine = rope_tables(positions, DH)
    query_lin = low_back(jnp.dot(normed, w_query, precision=HIGH).reshape(count_tok, H, DH))
    key_lin = low_back(rotate(jnp.dot(normed, w_key, precision=HIGH).reshape(count_tok, KV, DH), cosine, sine))
    value_lin = low_back(jnp.dot(normed, w_value, precision=HIGH).reshape(count_tok, KV, DH))
    queries = low(rotate(query_lin, cosine, sine) * DH ** (-0.5))
    keys_rot = jnp.repeat(low(key_lin), H // KV, axis=1)
    values_low = jnp.repeat(low(value_lin), H // KV, axis=1)
    raw_scores = low_back(jnp.einsum('qhd,khd->hqk', queries, keys_rot, precision=HIGH))
    curved = jnp.tanh(raw_scores / CAP)
    capped = jnp.where(visible[None], CAP * curved, -1e+30)
    row_peak = lax.optimization_barrier(jnp.max(capped, axis=-1, keepdims=True))
    exp_scores = jnp.exp(capped - row_peak)
    attn_probs = exp_scores / lax.optimization_barrier(jnp.sum(exp_scores, axis=-1, keepdims=True))
    attended = jnp.einsum('hqk,khd->qhd', low(attn_probs), values_low, precision=HIGH)
    attended = low(low_back(attended)).reshape(count_tok, H * DH)
    branch = low_back(jnp.dot(attended, w_output.T, precision=HIGH))
    mixed_h = inputs + rms_norm(branch, gain_attn_out)
    normed_mlp = low(rms_norm(mixed_h, gain_mlp_in))
    gate = low_back(jnp.dot(normed_mlp, w_gate, precision=HIGH))
    up_proj = low_back(jnp.dot(normed_mlp, w_up, precision=HIGH))
    hidden = low(jax.nn.gelu(gate, approximate=True) * up_proj)
    mlp_out = low_back(jnp.dot(hidden, w_down.T, precision=HIGH))
    return mixed_h + rms_norm(mlp_out, gain_mlp_out)

def reference(tokens, lengths, w_query, w_key, w_value, w_output, w_gate, w_up, w_down, gain_attn_in, gain_attn_out, gain_mlp_in, gain_mlp_out, out_grad):
    params = (quantize(w_query, QEXP_MODEL, 8), quantize(w_key, QEXP_MODEL, 8), quantize(w_value, QEXP_MODEL, 8), quantize(w_output, QEXP_MODEL, 8), quantize(w_gate, QEXP_MODEL, 4), quantize(w_up, QEXP_MODEL, 4), quantize(w_down, QEXP_HIDDEN, 2), gain_attn_in.astype(jnp.float32), gain_attn_out.astype(jnp.float32), gain_mlp_in.astype(jnp.float32), gain_mlp_out.astype(jnp.float32))
    token_ids = jnp.arange(BUCKET, dtype=jnp.int32)

    def one_bucket(totals, items):
        bucket_x, length_row, bucket_dy = items
        doc_ids, positions = token_docs(token_ids, length_row)
        visible = (doc_ids[:, None] == doc_ids[None, :]) & (token_ids[None, :] <= token_ids[:, None])

        def apply_layer(inputs, *params_in):
            return layer(inputs, *params_in, visible, positions)
        mixed_b, back_fn = jax.vjp(apply_layer, bucket_x.astype(jnp.float32), *params)
        grads = back_fn(bucket_dy.astype(jnp.float32))
        totals = tuple((running + piece_grad for running, piece_grad in zip(totals, grads[1:])))
        return (totals, (mixed_b.astype(jnp.bfloat16), grads[0].astype(jnp.bfloat16)))
    initial = tuple((jnp.zeros_like(param) for param in params))
    totals, outputs = lax.scan(one_bucket, initial, (tokens.reshape(BUCKETS, BUCKET, D), lengths, out_grad.reshape(BUCKETS, BUCKET, D)))
    mixed_all, input_grads = outputs
    return (mixed_all.reshape(TOKENS, D), input_grads.reshape(TOKENS, D), totals[0], totals[1], totals[2], totals[3], totals[4], totals[5], totals[6], totals[7], totals[8], totals[9], totals[10])
```

```python
import math

import jax
import jax.numpy as jnp
from jax import lax
from jax.sharding import PartitionSpec as P

DH = 128
QEXP_MODEL = 10
QEXP_HIDDEN = 11


CAP = 50.0
EPSILON = 1e-06
THETA = 10000.0


def quantize(weight, exponent, bit_count):
    bit_shift = 8 - bit_count
    scaled = jnp.floor(weight.astype(jnp.float32) * 2.0**exponent)
    int_codes = jnp.clip(scaled.astype(jnp.int32) + 128, 0, 255)
    if bit_shift > 0:
        levels = (
            jnp.minimum((int_codes + 2 ** (bit_shift - 1)) // 2**bit_shift, 2**bit_count - 1)
            * 2**bit_shift
        )
    else:
        levels = int_codes
    return ((levels - 128).astype(jnp.float32) * 2.0 ** (-exponent)).astype(jnp.bfloat16)


def rms_norm(values, gain_vec):
    return (
        values * lax.rsqrt(jnp.mean(values * values, axis=-1, keepdims=True) + EPSILON) * gain_vec
    )


def rope_tables(positions, head_size):
    half_size = head_size // 2
    freqs = jnp.exp(jnp.arange(half_size, dtype=jnp.float32) * (-2.0 * math.log(THETA) / head_size))
    angles = positions.astype(jnp.float32)[:, None] * freqs[None, :]
    return (jnp.cos(angles), jnp.sin(angles))


def rotate(values, cosine, sine):
    half_size = values.shape[-1] // 2
    first_half = values[..., :half_size]
    second_half = values[..., half_size:]
    cos_b = cosine[:, None, :]
    sin_b = sine[:, None, :]
    return jnp.concatenate(
        [first_half * cos_b - second_half * sin_b, second_half * cos_b + first_half * sin_b],
        axis=-1,
    )


def rotate_back(incoming, cosine, sine):
    half_size = incoming.shape[-1] // 2
    first_half = incoming[..., :half_size]
    second_half = incoming[..., half_size:]
    cos_b = cosine[:, None, :]
    sin_b = sine[:, None, :]
    return jnp.concatenate(
        [first_half * cos_b + second_half * sin_b, second_half * cos_b - first_half * sin_b],
        axis=-1,
    )


def token_docs(token_ids, length_row):
    seq_ends = jnp.cumsum(length_row)
    passed = token_ids[:, None] >= seq_ends[None, :]
    doc_ids = jnp.sum(passed.astype(jnp.int32), axis=1)
    starts = jnp.sum(jnp.where(passed, length_row[None, :], 0), axis=1)
    return (doc_ids, token_ids - starts)


def times_transposed(left, right):
    return lax.dot_general(
        left, right, (((1,), (1,)), ((), ())), preferred_element_type=jnp.float32
    )


def outer_sum(left, right):
    return lax.dot_general(
        left, right, (((0,), (0,)), ((), ())), preferred_element_type=jnp.float32
    )


def gather_heads(values):
    return lax.all_gather(values, "head", axis=0, tiled=True)


def sum_heads(term_fn, tok_block):
    return lax.psum_scatter(
        term_fn(jnp.int32(0), tok_block * lax.axis_size("head")).astype(jnp.bfloat16),
        "head",
        scatter_dimension=0,
        tiled=True,
    ).astype(jnp.float32)


def gather_keys(key_part, value_part):
    return (
        lax.all_gather(key_part, "rows", axis=0, tiled=True),
        lax.all_gather(value_part, "rows", axis=0, tiled=True),
    )


def attention_probs(query_b, keys_b, visible, kv_heads, group):
    query_count = query_b.shape[0]
    grouped_heads = query_b.reshape(query_count, kv_heads, group, -1)
    keys_layout = keys_b.reshape(keys_b.shape[0], kv_heads, -1)
    raw_scores = jnp.einsum(
        "upfa,ypa->pfuy", grouped_heads, keys_layout, preferred_element_type=jnp.float32
    )
    curved = jnp.tanh(raw_scores / CAP)
    capped = jnp.where(visible, CAP * curved, -1e30)
    row_peak = jnp.max(capped, axis=-1, keepdims=True)
    exp_scores = jnp.exp(capped - row_peak)
    return (exp_scores / jnp.sum(exp_scores, axis=-1, keepdims=True), curved)


def per_device(
    tokens,
    lengths,
    w_query,
    w_key,
    w_value,
    w_output,
    w_gate,
    w_up,
    w_down,
    gain_attn_in,
    gain_attn_out,
    gain_mlp_in,
    gain_mlp_out,
    out_grad,
):
    head_count = lax.axis_size("head")
    row_count = lax.axis_size("rows")
    head_index = lax.axis_index("head")
    row_index = lax.axis_index("rows")
    tok_block = tokens.shape[0]
    model_dim = tokens.shape[1]
    query_rows = tok_block * head_count
    bucket_len = query_rows * row_count
    qcols = w_query.shape[1]
    local_heads = qcols // DH
    kv_heads = local_heads // 2
    group = local_heads // kv_heads
    kv_cols = kv_heads * DH
    kv_first = head_index * kv_cols
    scale = DH ** (-0.5)
    key_sel = lax.dynamic_slice_in_dim(w_key, kv_first, kv_cols, 1)
    value_sel = lax.dynamic_slice_in_dim(w_value, kv_first, kv_cols, 1)
    full_q, full_k, full_v, full_o, full_gate, full_up, full_down = (
        lax.all_gather(w_query, "rows", axis=0, tiled=True),
        lax.all_gather(key_sel, "rows", axis=0, tiled=True),
        lax.all_gather(value_sel, "rows", axis=0, tiled=True),
        lax.all_gather(w_output, "rows", axis=0, tiled=True),
        lax.all_gather(w_gate, "rows", axis=0, tiled=True),
        lax.all_gather(w_up, "rows", axis=0, tiled=True),
        lax.all_gather(w_down, "rows", axis=0, tiled=True),
    )
    quant_q = quantize(full_q, QEXP_MODEL, 8)
    quant_k = quantize(full_k, QEXP_MODEL, 8)
    quant_v = quantize(full_v, QEXP_MODEL, 8)
    quant_o = quantize(full_o, QEXP_MODEL, 8)
    quant_gate = quantize(full_gate, QEXP_MODEL, 4)
    quant_up = quantize(full_up, QEXP_MODEL, 4)
    quant_down = quantize(full_down, QEXP_HIDDEN, 2)
    local_ids = jnp.arange(query_rows, dtype=jnp.int32)
    query_tok = (local_ids // tok_block * row_count + row_index) * tok_block + local_ids % tok_block
    key_ids = jnp.arange(bucket_len, dtype=jnp.int32)
    key_tok = (
        key_ids % query_rows // tok_block * row_count + key_ids // query_rows
    ) * tok_block + key_ids % tok_block
    length_row = lengths[0]
    query_doc, query_pos = token_docs(query_tok, length_row)
    key_doc = token_docs(key_tok, length_row)[0]
    visible = (query_doc[:, None] == key_doc[None, :]) & (key_tok[None, :] <= query_tok[:, None])
    inputs = tokens.astype(jnp.float32)
    normed_b = rms_norm(inputs, gain_attn_in).astype(jnp.bfloat16)
    normed_blk = gather_heads(normed_b)
    proj_weights = jnp.concatenate([quant_q, quant_k, quant_v], axis=1)
    projected = jnp.dot(normed_blk, proj_weights, preferred_element_type=jnp.float32)
    cosine, sine = rope_tables(query_pos, DH)
    query_lin = projected[:, :qcols].reshape(query_rows, local_heads, DH)
    key_lin = projected[:, qcols : qcols + kv_cols].reshape(query_rows, kv_heads, DH)
    value_lin = projected[:, qcols + kv_cols :]
    query_b = (
        (rotate(query_lin, cosine, sine) * scale).astype(jnp.bfloat16).reshape(query_rows, qcols)
    )
    key_b = rotate(key_lin, cosine, sine).astype(jnp.bfloat16).reshape(query_rows, kv_cols)
    value_b = value_lin.astype(jnp.bfloat16)
    keys_all, values_all = gather_keys(key_b, value_b)
    attn_probs, curved = attention_probs(query_b, keys_all, visible, kv_heads, group)
    probs_bucket = attn_probs.astype(jnp.bfloat16)
    values_layout = values_all.reshape(bucket_len, kv_heads, DH)
    attended_b = (
        jnp.einsum(
            "xlrn,nxt->rxlt", probs_bucket, values_layout, preferred_element_type=jnp.float32
        )
        .reshape(query_rows, qcols)
        .astype(jnp.bfloat16)
    )

    def attn_term(first_row, row_total):
        return times_transposed(attended_b, quant_o)

    branch = sum_heads(attn_term, tok_block)
    mixed_h = inputs + rms_norm(branch, gain_attn_out)
    normed_mlp_b = rms_norm(mixed_h, gain_mlp_in).astype(jnp.bfloat16)
    mlp_blk = gather_heads(normed_mlp_b)
    gate = jnp.dot(mlp_blk, quant_gate, preferred_element_type=jnp.float32)
    up_proj = jnp.dot(mlp_blk, quant_up, preferred_element_type=jnp.float32)
    hidden_b = (jax.nn.gelu(gate, approximate=True) * up_proj).astype(jnp.bfloat16)

    def down_term(first_row, row_total):
        return times_transposed(hidden_b, quant_down)

    mlp_out = sum_heads(down_term, tok_block)
    mixed = (mixed_h + rms_norm(mlp_out, gain_mlp_out)).astype(jnp.bfloat16)
    out_cot = out_grad.astype(jnp.float32)
    d_mlp, d_gain_four = jax.vjp(rms_norm, mlp_out, gain_mlp_out)[1](out_cot)
    d_mlp_b = d_mlp.astype(jnp.bfloat16)
    d_mlp_blk = gather_heads(d_mlp_b)
    d_hidden = jnp.dot(d_mlp_blk, quant_down, preferred_element_type=jnp.float32)

    def gated(gate_in, up_in):
        return jax.nn.gelu(gate_in, approximate=True) * up_in

    d_gate, d_up = jax.vjp(gated, gate, up_proj)[1](d_hidden)
    d_gate_b = d_gate.astype(jnp.bfloat16)
    d_up_b = d_up.astype(jnp.bfloat16)

    def mlp_back_term(first_row, row_total):
        return times_transposed(d_gate_b, quant_gate) + times_transposed(d_up_b, quant_up)

    d_normed_mlp = sum_heads(mlp_back_term, tok_block)
    d_mixed_part, d_gain_three = jax.vjp(rms_norm, mixed_h, gain_mlp_in)[1](d_normed_mlp)
    d_mixed = out_cot + d_mixed_part
    d_branch, d_gain_two = jax.vjp(rms_norm, branch, gain_attn_out)[1](d_mixed)
    d_branch_b = d_branch.astype(jnp.bfloat16)
    d_branch_blk = gather_heads(d_branch_b)
    d_attended_b = jnp.dot(d_branch_blk, quant_o, preferred_element_type=jnp.float32).astype(
        jnp.bfloat16
    )
    keys_back, values_back, back_probs, back_curved, backward_probs_bucket = (
        keys_all,
        values_all,
        attn_probs,
        curved,
        probs_bucket,
    )
    attended_layout = d_attended_b.reshape(query_rows, kv_heads, group, DH)
    backward_values_layout = values_back.reshape(bucket_len, kv_heads, DH)
    backward_keys_layout = keys_back.reshape(bucket_len, kv_heads, DH)
    d_probs = jnp.einsum(
        "upfa,ypa->pfuy",
        attended_layout,
        backward_values_layout,
        preferred_element_type=jnp.float32,
    )
    inner = jnp.sum(back_probs * d_probs, axis=-1, keepdims=True)
    raw_scores_grad_bucket = (
        back_probs * (d_probs - inner) * (1.0 - back_curved * back_curved)
    ).astype(jnp.bfloat16)
    d_query = jnp.einsum(
        "xlrn,nxt->rxlt",
        raw_scores_grad_bucket,
        backward_keys_layout,
        preferred_element_type=jnp.float32,
    ).reshape(query_rows, local_heads, DH)
    query_layout = query_b.reshape(query_rows, kv_heads, group, DH)
    d_keys = jnp.einsum(
        "rnej,ernu->jru", raw_scores_grad_bucket, query_layout, preferred_element_type=jnp.float32
    ).reshape(query_rows * lax.axis_size("rows"), kv_cols)
    d_values = jnp.einsum(
        "rnej,ernu->jru", backward_probs_bucket, attended_layout, preferred_element_type=jnp.float32
    ).reshape(query_rows * lax.axis_size("rows"), kv_cols)
    key_grad = lax.psum_scatter(
        jnp.concatenate([d_keys, d_values], axis=1).astype(jnp.bfloat16),
        "rows",
        scatter_dimension=0,
        tiled=True,
    ).astype(jnp.float32)
    d_query_lin = rotate_back(d_query * scale, cosine, sine).reshape(query_rows, qcols)
    d_key_lin = rotate_back(
        key_grad[:, :kv_cols].reshape(query_rows, kv_heads, DH), cosine, sine
    ).reshape(query_rows, kv_cols)
    grads_b = jnp.concatenate([d_query_lin, d_key_lin, key_grad[:, kv_cols:]], axis=1).astype(
        jnp.bfloat16
    )

    def input_term(first_row, row_total):
        return times_transposed(grads_b, proj_weights)

    d_normed = sum_heads(input_term, tok_block)
    d_input_part, d_gain_one = jax.vjp(rms_norm, inputs, gain_attn_in)[1](d_normed)
    tokens_grad = (d_mixed + d_input_part).astype(jnp.bfloat16)
    main_grads = lax.psum_scatter(
        jnp.concatenate(
            [
                outer_sum(normed_blk, grads_b[:, :qcols]),
                outer_sum(d_branch_blk, attended_b),
                outer_sum(mlp_blk, d_gate_b),
                outer_sum(mlp_blk, d_up_b),
                outer_sum(d_mlp_blk, hidden_b),
            ],
            axis=1,
        ).astype(jnp.bfloat16),
        ("seq", "rows"),
        scatter_dimension=0,
        tiled=True,
    ).astype(jnp.float32)
    kv_grad_local = outer_sum(normed_blk, grads_b[:, qcols:])
    gain_terms = jnp.stack([d_gain_one, d_gain_two, d_gain_three, d_gain_four], axis=1)
    seq_count = lax.axis_size("seq")

    def own_rows_by_head(terms):
        width = terms.shape[1]
        ordered = terms.reshape(seq_count, head_count, row_count, -1, width)
        ordered = ordered.transpose(0, 2, 1, 3, 4).reshape(model_dim, width)
        return lax.psum_scatter(ordered, ("seq", "rows"), scatter_dimension=0, tiled=True)

    kv_rows = own_rows_by_head(kv_grad_local)
    kv_parts = lax.all_to_all(
        kv_rows.reshape(head_count, -1, 2 * kv_cols), "head", split_axis=0, concat_axis=0, tiled=True
    )
    kv_parts = kv_parts.transpose(1, 0, 2)
    own_count = kv_parts.shape[0]
    key_sum = kv_parts[:, :, :kv_cols].reshape(own_count, -1)
    value_sum = kv_parts[:, :, kv_cols:].reshape(own_count, -1)
    gain_sum = lax.psum_scatter(
        own_rows_by_head(gain_terms), "head", scatter_dimension=0, tiled=True
    )
    ffcols = w_gate.shape[1]
    gate_first = 2 * qcols
    return (
        mixed,
        tokens_grad,
        main_grads[:, :qcols],
        key_sum,
        value_sum,
        main_grads[:, qcols:gate_first],
        main_grads[:, gate_first : gate_first + ffcols],
        main_grads[:, gate_first + ffcols : gate_first + 2 * ffcols],
        main_grads[:, gate_first + 2 * ffcols :],
        gain_sum[:, 0],
        gain_sum[:, 1],
        gain_sum[:, 2],
        gain_sum[:, 3],
    )


def solution(mesh):
    placed = (
        P(("seq", "head", "rows"), None),
        P("seq", None),
        P("rows", "head"),
        P("rows", None),
        P("rows", None),
        P("rows", "head"),
        P("rows", "head"),
        P("rows", "head"),
        P("rows", "head"),
        P(),
        P(),
        P(),
        P(),
        P(("seq", "head", "rows"), None),
    )
    return jax.shard_map(
        per_device,
        mesh=mesh,
        in_specs=placed,
        out_specs=(
            P(("seq", "head", "rows"), None),
            P(("seq", "head", "rows"), None),
            P(("seq", "rows"), "head"),
            P(("seq", "head", "rows"), None),
            P(("seq", "head", "rows"), None),
            P(("seq", "rows"), "head"),
            P(("seq", "rows"), "head"),
            P(("seq", "rows"), "head"),
            P(("seq", "rows"), "head"),
            P(("seq", "head", "rows")),
            P(("seq", "head", "rows")),
            P(("seq", "head", "rows")),
            P(("seq", "head", "rows")),
        ),
        check_vma=False,
    )
```

```python
import math

import jax
import jax.numpy as jnp
from jax import lax
from jax.experimental import pallas as pl
from jax.experimental.pallas import tpu as pltpu
from jax.sharding import Mesh
from jax.sharding import PartitionSpec as P

DH = 128
QEXP_MODEL = 10
QEXP_HIDDEN = 11
CAP = 50.0
EPSILON = 1e-06
THETA = 10000.0
SCALE = DH ** (-0.5)
AXES = ("x", "yh", "z", "yl", "c")
BY_ID = pl.DeviceIdType.MESH
F32 = jnp.float32
BF16 = jnp.bfloat16
VM = pl.BlockSpec(memory_space=pltpu.VMEM)
SM = pl.BlockSpec(memory_space=pltpu.SMEM)
VMEM_LIMIT = 56 * 2**20


def here():
    return tuple(lax.axis_index(name) for name in AXES)


def z_device(step):
    x, yh, z, yl, c = here()
    return (x, yh, lax.rem(z + step, 4), yl, c)


def y_device(step):
    x, yh, z, yl, c = here()
    y = lax.rem(yh * 2 + yl + step, 4)
    return (x, lax.div(y, 2), z, lax.rem(y, 2), c)


def x_device(step):
    x, yh, z, yl, c = here()
    return (lax.rem(x + step, 4), yh, z, yl, c)


def sibling():
    x, yh, z, yl, c = here()
    return (x, yh, z, yl, 1 - c)


def greet(devices):
    barrier = pltpu.get_barrier_semaphore()
    for device in devices:
        pl.semaphore_signal(barrier, inc=1, device_id=device, device_id_type=BY_ID)
    pl.semaphore_wait(barrier, len(devices))


class Links:
    def __init__(self, send_sems, recv_sems):
        self.send_sems = send_sems
        self.recv_sems = recv_sems
        self.used = 0

    def plan(self, source, target, device):
        at = self.used
        self.used += 1
        return pltpu.make_async_remote_copy(
            src_ref=source,
            dst_ref=target,
            send_sem=self.send_sems.at[at],
            recv_sem=self.recv_sems.at[at],
            device_id=device,
            device_id_type=BY_ID,
        )

    def send(self, source, target, device):
        copy = self.plan(source, target, device)
        copy.start()
        return copy


def dot(left, right):
    return lax.dot_general(left, right, (((1,), (0,)), ((), ())), preferred_element_type=F32)


def dot_nt(left, right):
    return lax.dot_general(left, right, (((1,), (1,)), ((), ())), preferred_element_type=F32)


def dot_tn(left, right):
    return lax.dot_general(left, right, (((0,), (0,)), ((), ())), preferred_element_type=F32)


def quantized(weight, exponent, bits):
    shift = 8 - bits
    code = jnp.clip(jnp.floor(weight.astype(F32) * 2.0**exponent) + 128.0, 0.0, 255.0)
    if shift:
        code = (
            jnp.minimum(jnp.floor((code + 2.0 ** (shift - 1)) * 2.0 ** (-shift)), 2.0**bits - 1.0)
            * 2.0**shift
        )
    return ((code - 128.0) * 2.0 ** (-exponent)).astype(BF16)


def inverse_rms(values):
    return lax.rsqrt(jnp.mean(values * values, axis=-1, keepdims=True) + EPSILON)


def rms_back(values, gain, incoming):
    inverse = inverse_rms(values)
    scaled = incoming * gain
    inner = jnp.mean(scaled * values, axis=-1, keepdims=True)
    into = inverse * (scaled - values * (inverse * inverse) * inner)
    gain_part = jnp.sum(incoming * values * inverse, axis=0, keepdims=True)
    return into, gain_part


def swap_halves(values):
    half = values.shape[-1] // 2
    return jnp.concatenate([values[..., half:], values[..., :half]], axis=-1)


class Gather:
    def __init__(self, links, buffer, lead=()):
        x, yh, z, yl, c = here()
        self.links = links
        self.buffer = buffer
        self.lead = lead
        own = buffer.at[lead + (yh, yl * 2 + c)]
        self.ring = {step: links.send(own, own, y_device(step)) for step in (2, 1, 3)}
        self.pair = links.send(own, own, sibling())
        self.passed = []

    def forward(self):
        x, yh, z, yl, c = here()
        for step in (1, 3, 2):
            self.ring[step].wait_recv()
            origin = lax.rem(yh * 2 + yl + 4 - step, 4)
            block = self.buffer.at[
                self.lead + (lax.div(origin, 2), lax.rem(origin, 2) * 2 + c)
            ]
            self.passed.append(self.links.send(block, block, sibling()))

    def finish(self):
        self.pair.wait()
        for step in (1, 3, 2):
            self.ring[step].wait_send()
        for copy in self.passed:
            copy.wait()


def call(body, name, cid, outs, specs, scratch, sems, flops=0, nbytes=0):
    shapes = tuple(jax.ShapeDtypeStruct(shape, kind) for shape, kind in outs)
    return pl.pallas_call(
        body,
        name=name,
        out_shape=shapes,
        in_specs=specs,
        out_specs=tuple(VM for _ in outs),
        scratch_shapes=list(scratch)
        + [pltpu.SemaphoreType.DMA((sems,)), pltpu.SemaphoreType.DMA((sems,))],
        compiler_params=pltpu.CompilerParams(
            collective_id=cid, has_side_effects=True, vmem_limit_bytes=VMEM_LIMIT
        ),
    )


def qkv_kernel(
    tokens, gain, w_query, w_key, w_value, lengths,
    xn_all, wq_all, wkv_all, q_out, kv_out, cos_out, sin_out,
    send_sems, recv_sems,
):
    x, yh, z, yl, c = here()
    links = Links(send_sems, recv_sems)
    xin = tokens[...].astype(F32)
    xn_all[z] = (xin * inverse_rms(xin) * gain[...]).astype(BF16)
    for group in range(2):
        first = pl.multiple_of(group * 512 + z * 128, 128)
        wkv_all[yl * 2 + c, :, pl.ds(group * 128, 128)] = quantized(
            w_key[:, pl.ds(first, 128)], QEXP_MODEL, 8
        )
        wkv_all[yl * 2 + c, :, pl.ds(256 + group * 128, 128)] = quantized(
            w_value[:, pl.ds(first, 128)], QEXP_MODEL, 8
        )
    wq_all[yh, yl * 2 + c] = quantized(w_query[...], QEXP_MODEL, 8)
    greet([z_device(s) for s in (1, 2, 3)] + [y_device(s) for s in (1, 2, 3)] + [sibling()])
    ring = {s: links.send(xn_all.at[z], xn_all.at[z], z_device(s)) for s in (2, 1, 3)}
    own = wkv_all.at[yl * 2 + c]
    near = links.send(own, own, (x, yh, z, 1 - yl, c))
    pair = links.send(own, own, sibling())
    gather = Gather(links, wq_all)
    start = lengths[0, 0]
    half_lane = lax.rem(lax.broadcasted_iota(jnp.int32, (128, 128), 1), 64).astype(F32)
    freqs = jnp.exp(half_lane * (-2.0 * math.log(THETA) / DH))
    row = lax.broadcasted_iota(jnp.int32, (128, 128), 0)
    lane = lax.broadcasted_iota(jnp.int32, (128, 128), 1)
    for block in range(4):
        tok = row + (yh * 2048 + block * 512 + yl * 256 + c * 128)
        pos = jnp.where(tok >= start, tok - start, tok)
        angle = pos.astype(F32) * freqs
        cos_out[block] = jnp.cos(angle)
        sine = jnp.sin(angle)
        sin_out[block] = jnp.where(lane < 64, -sine, sine)
    near.wait_recv()
    other = wkv_all.at[(1 - yl) * 2 + c]
    passed = links.send(other, other, sibling())
    gather.forward()
    for s in (1, 3, 2):
        ring[s].wait_recv()
    pair.wait_recv()
    passed.wait_recv()
    xa = xn_all[...].reshape(512, 1024)
    cosd = cos_out[...].reshape(512, 128)
    sind = sin_out[...].reshape(512, 128)
    kv_lin = dot(xa, wkv_all[...].reshape(1024, 512))
    for group in range(2):
        key = kv_lin[:, group * 128 : group * 128 + 128]
        key = (key * cosd + swap_halves(key) * sind).astype(BF16)
        kv_out[group, :, :, 0:128] = key.reshape(4, 128, 128)
        value = kv_lin[:, 256 + group * 128 : 256 + group * 128 + 128].astype(BF16)
        kv_out[group, :, :, 128:256] = value.reshape(4, 128, 128)
    gather.finish()
    for group in range(2):
        q_lin = dot(xa, wq_all[group].reshape(1024, 256))
        for head in range(2):
            query = q_lin[:, head * 128 : head * 128 + 128]
            query = ((query * cosd + swap_halves(query) * sind) * SCALE).astype(BF16)
            q_out[group, :, head] = query.reshape(4, 128, 128)
    for copy in ring.values():
        copy.wait_send()
    near.wait_send()
    pair.wait_send()
    passed.wait_send()


def run_qkv(tokens, gain, w_query, w_key, w_value, lengths):
    return call(
        qkv_kernel, "qkv", 1,
        [
            ((4, 128, 1024), BF16), ((2, 4, 256, 256), BF16), ((4, 256, 512), BF16),
            ((2, 4, 2, 128, 128), BF16), ((2, 4, 128, 256), BF16),
            ((4, 128, 128), F32), ((4, 128, 128), F32),
        ],
        [VM] * 5 + [SM], [], 16,
    )(tokens, gain, w_query, w_key, w_value, lengths)


def score_block(query, key, key_base, query_base, start, causal):
    rows, keys = query.shape[0], key.shape[0]
    curved = jnp.tanh(dot_nt(query, key) * (1.0 / CAP))
    weight = jnp.exp(curved * CAP)
    token_q = query_base + lax.rem(lax.broadcasted_iota(jnp.int32, (rows, 1), 0), 128)
    first = jnp.where(token_q >= start, start, 0)
    token_k = key_base
    seen = token_k >= first
    if causal:
        seen = seen & (token_k <= token_q)
    return jnp.where(seen, weight, 0.0).astype(BF16)


def attention_kernel(
    q, kv, w_output, lengths,
    kv_all, attn, recip, wo_all,
    acc, send_sems, recv_sems,
):
    x, yh, z, yl, c = here()
    links = Links(send_sems, recv_sems)
    wo_all[yh, yl * 2 + c] = quantized(w_output[...], QEXP_MODEL, 8)
    greet([y_device(s) for s in (1, 2, 3)] + [sibling()])
    mine = kv_all.at[:, yh, yl, :, c]
    pair = links.send(kv, mine, sibling())
    near = links.send(kv, mine, (x, yh, z, 1 - yl, c))
    far = [
        links.plan(kv, mine, (x, 1, z, 1 - yl, c)),
        links.plan(kv, mine, (x, 1, z, yl, c)),
    ]

    @pl.when(yh == 0)
    def _():
        for copy in far:
            copy.start()

    gather = Gather(links, wo_all)
    kv_all[:, yh, yl, :, c] = kv[...]
    start = lengths[0, 0]
    lane = lax.broadcasted_iota(jnp.int32, (1, 256), 1)
    ones = jnp.ones((256, 128), BF16)

    def add_block(group, block, from_h, from_l, units, first):
        query = q[group, block].reshape(256, 128)
        q_base = yh * 2048 + block * 512 + yl * 256 + c * 128
        total = None
        for unit, causal in units:
            both = kv_all[group, from_h, from_l, unit].reshape(256, 256)
            k_base = from_h * 2048 + unit * 512 + from_l * 256 + lane
            weight = score_block(query, both[:, :128], k_base, q_base, start, causal)
            term = dot(weight, jnp.concatenate([both[:, 128:], ones], axis=1))
            total = term if total is None else total + term
        if first:
            acc[group, block] = total
        else:
            acc[group, block] += total

    def same_half(from_l, first):
        @pl.loop(0, 2)
        def _(group):
            for block in range(4):
                add_block(
                    group, block, yh, from_l,
                    [(unit, False) for unit in range(block)] + [(block, True)], first,
                )

    def other_half(from_l):
        @pl.loop(0, 8)
        def _(at):
            add_block(
                lax.div(at, 4), lax.rem(at, 4), 0, from_l,
                [(unit, False) for unit in range(4)], False,
            )

    pair.wait_recv()
    same_half(yl, True)
    near.wait_recv()
    block = kv_all.at[:, yh, 1 - yl, :, c]
    passed = links.send(block, block, sibling())
    passed.wait_recv()
    same_half(1 - yl, False)
    gather.forward()
    onward = []
    for copy, from_l in zip(far, (1 - yl, yl)):
        block = kv_all.at[:, 0, from_l, :, c]
        onward.append(links.plan(block, block, sibling()))

    @pl.when(yh == 1)
    def _():
        for copy, step, from_l in zip(far, onward, (1 - yl, yl)):
            copy.wait_recv()
            step.start()
            step.wait_recv()
            other_half(from_l)
        for step in onward:
            step.wait_send()

    for group in range(2):
        for block in range(4):
            total = acc[group, block]
            inverse = 1.0 / total[:, 128:256]
            recip[group, block] = inverse
            out = (total[:, :128] * inverse).astype(BF16)
            for head in range(2):
                first = group * 256 + head * 128
                attn[block, :, first : first + 128] = out[head * 128 : head * 128 + 128]
    gather.finish()
    pair.wait_send()
    near.wait_send()
    passed.wait_send()

    @pl.when(yh == 0)
    def _():
        for copy in far:
            copy.wait_send()


def run_attention(q, kv, w_output, lengths):
    return call(
        attention_kernel, "attention", 2,
        [
            ((2, 2, 2, 4, 2, 128, 256), BF16), ((4, 128, 512), BF16),
            ((2, 4, 256, 128), F32), ((2, 4, 256, 256), BF16),
        ],
        [VM] * 3 + [SM], [pltpu.VMEM((2, 4, 256, 256), F32)], 16,
    )(q, kv, w_output, lengths)


def scatter_z(links, partial_of, send_buf, recv_buf):
    x, yh, z, yl, c = here()
    copies = []
    for step in (2, 1, 3):
        send_buf[step - 1] = partial_of(lax.rem(z + step, 4)).astype(BF16)
        copies.append(links.send(send_buf.at[step - 1], recv_buf.at[step - 1], z_device(step)))
    return copies, partial_of(z)


def gather_z(links, buffer):
    x, yh, z, yl, c = here()
    return [links.send(buffer.at[z], buffer.at[z], z_device(s)) for s in (2, 1, 3)]


def outproj_kernel(
    attn, wo_all, tokens, gain_out, gain_in, w_gate, w_up, w_down,
    branch_out, h1_out, hn_all, wf_all,
    send_buf, recv_buf, send_sems, recv_sems,
):
    x, yh, z, yl, c = here()
    links = Links(send_sems, recv_sems)
    greet([z_device(s) for s in (1, 2, 3)] + [y_device(s) for s in (1, 2, 3)] + [sibling()])

    def partial_of(block):
        left = attn[block]
        return dot_nt(left[:, :256], wo_all[0].reshape(1024, 256)) + dot_nt(
            left[:, 256:], wo_all[1].reshape(1024, 256)
        )

    copies, own = scatter_z(links, partial_of, send_buf, recv_buf)
    gathers = []
    for which, (weight, exponent, bits) in enumerate(
        ((w_gate, QEXP_MODEL, 4), (w_up, QEXP_MODEL, 4), (w_down, QEXP_HIDDEN, 2))
    ):
        wf_all[which, yh, yl * 2 + c] = quantized(weight[...], exponent, bits)
        gathers.append(Gather(links, wf_all, (which,)))
    branch = own
    for copy, slot in zip(copies, (1, 0, 2)):
        copy.wait_recv()
        branch = branch + recv_buf[slot].astype(F32)
    branch_out[...] = branch
    h1 = tokens[...].astype(F32) + branch * inverse_rms(branch) * gain_out[...]
    h1_out[...] = h1
    hn_all[z] = (h1 * inverse_rms(h1) * gain_in[...]).astype(BF16)
    ring = gather_z(links, hn_all)
    for gather in gathers:
        gather.forward()
    for copy in ring:
        copy.wait()
    for gather in gathers:
        gather.finish()
    for copy in copies:
        copy.wait_send()


def run_outproj(attn, wo_all, tokens, gain_out, gain_in, w_gate, w_up, w_down):
    return call(
        outproj_kernel, "outproj", 3,
        [
            ((128, 1024), F32), ((128, 1024), F32), ((4, 128, 1024), BF16),
            ((3, 2, 4, 256, 384), BF16),
        ],
        [VM] * 8, [pltpu.VMEM((3, 128, 1024), BF16)] * 2, 32,
    )(attn, wo_all, tokens, gain_out, gain_in, w_gate, w_up, w_down)


GELU_A = math.sqrt(2.0 / math.pi)
GELU_B = 0.044715


def gelu_parts(gate):
    square = gate * gate
    curve = jnp.tanh(GELU_A * gate * (1.0 + GELU_B * square))
    half = 0.5 * (1.0 + curve)
    slope = half + 0.5 * gate * (1.0 - curve * curve) * (
        GELU_A * (1.0 + 3.0 * GELU_B * square)
    )
    return gate * half, slope


def mlp_kernel(
    hn_all, wf_all, h1, gain_out, out_grad,
    gate_all, up_all, hidden_all, mixed_out, d_mlp_all, gain_grad,
    send_buf, recv_buf, send_sems, recv_sems,
):
    x, yh, z, yl, c = here()
    links = Links(send_sems, recv_sems)

    def partial_of(block):
        left = hn_all[block]
        total = None
        for group in range(2):
            cols = slice(group * 384, group * 384 + 384)
            gate = dot(left, wf_all[0, group].reshape(1024, 384))
            up = dot(left, wf_all[1, group].reshape(1024, 384))
            gate_all[block, :, cols] = gate
            up_all[block, :, cols] = up
            curve = jnp.tanh(GELU_A * gate * (1.0 + GELU_B * gate * gate))
            hidden = (0.5 * gate * (1.0 + curve) * up).astype(BF16)
            hidden_all[block, :, cols] = hidden
            term = dot_nt(hidden, wf_all[2, group].reshape(1024, 384))
            total = term if total is None else total + term
        return total

    greet([z_device(s) for s in (1, 2, 3)])
    copies, own = scatter_z(links, partial_of, send_buf, recv_buf)
    mlp = own
    for copy, slot in zip(copies, (1, 0, 2)):
        copy.wait_recv()
        mlp = mlp + recv_buf[slot].astype(F32)
    d_mlp, gain_part = rms_back(mlp, gain_out[...], out_grad[...].astype(F32))
    d_mlp_all[z] = d_mlp.astype(BF16)
    ring = gather_z(links, d_mlp_all)
    gain_grad[...] = gain_part
    mixed_out[...] = (h1[...] + mlp * inverse_rms(mlp) * gain_out[...]).astype(BF16)
    for copy in ring:
        copy.wait()
    for copy in copies:
        copy.wait_send()


def run_mlp(hn_all, wf_all, h1, gain_out, out_grad):
    return call(
        mlp_kernel, "mlp", 4,
        [
            ((4, 128, 768), F32), ((4, 128, 768), F32), ((4, 128, 768), BF16),
            ((128, 1024), BF16), ((4, 128, 1024), BF16), ((1, 1024), F32),
        ],
        [VM] * 5, [pltpu.VMEM((3, 128, 1024), BF16)] * 2, 8,
    )(hn_all, wf_all, h1, gain_out, out_grad)


class Shrink:
    def __init__(self, links, terms, pair_sum, middle, first_recv, last_recv, y_first):
        self.links = links
        self.terms = terms
        self.pair_sum = pair_sum
        self.middle = middle
        self.first_recv = first_recv
        self.last_recv = last_recv
        self.y_first = y_first
        self.copies = []

    def start(self):
        x, yh, z, yl, c = here()
        self.pair = self.links.send(self.terms.at[:, :, :, 1 - c], self.pair_sum, sibling())

    def send_first(self):
        x, yh, z, yl, c = here()
        self.pair.wait()
        terms, pair_sum = self.terms, self.pair_sum

        @pl.loop(0, 8)
        def _(at):
            h, k = lax.div(at, 4), lax.rem(at, 4)
            for low in range(2):
                pair_sum[h, k, low] = (
                    terms[h, k, low, c].astype(F32) + pair_sum[h, k, low].astype(F32)
                ).astype(BF16)

        self.first = []
        for step in (2, 1, 3):
            if self.y_first:
                device = y_device(step)
                source = pair_sum.at[device[1], :, device[3]]
            else:
                device = x_device(step)
                source = pair_sum.at[:, device[0]]
            self.first.append(self.links.send(source, self.first_recv.at[step - 1], device))

    def send_last(self):
        x, yh, z, yl, c = here()
        for copy in self.first:
            copy.wait()
        got = self.first_recv

        @pl.loop(0, 4)
        def _(at):
            if self.y_first:
                total = self.pair_sum[yh, at, yl].astype(F32)
                for slot in range(3):
                    total = total + got[slot, at].astype(F32)
                self.middle[at] = total.astype(BF16)
            else:
                h, low = lax.div(at, 2), lax.rem(at, 2)
                total = self.pair_sum[h, x, low].astype(F32)
                for slot in range(3):
                    total = total + got[slot, h, low].astype(F32)
                self.middle[h, low] = total.astype(BF16)

        self.second = []
        for step in (2, 1, 3):
            if self.y_first:
                device = x_device(step)
                source = self.middle.at[device[0]]
            else:
                device = y_device(step)
                source = self.middle.at[device[1], device[3]]
            self.second.append(self.links.send(source, self.last_recv.at[step - 1], device))

    def result(self):
        x, yh, z, yl, c = here()
        for copy in self.second:
            copy.wait()
        total = (self.middle[x] if self.y_first else self.middle[yh, yl]).astype(F32)
        for slot in range(3):
            total = total + self.last_recv[slot].astype(F32)
        return total


def shrink_scratch(rows, width, y_first):
    first = (4, rows, width) if y_first else (2, 2, rows, width)
    return [
        pltpu.VMEM((2, 4, 2, 2, rows, width), BF16),
        pltpu.VMEM((2, 4, 2, rows, width), BF16),
        pltpu.VMEM(first, BF16),
        pltpu.VMEM((3,) + first, BF16),
        pltpu.VMEM((3, rows, width), BF16),
    ]


def everyone():
    return (
        [z_device(s) for s in (1, 2, 3)]
        + [y_device(s) for s in (1, 2, 3)]
        + [x_device(s) for s in (1, 2, 3)]
        + [sibling()]
    )


def mlp_back_kernel(
    d_mlp_all, hidden_all, gate_all, up_all, wf_all, hn_all, h1, branch, out_grad, gain_in, gain_out,
    d_h1_out, d_branch_all, gain_in_grad, gain_out_grad, dwd_out, dwg_out, dwu_out,
    send_buf, recv_buf, d_gate_all, d_up_all,
    ta, pa, ma, fa, la, tb, pb, mb, fb, lb,
    send_sems, recv_sems,
):
    x, yh, z, yl, c = here()
    links = Links(send_sems, recv_sems)
    one = Shrink(links, ta, pa, ma, fa, la, True)
    two = Shrink(links, tb, pb, mb, fb, lb, False)

    def partial_of(block):
        left = d_mlp_all[block]
        total = None
        for group in range(2):
            cols = slice(group * 384, group * 384 + 384)
            d_hidden = dot(left, wf_all[2, group].reshape(1024, 384))
            value, slope = gelu_parts(gate_all[block, :, cols])
            d_gate = (d_hidden * up_all[block, :, cols] * slope).astype(BF16)
            d_up = (d_hidden * value).astype(BF16)
            d_gate_all[block, :, cols] = d_gate
            d_up_all[block, :, cols] = d_up
            term = dot_nt(d_gate, wf_all[0, group].reshape(1024, 384)) + dot_nt(
                d_up, wf_all[1, group].reshape(1024, 384)
            )
            total = term if total is None else total + term
        return total

    greet(everyone())
    copies, own = scatter_z(links, partial_of, send_buf, recv_buf)
    d_mlp = d_mlp_all[...].reshape(512, 1024)
    hn = hn_all[...].reshape(512, 1024)
    for group in range(2):
        cols = slice(group * 384, group * 384 + 384)
        down = dot_tn(d_mlp, hidden_all[:, :, cols].reshape(512, 384)).astype(BF16)
        ta[group, :, :, :, :, 0:384] = down.reshape(4, 2, 2, 64, 384)
        gate = dot_tn(hn, d_gate_all[:, :, cols].reshape(512, 384)).astype(BF16)
        gate = gate.reshape(4, 2, 2, 64, 384)
        ta[group, :, :, :, :, 384:640] = gate[..., 0:256]
        tb[group, :, :, :, :, 0:128] = gate[..., 256:384]
        up = dot_tn(hn, d_up_all[:, :, cols].reshape(512, 384)).astype(BF16)
        tb[group, :, :, :, :, 128:512] = up.reshape(4, 2, 2, 64, 384)
    one.start()
    two.start()
    d_hn = own
    for copy, slot in zip(copies, (1, 0, 2)):
        copy.wait_recv()
        d_hn = d_hn + recv_buf[slot].astype(F32)
    into, gain_part = rms_back(h1[...], gain_in[...], d_hn)
    gain_in_grad[...] = gain_part
    d_h1 = out_grad[...].astype(F32) + into
    d_h1_out[...] = d_h1
    into, gain_part = rms_back(branch[...], gain_out[...], d_h1)
    gain_out_grad[...] = gain_part
    d_branch_all[z] = into.astype(BF16)
    ring = gather_z(links, d_branch_all)
    one.send_first()
    two.send_first()
    one.send_last()
    two.send_last()
    first = one.result()
    dwd_out[...] = first[:, 0:384]
    dwg_out[:, 0:256] = first[:, 384:640]
    second = two.result()
    dwg_out[:, 256:384] = second[:, 0:128]
    dwu_out[...] = second[:, 128:512]
    for copy in ring:
        copy.wait()
    for copy in copies:
        copy.wait_send()


def run_mlp_back(d_mlp_all, hidden, gate, up, wf_all, hn_all, h1, branch, out_grad, gain_in, gain_out):
    return call(
        mlp_back_kernel, "mlp_back", 5,
        [
            ((128, 1024), F32), ((4, 128, 1024), BF16), ((1, 1024), F32), ((1, 1024), F32),
            ((64, 384), F32), ((64, 384), F32), ((64, 384), F32),
        ],
        [VM] * 11,
        [pltpu.VMEM((3, 128, 1024), BF16)] * 2
        + [pltpu.VMEM((4, 128, 768), BF16)] * 2
        + shrink_scratch(64, 640, True)
        + shrink_scratch(64, 512, False),
        24,
    )(d_mlp_all, hidden, gate, up, wf_all, hn_all, h1, branch, out_grad, gain_in, gain_out)


def attention_back_kernel(
    d_branch_all, wo_all, attn, recip, q, kv_all, cosd, sind, lengths,
    grads, dwo_out,
    d_out, d_q, d_kv, pair_recv, y_send, y_recv, total_kv,
    ta, pa, ma, fa, la, tb, pb, mb, fb, lb,
    send_sems, recv_sems,
):
    x, yh, z, yl, c = here()
    links = Links(send_sems, recv_sems)
    one = Shrink(links, ta, pa, ma, fa, la, True)
    two = Shrink(links, tb, pb, mb, fb, lb, False)
    greet(
        [y_device(s) for s in (1, 2, 3)] + [x_device(s) for s in (1, 2, 3)] + [sibling()]
    )
    d_branch = d_branch_all[...].reshape(512, 1024)
    for group in range(2):
        cols = slice(group * 256, group * 256 + 256)
        back = dot_tn(d_branch, attn[:, :, cols].reshape(512, 256)).astype(BF16)
        back = back.reshape(4, 2, 2, 64, 256)
        ta[group] = back[..., 0:128]
        tb[group] = back[..., 128:256]
    one.start()
    two.start()
    lane = lax.broadcasted_iota(jnp.int32, (256, 128), 1)
    for group in range(2):
        cols = slice(group * 256, group * 256 + 256)
        d_attn = dot(d_branch, wo_all[group].reshape(1024, 256)).astype(BF16)
        for block in range(4):
            rows = d_attn[block * 128 : block * 128 + 128].astype(F32)
            rows = jnp.concatenate([rows[:, :128], rows[:, 128:]], axis=0)
            outs = attn[block, :, cols].astype(F32)
            outs = jnp.concatenate([outs[:, :128], outs[:, 128:]], axis=0)
            scaled = (rows * recip[group, block]).astype(BF16)
            inner = -jnp.sum(scaled.astype(F32) * outs, axis=1, keepdims=True)
            high = inner.astype(BF16)
            low = (inner - high.astype(F32)).astype(BF16)
            extra = jnp.where(
                lane == 0, high.astype(F32), jnp.where(lane == 1, low.astype(F32), 0.0)
            )
            d_out[group, block] = jnp.concatenate([scaled, extra.astype(BF16)], axis=1)
    d_q[...] = jnp.zeros_like(d_q)
    start = lengths[0, 0]
    ones = jnp.where(lane < 2, 1.0, 0.0).astype(BF16)
    token_row = lax.broadcasted_iota(jnp.int32, (1, 256), 1)

    def unit_back(group, from_h, from_l, unit, first_block):
        both = kv_all[group, from_h, from_l, unit].reshape(256, 256)
        key, value = both[:, :128], both[:, 128:]
        count = 4 - first_block
        query = q[group, first_block:].reshape(count * 256, 128)
        cot = d_out[group, first_block:].reshape(count * 256, 256)
        curved = jnp.tanh(dot_nt(key, query) * (1.0 / CAP))
        weight = jnp.exp(curved * CAP)
        base = yh * 2048 + yl * 256 + c * 128
        token_q = jnp.concatenate(
            [
                base + block * 512 + lax.rem(token_row, 128)
                for block in range(first_block, 4)
            ],
            axis=1,
        )
        floor = jnp.where(token_q >= start, start, 0)
        key_base = from_h * 2048 + unit * 512 + from_l * 256
        token_k = key_base + lax.broadcasted_iota(jnp.int32, (256, 1), 0)
        seen = (token_k >= floor) & (token_k <= token_q)
        weight = jnp.where(seen, weight, 0.0)
        grown = dot_nt(jnp.concatenate([value, ones], axis=1), cot)
        slope = (weight * grown * (1.0 - curved * curved)).astype(BF16)
        d_key = dot(slope, query)
        d_value = dot(weight.astype(BF16), cot[:, :128])
        d_kv[group, from_h, from_l, unit] = (
            jnp.concatenate([d_key, d_value], axis=1).astype(BF16).reshape(2, 128, 256)
        )
        d_q[group, :, first_block * 256 :] += dot(key.T, slope)

    def same_half(from_l):
        @pl.loop(0, 2)
        def _(group):
            for unit in range(4):
                unit_back(group, yh, from_l, unit, unit)

    def other_half(from_l):
        @pl.loop(0, 8)
        def _(at):
            unit_back(lax.div(at, 4), 0, from_l, lax.rem(at, 4), 0)

    def pair_plan(slot, from_h, from_l):
        return links.plan(
            d_kv.at[:, from_h, from_l, :, 1 - c], pair_recv.at[slot], sibling()
        )

    def add_pair(slot, from_h, from_l):
        return d_kv[:, from_h, from_l, :, c].astype(F32) + pair_recv[slot].astype(F32)

    far_pair = [pair_plan(0, 0, 1 - yl), pair_plan(1, 0, yl)]
    far_send = [
        links.plan(y_send.at[0], y_recv.at[0], (x, 0, z, 1 - yl, c)),
        links.plan(y_send.at[1], y_recv.at[1], (x, 0, z, yl, c)),
    ]

    @pl.when(yh == 1)
    def _():
        other_half(1 - yl)
        far_pair[0].start()
        other_half(yl)
        far_pair[1].start()
        far_pair[0].wait()
        y_send[0] = add_pair(0, 0, 1 - yl).astype(BF16)
        far_send[0].start()

    one.send_first()
    two.send_first()
    same_half(1 - yl)
    near_pair = pair_plan(2, yh, 1 - yl)
    near_pair.start()

    @pl.when(yh == 1)
    def _():
        far_pair[1].wait()
        y_send[1] = add_pair(1, 0, yl).astype(BF16)
        far_send[1].start()

    near_pair.wait()
    y_send[2] = add_pair(2, yh, 1 - yl).astype(BF16)
    near_send = links.send(y_send.at[2], y_recv.at[2], (x, yh, z, 1 - yl, c))
    one.send_last()
    two.send_last()
    same_half(yl)
    own_pair = pair_plan(3, yh, yl)
    own_pair.start()
    cos_rows = cosd[...]
    sin_rows = sind[...]

    def rope_back(values, block):
        return values * cos_rows[block] - swap_halves(values) * sin_rows[block]

    for group in range(2):
        d_query = d_q[group].T
        for block in range(4):
            for head in range(2):
                first = block * 256 + head * 128
                turned = rope_back(d_query[first : first + 128], block) * SCALE
                at = group * 256 + head * 128
                grads[block, :, at : at + 128] = turned.astype(BF16)
    dwo_out[:, 0:128] = one.result()
    dwo_out[:, 128:256] = two.result()
    own_pair.wait()
    total_kv[...] = add_pair(3, yh, yl)
    near_send.wait()
    total_kv[...] += y_recv[2].astype(F32)

    @pl.when(yh == 0)
    def _():
        for slot in range(2):
            far_send[slot].wait_recv()
            total_kv[...] += y_recv[slot].astype(F32)

    @pl.when(yh == 1)
    def _():
        for slot in range(2):
            far_send[slot].wait_send()

    for group in range(2):
        for block in range(4):
            both = total_kv[group, block]
            d_key = both[:, :128].astype(BF16).astype(F32)
            at = 512 + group * 128
            grads[block, :, at : at + 128] = rope_back(d_key, block).astype(BF16)
            at = 768 + group * 128
            grads[block, :, at : at + 128] = both[:, 128:].astype(BF16)


def run_attention_back(d_branch_all, wo_all, attn, recip, q, kv_all, cosd, sind, lengths):
    return call(
        attention_back_kernel, "attention_back", 6,
        [((4, 128, 1024), BF16), ((64, 256), F32)],
        [VM] * 8 + [SM],
        [
            pltpu.VMEM((2, 4, 256, 256), BF16),
            pltpu.VMEM((2, 128, 1024), F32),
            pltpu.VMEM((2, 2, 2, 4, 2, 128, 256), BF16),
            pltpu.VMEM((4, 2, 4, 128, 256), BF16),
            pltpu.VMEM((3, 2, 4, 128, 256), BF16),
            pltpu.VMEM((3, 2, 4, 128, 256), BF16),
            pltpu.VMEM((2, 4, 128, 256), F32),
        ]
        + shrink_scratch(64, 128, True)
        + shrink_scratch(64, 128, False),
        24,
    )(d_branch_all, wo_all, attn, recip, q, kv_all, cosd, sind, lengths)


def input_back_kernel(
    grads, wq_all, wkv_all, xn_all, tokens, gain, d_h1, gain_two, gain_three, gain_four,
    tokens_grad, dwq_out, dwk_out, dwv_out, gain_sums,
    send_buf, recv_buf, folded, kv_send, kv_recv, gain_own, gain_pair, gain_y, gain_x, gain_z,
    ta, pa, ma, fa, la, tb, pb, mb, fb, lb,
    send_sems, recv_sems,
):
    x, yh, z, yl, c = here()
    links = Links(send_sems, recv_sems)
    one = Shrink(links, ta, pa, ma, fa, la, True)
    two = Shrink(links, tb, pb, mb, fb, lb, False)
    gain_own[...] = jnp.zeros_like(gain_own)

    def partial_of(block):
        left = grads[block]
        total = dot_nt(left[:, 512:], wkv_all[...].reshape(1024, 512))
        for group in range(2):
            total = total + dot_nt(
                left[:, group * 256 : group * 256 + 256], wq_all[group].reshape(1024, 256)
            )
        gain_own[0:1] += jnp.sum(total * xn_all[block].astype(F32), axis=0, keepdims=True)
        return total

    greet(everyone())
    copies, own = scatter_z(links, partial_of, send_buf, recv_buf)
    gain_own[0:1] = gain_own[0:1] / gain[...]
    gain_own[1:2] = gain_two[...]
    gain_own[2:3] = gain_three[...]
    gain_own[3:4] = gain_four[...]
    pair = links.send(gain_own, gain_pair, sibling())
    xa = xn_all[...].reshape(512, 1024)
    for group in range(2):
        back = dot_tn(xa, grads[:, :, group * 256 : group * 256 + 256].reshape(512, 256))
        ta[group] = back.astype(BF16).reshape(4, 2, 2, 64, 256)
    one.start()
    back = dot_tn(xa, grads[:, :, 512:].reshape(512, 512))
    for k in range(4):
        for h in range(2):
            for block in range(4):
                first = k * 256 + h * 128 + block * 32
                folded[k, h, :, :, block] = back[first : first + 32].reshape(2, 2, 8, 512)
    for h in range(2):
        for k in range(4):
            for low in range(2):
                tb[h, k, low] = folded[k, h, low].reshape(2, 32, 512).astype(BF16)
    two.start()
    pair.wait()
    gain_pair[...] += gain_own[...]
    sent = [links.send(gain_pair, gain_y.at[s - 1], y_device(s)) for s in (2, 1, 3)]
    one.send_first()
    two.send_first()
    for copy in sent:
        copy.wait()
    total = gain_pair[...]
    gain_own[...] = total + (gain_y[0] + gain_y[2]) + gain_y[1]
    sent = [links.send(gain_own, gain_x.at[s - 1], x_device(s)) for s in (2, 1, 3)]
    d_xn = own
    for copy, slot in zip(copies, (1, 0, 2)):
        copy.wait_recv()
        d_xn = d_xn + recv_buf[slot].astype(F32)
    into, _ = rms_back(tokens[...].astype(F32), gain[...], d_xn)
    tokens_grad[...] = (d_h1[...] + into).astype(BF16)
    for copy in sent:
        copy.wait()
    gain_pair[...] = gain_own[...] + (gain_x[0] + gain_x[2]) + gain_x[1]
    sent = [links.send(gain_pair, gain_z.at[s - 1], z_device(s)) for s in (2, 1, 3)]
    one.send_last()
    two.send_last()
    dwq_out[...] = one.result()
    kv_send[...] = two.result().reshape(4, 8, 512)
    moved = []
    for s in (2, 1, 3):
        device = z_device(s)
        moved.append(links.send(kv_send.at[device[2]], kv_recv.at[z], device))
    kv_recv[z] = kv_send[z]
    for copy in sent:
        copy.wait()
    gain_sums[...] = gain_pair[...] + (gain_z[0] + gain_z[2]) + gain_z[1]
    for copy in moved:
        copy.wait()
    for origin in range(4):
        for group in range(2):
            at = group * 512 + origin * 128
            dwk_out[:, at : at + 128] = kv_recv[origin, :, group * 128 : group * 128 + 128]
            dwv_out[:, at : at + 128] = kv_recv[
                origin, :, 256 + group * 128 : 384 + group * 128
            ]
    for copy in copies:
        copy.wait_send()


def run_input_back(
    grads, wq_all, wkv_all, xn_all, tokens, gain, d_h1, gain_two, gain_three, gain_four
):
    return call(
        input_back_kernel, "input_back", 7,
        [
            ((128, 1024), BF16), ((64, 256), F32), ((8, 1024), F32), ((8, 1024), F32),
            ((8, 1024), F32),
        ],
        [VM] * 10,
        [pltpu.VMEM((3, 128, 1024), BF16)] * 2
        + [
            pltpu.VMEM((4, 2, 2, 2, 4, 8, 512), F32),
            pltpu.VMEM((4, 8, 512), F32),
            pltpu.VMEM((4, 8, 512), F32),
            pltpu.VMEM((8, 1024), F32),
            pltpu.VMEM((8, 1024), F32),
            pltpu.VMEM((3, 8, 1024), F32),
            pltpu.VMEM((3, 8, 1024), F32),
            pltpu.VMEM((3, 8, 1024), F32),
        ]
        + shrink_scratch(64, 256, True)
        + shrink_scratch(32, 512, False),
        32,
    )(grads, wq_all, wkv_all, xn_all, tokens, gain, d_h1, gain_two, gain_three, gain_four)


def per_device(
    tokens, lengths, w_query, w_key, w_value, w_output, w_gate, w_up, w_down,
    gain_attn_in, gain_attn_out, gain_mlp_in, gain_mlp_out, out_grad,
):
    gain_attn_in, gain_attn_out, gain_mlp_in, gain_mlp_out = (
        gain.reshape(1, -1) for gain in (gain_attn_in, gain_attn_out, gain_mlp_in, gain_mlp_out)
    )
    xn_all, wq_all, wkv_all, q, kv, cosd, sind = run_qkv(
        tokens, gain_attn_in, w_query, w_key, w_value, lengths
    )
    kv_all, attn, recip, wo_all = run_attention(q, kv, w_output, lengths)
    branch, h1, hn_all, wf_all = run_outproj(
        attn, wo_all, tokens, gain_attn_out, gain_mlp_in, w_gate, w_up, w_down
    )
    gate, up, hidden, mixed, d_mlp_all, gain_four = run_mlp(
        hn_all, wf_all, h1, gain_mlp_out, out_grad
    )
    d_h1, d_branch_all, gain_three, gain_two, dwd, dwg, dwu = run_mlp_back(
        d_mlp_all, hidden, gate, up, wf_all, hn_all, h1, branch, out_grad,
        gain_mlp_in, gain_attn_out,
    )
    grads, dwo = run_attention_back(
        d_branch_all, wo_all, attn, recip, q, kv_all, cosd, sind, lengths
    )
    tokens_grad, dwq, dwk, dwv, gains = run_input_back(
        grads, wq_all, wkv_all, xn_all, tokens, gain_attn_in, d_h1,
        gain_two, gain_three, gain_four,
    )
    x, yh, z, yl, c = here()
    first = ((((x * 2 + yh) * 4 + z) * 2 + yl) * 2 + c) * 8
    own_gains = lax.dynamic_slice(gains, (0, first), (4, 8))
    return (
        mixed, tokens_grad, dwq, dwk, dwv, dwo, dwg, dwu, dwd,
        own_gains[0], own_gains[1], own_gains[2], own_gains[3],
    )


def solution(mesh):
    grid = Mesh(mesh.devices.reshape(4, 2, 4, 2, 2), AXES)
    tokens = P(AXES, None)
    split = P(("yl", "c"), ("yh", "z"))
    rows = P(("yl", "c"), None)
    grads = P(("x", "yl", "c"), ("yh", "z"))
    gains = P(AXES)
    return jax.shard_map(
        per_device,
        mesh=grid,
        in_specs=(tokens, P("x", None), split, rows, rows, split, split, split, split)
        + (P(),) * 4
        + (tokens,),
        out_specs=(tokens, tokens, grads, tokens, tokens, grads, grads, grads, grads)
        + (gains,) * 4,
        check_vma=False,
    )
```

```python
import math

import jax
import jax.numpy as jnp
from jax import lax
from jax.experimental import pallas as pl
from jax.experimental.pallas import tpu as pltpu
from jax.sharding import Mesh
from jax.sharding import PartitionSpec as P

DH = 128
QEXP_MODEL = 10
QEXP_HIDDEN = 11
CAP = 50.0
EPSILON = 1e-06
THETA = 10000.0
SCALE = DH ** (-0.5)
AXES = ("x", "yh", "z", "yl", "c")
BY_ID = pl.DeviceIdType.MESH
F32 = jnp.float32
BF16 = jnp.bfloat16
VM = pl.BlockSpec(memory_space=pltpu.VMEM)
SM = pl.BlockSpec(memory_space=pltpu.SMEM)
LOG2E = 1.4426950408889634
VMEM_LIMIT = 63 * 2**20


def here():
    return tuple(lax.axis_index(name) for name in AXES)


def z_device(step):
    x, yh, z, yl, c = here()
    return (x, yh, lax.rem(z + step, 4), yl, c)


def y_device(step):
    x, yh, z, yl, c = here()
    y = lax.rem(yh * 2 + yl + step, 4)
    return (x, lax.div(y, 2), z, lax.rem(y, 2), c)


def x_device(step):
    x, yh, z, yl, c = here()
    return (lax.rem(x + step, 4), yh, z, yl, c)


def sibling():
    x, yh, z, yl, c = here()
    return (x, yh, z, yl, 1 - c)


def greet(devices):
    barrier = pltpu.get_barrier_semaphore()
    for device in devices:
        pl.semaphore_signal(barrier, inc=1, device_id=device, device_id_type=BY_ID)
    pl.semaphore_wait(barrier, len(devices))


class Links:
    def __init__(self, send_sems, recv_sems):
        self.send_sems = send_sems
        self.recv_sems = recv_sems
        self.used = 0

    def plan(self, source, target, device):
        at = self.used
        self.used += 1
        return pltpu.make_async_remote_copy(
            src_ref=source,
            dst_ref=target,
            send_sem=self.send_sems.at[at],
            recv_sem=self.recv_sems.at[at],
            device_id=device,
            device_id_type=BY_ID,
        )

    def send(self, source, target, device):
        copy = self.plan(source, target, device)
        copy.start()
        return copy


def dot(left, right):
    return lax.dot_general(left, right, (((1,), (0,)), ((), ())), preferred_element_type=F32)


def dot_nt(left, right):
    return lax.dot_general(left, right, (((1,), (1,)), ((), ())), preferred_element_type=F32)


def dot_tn(left, right):
    return lax.dot_general(left, right, (((0,), (0,)), ((), ())), preferred_element_type=F32)


def quantized(weight, exponent, bits):
    shift = 8 - bits
    code = jnp.clip(jnp.floor(weight.astype(F32) * 2.0**exponent) + 128.0, 0.0, 255.0)
    if shift:
        code = (
            jnp.minimum(jnp.floor((code + 2.0 ** (shift - 1)) * 2.0 ** (-shift)), 2.0**bits - 1.0)
            * 2.0**shift
        )
    return ((code - 128.0) * 2.0 ** (-exponent)).astype(BF16)


def inverse_rms(values):
    return lax.rsqrt(jnp.mean(values * values, axis=-1, keepdims=True) + EPSILON)


def rms_back(values, gain, incoming):
    inverse = inverse_rms(values)
    scaled = incoming * gain
    inner = jnp.mean(scaled * values, axis=-1, keepdims=True)
    into = inverse * (scaled - values * (inverse * inverse) * inner)
    gain_part = jnp.sum(incoming * values * inverse, axis=0, keepdims=True)
    return into, gain_part


def swap_halves(values):
    half = values.shape[-1] // 2
    return jnp.concatenate([values[..., half:], values[..., :half]], axis=-1)


class Gather:
    def __init__(self, links, buffer):
        x, yh, z, yl, c = here()
        self.links = links
        self.buffer = buffer
        own = buffer.at[yh, yl * 2 + c]
        self.ring = {step: links.send(own, own, y_device(step)) for step in (2, 1, 3)}
        self.pair = links.send(own, own, sibling())
        self.passed = []

    def forward(self):
        x, yh, z, yl, c = here()
        for step in (1, 3, 2):
            self.ring[step].wait_recv()
            origin = lax.rem(yh * 2 + yl + 4 - step, 4)
            block = self.buffer.at[lax.div(origin, 2), lax.rem(origin, 2) * 2 + c]
            self.passed.append(self.links.send(block, block, sibling()))

    def arrived(self):
        for copy in [self.pair] + self.passed:
            copy.wait_recv()

    def done(self):
        for copy in [self.pair] + self.passed + list(self.ring.values()):
            copy.wait_send()


class ZGather:
    def __init__(self, links, buffer):
        x, yh, z, yl, c = here()
        self.links = links
        self.buffer = buffer
        self.right, self.left = z_device(1), z_device(3)
        first, second = buffer.at[z, 0:64], buffer.at[z, 64:128]
        self.right_first = links.send(first, first, self.right)
        self.left_second = links.send(second, second, self.left)
        self.right_second = links.send(second, second, self.right)
        self.left_first = links.send(first, first, self.left)

    def forward(self):
        self.right_first.wait_recv()
        block = self.buffer.at[self.left[2], 0:64]
        self.on_right = self.links.send(block, block, self.right)
        self.left_second.wait_recv()
        block = self.buffer.at[self.right[2], 64:128]
        self.on_left = self.links.send(block, block, self.left)

    def near(self):
        self.right_second.wait_recv()
        self.left_first.wait_recv()

    def far(self):
        self.on_right.wait_recv()
        self.on_left.wait_recv()

    def done(self):
        for copy in (
            self.right_first, self.left_second, self.right_second, self.left_first,
            self.on_right, self.on_left,
        ):
            copy.wait_send()


class ZScatter:
    def __init__(self, links, sends, recv_far, recv_near):
        self.links = links
        self.to_far, self.to_right, self.to_left = (sends.at[i] for i in range(3))
        self.recv_far = recv_far
        self.recv_near = recv_near
        self.right_of, self.left_of = z_device(1), z_device(3)
        self.copies = []
        self.near = []

    def send(self, source, target, device):
        copy = self.links.send(source, target, device)
        self.copies.append(copy)
        return copy

    def far(self, term):
        self.to_far[...] = term.astype(BF16)
        self.far_first = self.send(self.to_far.at[0:64], self.recv_far.at[0], self.right_of)
        self.far_second = self.send(self.to_far.at[64:128], self.recv_far.at[1], self.left_of)

    def right(self, term):
        self.to_right[...] = term.astype(BF16)
        self.near.append(
            self.send(self.to_right.at[64:128], self.recv_near.at[0, 64:128], self.right_of)
        )

    def left(self, term):
        self.to_left[...] = term.astype(BF16)
        self.near.append(
            self.send(self.to_left.at[0:64], self.recv_near.at[1, 0:64], self.left_of)
        )

    def merge(self):
        self.far_first.wait_recv()
        merged = self.to_right[0:64].astype(F32) + self.recv_far[0].astype(F32)
        self.to_right[0:64] = merged.astype(BF16)
        self.near.append(
            self.send(self.to_right.at[0:64], self.recv_near.at[0, 0:64], self.right_of)
        )
        self.far_second.wait_recv()
        merged = self.to_left[64:128].astype(F32) + self.recv_far[1].astype(F32)
        self.to_left[64:128] = merged.astype(BF16)
        self.near.append(
            self.send(self.to_left.at[64:128], self.recv_near.at[1, 64:128], self.left_of)
        )

    def total(self, own):
        for copy in self.near:
            copy.wait_recv()
        return own + self.recv_near[0].astype(F32) + self.recv_near[1].astype(F32)

    def done(self):
        for copy in self.copies:
            copy.wait_send()


class Shrink:
    def __init__(self, links, terms, pair_sum, middle, first_recv, last_recv, y_first):
        self.links = links
        self.terms = terms
        self.pair_sum = pair_sum
        self.middle = middle
        self.first_recv = first_recv
        self.last_recv = last_recv
        self.y_first = y_first
        self.copies = []

    def start(self):
        x, yh, z, yl, c = here()
        self.pair = self.links.send(self.terms.at[:, :, :, 1 - c], self.pair_sum, sibling())

    def send_first(self):
        x, yh, z, yl, c = here()
        self.pair.wait()
        terms, pair_sum = self.terms, self.pair_sum

        @pl.loop(0, 8)
        def _(at):
            h, k = lax.div(at, 4), lax.rem(at, 4)
            for low in range(2):
                pair_sum[h, k, low] = (
                    terms[h, k, low, c].astype(F32) + pair_sum[h, k, low].astype(F32)
                ).astype(BF16)

        self.first = []
        for step in (2, 1, 3):
            if self.y_first:
                device = y_device(step)
                source = pair_sum.at[device[1], :, device[3]]
            else:
                device = x_device(step)
                source = pair_sum.at[:, device[0]]
            self.first.append(self.links.send(source, self.first_recv.at[step - 1], device))

    def send_last(self):
        x, yh, z, yl, c = here()
        for copy in self.first:
            copy.wait()
        got = self.first_recv

        @pl.loop(0, 4)
        def _(at):
            if self.y_first:
                total = self.pair_sum[yh, at, yl].astype(F32)
                for slot in range(3):
                    total = total + got[slot, at].astype(F32)
                self.middle[at] = total.astype(BF16)
            else:
                h, low = lax.div(at, 2), lax.rem(at, 2)
                total = self.pair_sum[h, x, low].astype(F32)
                for slot in range(3):
                    total = total + got[slot, h, low].astype(F32)
                self.middle[h, low] = total.astype(BF16)

        self.second = []
        for step in (2, 1, 3):
            if self.y_first:
                device = x_device(step)
                source = self.middle.at[device[0]]
            else:
                device = y_device(step)
                source = self.middle.at[device[1], device[3]]
            self.second.append(self.links.send(source, self.last_recv.at[step - 1], device))

    def result(self):
        x, yh, z, yl, c = here()
        for copy in self.second:
            copy.wait()
        total = (self.middle[x] if self.y_first else self.middle[yh, yl]).astype(F32)
        for slot in range(3):
            total = total + self.last_recv[slot].astype(F32)
        return total


def shrink_scratch(rows, width, y_first):
    first = (4, rows, width) if y_first else (2, 2, rows, width)
    return [
        pltpu.VMEM((2, 4, 2, rows, width), BF16),
        pltpu.VMEM(first, BF16),
        pltpu.VMEM((3,) + first, BF16),
        pltpu.VMEM((3, rows, width), BF16),
    ]


def everyone():
    return (
        [z_device(s) for s in (1, 2, 3)]
        + [y_device(s) for s in (1, 2, 3)]
        + [x_device(s) for s in (1, 2, 3)]
        + [sibling()]
    )


GELU_A = math.sqrt(2.0 / math.pi)
GELU_B = 0.044715


def gelu_parts(gate):
    square = gate * gate
    curve = jnp.tanh(GELU_A * gate * (1.0 + GELU_B * square))
    half = 0.5 * (1.0 + curve)
    slope = half + 0.5 * gate * (1.0 - curve * curve) * (
        GELU_A * (1.0 + 3.0 * GELU_B * square)
    )
    return gate * half, slope

SCRATCH = dict(
    xn_all=((4, 128, 1024), BF16), wq_all=((2, 4, 256, 256), BF16), wkv_all=((4, 256, 512), BF16),
    q=((2, 4, 2, 128, 128), BF16), cosd=((4, 128, 128), F32), sind=((4, 128, 128), F32),
    kv_all=((2, 2, 2, 4, 2, 128, 256), BF16), attn=((4, 128, 512), BF16),
    recip=((2, 4, 256, 128), F32), wo_all=((2, 4, 256, 256), BF16), acc=((2, 4, 256, 256), F32),
    branch=((128, 1024), F32), h1=((128, 1024), F32), hn_all=((4, 128, 1024), BF16),
    wg_all=((2, 4, 256, 384), BF16), wu_all=((2, 4, 256, 384), BF16),
    wd_all=((2, 4, 256, 384), BF16),
    gate_all=((4, 128, 768), BF16), up_all=((4, 128, 768), BF16), hidden_all=((4, 128, 768), BF16),
    d_mlp_all=((4, 128, 1024), BF16), d_h1=((128, 1024), F32), d_branch_all=((4, 128, 1024), BF16),
    gain_rows=((4, 1, 1024), F32), grads=((4, 128, 1024), BF16),
    d_out=((2, 4, 256, 256), BF16), d_q=((2, 128, 1024), F32),
    d_kv=((2, 2, 2, 4, 2, 128, 256), BF16), pair_recv=((4, 2, 4, 128, 256), BF16),
    y_recv=((3, 2, 4, 128, 256), BF16),
    kv_send=((4, 8, 512), F32), kv_recv=((4, 8, 512), F32),
    gain_own=((8, 1024), F32), gain_pair=((8, 1024), F32), gain_y=((3, 8, 1024), F32),
    gain_x=((3, 8, 1024), F32), gain_z=((3, 8, 1024), F32),
    own_sum=((128, 1024), F32), z_send=((3, 128, 1024), BF16),
    z_far=((4, 2, 64, 1024), BF16), z_near=((4, 2, 128, 1024), BF16),
    terms_a=((2, 4, 2, 2, 64, 640), BF16), terms_b=((2, 4, 2, 2, 64, 512), BF16),
    terms_k=((2, 4, 2, 2, 32, 256), BF16), terms_v=((2, 4, 2, 2, 32, 256), BF16),
)
SHRINKS = (
    (64, 640, True), (64, 512, False), (64, 128, True), (64, 128, False),
    (64, 128, True), (64, 128, False), (32, 256, True), (32, 256, False),
)
SEMS = 240


class Refs:
    pass


def begin(s, links):
    x, yh, z, yl, c = here()
    xin = s.tokens[...].astype(F32)
    s.xn_all[z] = (xin * inverse_rms(xin) * s.gain_attn_in[...]).astype(BF16)
    for group in range(2):
        first = pl.multiple_of(group * 512 + z * 128, 128)
        s.wkv_all[yl * 2 + c, :, pl.ds(group * 128, 128)] = quantized(
            s.w_key[:, pl.ds(first, 128)], QEXP_MODEL, 8
        )
        s.wkv_all[yl * 2 + c, :, pl.ds(256 + group * 128, 128)] = quantized(
            s.w_value[:, pl.ds(first, 128)], QEXP_MODEL, 8
        )
    s.wq_all[yh, yl * 2 + c] = quantized(s.w_query[...], QEXP_MODEL, 8)
    s.wo_all[yh, yl * 2 + c] = quantized(s.w_output[...], QEXP_MODEL, 8)
    greet(everyone())
    ring = ZGather(links, s.xn_all)
    key_part = s.wkv_all.at[yl * 2 + c, :, 0:256]
    value_part = s.wkv_all.at[yl * 2 + c, :, 256:512]
    from_low = links.send(key_part, key_part, y_device(1))
    from_high = links.send(value_part, value_part, y_device(3))
    own = s.wkv_all.at[yl * 2 + c]
    pair = links.send(own, own, sibling())
    s.gather_q = Gather(links, s.wq_all)
    s.gather_o = Gather(links, s.wo_all)
    lane = lax.broadcasted_iota(jnp.int32, (128, 128), 1)
    row = lax.broadcasted_iota(jnp.int32, (128, 128), 0)
    freqs = jnp.exp(lax.rem(lane, 64).astype(F32) * (-2.0 * math.log(THETA) / DH))
    start = s.lengths[0, 0]
    base = yh * 2048 + yl * 256 + c * 128

    def tables(block):
        tok = row + (base + block * 512)
        angle = jnp.where(tok >= start, tok - start, tok).astype(F32) * freqs
        s.cosd[block] = jnp.cos(angle)
        sine = jnp.sin(angle)
        s.sind[block] = jnp.where(lane < 64, -sine, sine)

    tables(0)
    tables(1)
    ring.forward()
    from_low.wait_recv()
    from_high.wait_recv()
    other = s.wkv_all.at[(1 - yl) * 2 + c]
    passed = links.send(other, other, sibling())
    tables(2)
    tables(3)
    s.gather_q.forward()
    pair.wait_recv()
    passed.wait_recv()

    def project_kv(block):
        lin = dot(s.xn_all[block], s.wkv_all[...].reshape(1024, 512))
        cosd, sind = s.cosd[block], s.sind[block]
        for group in range(2):
            key = lin[:, group * 128 : group * 128 + 128]
            key = (key * cosd + swap_halves(key) * sind).astype(BF16)
            value = lin[:, 256 + group * 128 : 384 + group * 128].astype(BF16)
            s.kv_all[group, yh, yl, block, c, :, 0:128] = key
            s.kv_all[group, yh, yl, block, c, :, 128:256] = value

    def project_q(block):
        cosd, sind = s.cosd[block], s.sind[block]
        for group in range(2):
            lin = dot(s.xn_all[block], s.wq_all[group].reshape(1024, 256))
            for head in range(2):
                query = lin[:, head * 128 : head * 128 + 128]
                query = (query * cosd + swap_halves(query) * sind) * SCALE
                s.q[group, block, head] = query.astype(BF16)

    project_kv(z)
    ring.near()
    project_kv(ring.left[2])
    project_kv(ring.right[2])
    ring.far()
    project_kv(lax.rem(z + 2, 4))
    s.kv_pair, s.kv_near, s.kv_far, s.kv_last = [], [], [], []
    for group in range(2):
        mine = s.kv_all.at[group, yh, yl, :, c]
        s.kv_pair.append(links.send(mine, mine, sibling()))
        s.kv_near.append(links.send(mine, mine, (x, yh, z, 1 - yl, c)))
        s.kv_far.append(links.plan(mine, mine, (x, 1, z, 1 - yl, c)))
        s.kv_last.append(links.plan(mine, mine, (x, 1, z, yl, c)))

        @pl.when(yh == 0)
        def _():
            s.kv_far[group].start()

    s.gather_q.arrived()
    for block in range(4):
        project_q(block)
    ring.done()
    for copy in (from_low, from_high, pair, passed):
        copy.wait_send()
    s.gather_q.done()


def attend(s, links):
    x, yh, z, yl, c = here()
    start = s.lengths[0, 0]
    lane = lax.broadcasted_iota(jnp.int32, (1, 256), 1)
    ones = jnp.ones((256, 128), BF16)
    row = lax.rem(lax.broadcasted_iota(jnp.int32, (256, 1), 0), 128)

    def add_block(group, block, from_h, from_l, units, diagonal, first):
        query = s.q[group, block].reshape(256, 128)
        token_q = row + (yh * 2048 + block * 512 + yl * 256 + c * 128)
        floor = jnp.where(token_q >= start, start, 0)
        total = None
        for unit in units:
            both = s.kv_all[group, from_h, from_l, unit].reshape(256, 256)
            token_k = lane + (from_h * 2048 + unit * 512 + from_l * 256)
            curved = jnp.tanh(dot_nt(query, both[:, :128]) * (1.0 / CAP))
            weight = jnp.exp2(curved * (CAP * LOG2E))
            seen = token_k >= floor
            if diagonal and unit == units[-1]:
                seen = seen & (token_k <= token_q)
            weight = jnp.where(seen, weight, 0.0).astype(BF16)
            term = dot(weight, jnp.concatenate([both[:, 128:], ones], axis=1))
            total = term if total is None else total + term
        if first:
            s.acc[group, block] = total
        else:
            s.acc[group, block] += total

    def same_half(group, from_l, first):
        for block in range(4):
            add_block(group, block, yh, from_l, list(range(block + 1)), True, first)

    def other_half(group, from_l):
        @pl.loop(0, 4)
        def _(block):
            add_block(group, block, 0, from_l, [0, 1, 2, 3], False, False)

    def pass_plan(group, from_h, from_l):
        block = s.kv_all.at[group, from_h, from_l, :, c]
        return links.plan(block, block, sibling())

    near_pass = [pass_plan(group, yh, 1 - yl) for group in range(2)]
    far_pass = [pass_plan(group, 0, 1 - yl) for group in range(2)]
    last_pass = [pass_plan(group, 0, yl) for group in range(2)]
    s.kv_pair[0].wait_recv()
    same_half(0, yl, True)

    @pl.when(yh == 0)
    def _():
        for group in range(2):
            s.kv_last[group].start()

    s.kv_pair[1].wait_recv()
    same_half(1, yl, True)
    for group in range(2):
        s.kv_near[group].wait_recv()
        near_pass[group].start()

        @pl.when(yh == 1)
        def _():
            s.kv_far[group].wait_recv()
            far_pass[group].start()

        near_pass[group].wait_recv()
        same_half(group, 1 - yl, False)

        @pl.when(yh == 1)
        def _():
            far_pass[group].wait_recv()
            other_half(group, 1 - yl)

    for weight, target, exponent, bits in (
        (s.w_gate, s.wg_all, QEXP_MODEL, 4),
        (s.w_up, s.wu_all, QEXP_MODEL, 4),
        (s.w_down, s.wd_all, QEXP_HIDDEN, 2),
    ):
        target[yh, yl * 2 + c] = quantized(weight[...], exponent, bits)
    s.gather_gate = Gather(links, s.wg_all)
    s.gather_up = Gather(links, s.wu_all)
    s.gather_down = Gather(links, s.wd_all)

    @pl.when(yh == 1)
    def _():
        for group in range(2):
            s.kv_last[group].wait_recv()
            last_pass[group].start()
        for group in range(2):
            last_pass[group].wait_recv()
            other_half(group, yl)

    s.gather_o.forward()
    for group in range(2):
        for block in range(4):
            total = s.acc[group, block]
            inverse = 1.0 / total[:, 128:256]
            s.recip[group, block] = inverse
            out = (total[:, :128] * inverse).astype(BF16)
            for head in range(2):
                first = group * 256 + head * 128
                s.attn[block, :, first : first + 128] = out[head * 128 : head * 128 + 128]
    for group in range(2):
        s.kv_pair[group].wait_send()
        s.kv_near[group].wait_send()
        near_pass[group].wait_send()

    @pl.when(yh == 0)
    def _():
        for group in range(2):
            s.kv_far[group].wait_send()
            s.kv_last[group].wait_send()

    @pl.when(yh == 1)
    def _():
        for group in range(2):
            far_pass[group].wait_send()
            last_pass[group].wait_send()


def all_terms(scatter, term_of):
    x, yh, z, yl, c = here()
    scatter.far(term_of(lax.rem(z + 2, 4)))
    scatter.right(term_of(lax.rem(z + 1, 4)))
    scatter.left(term_of(lax.rem(z + 3, 4)))
    scatter.merge()
    return term_of(z)


def output_projection(s, links):
    x, yh, z, yl, c = here()

    def term_of(block):
        left = s.attn[block]
        return dot_nt(left[:, :256], s.wo_all[0].reshape(1024, 256)) + dot_nt(
            left[:, 256:], s.wo_all[1].reshape(1024, 256)
        )

    s.gather_o.arrived()
    scatter = ZScatter(links, s.z_send, s.z_far.at[0], s.z_near.at[0])
    own = all_terms(scatter, term_of)
    s.gather_gate.forward()
    branch = scatter.total(own)
    h1 = s.tokens[...].astype(F32) + branch * inverse_rms(branch) * s.gain_attn_out[...]
    s.hn_all[z] = (h1 * inverse_rms(h1) * s.gain_mlp_in[...]).astype(BF16)
    s.ring = ZGather(links, s.hn_all)
    s.branch[...] = branch
    s.h1[...] = h1
    s.gather_up.forward()
    s.gather_gate.arrived()
    s.gather_up.arrived()
    scatter.done()
    s.gather_o.done()
    s.gather_gate.done()


def feed_forward(s, links):
    x, yh, z, yl, c = here()

    def term_of(block):
        left = s.hn_all[block]
        total = None
        for group in range(2):
            cols = slice(group * 384, group * 384 + 384)
            gate = dot(left, s.wg_all[group].reshape(1024, 384))
            up = dot(left, s.wu_all[group].reshape(1024, 384))
            value, slope = gelu_parts(gate)
            s.gate_all[block, :, cols] = value.astype(BF16)
            s.up_all[block, :, cols] = (up * slope).astype(BF16)
            hidden = (value * up).astype(BF16)
            s.hidden_all[block, :, cols] = hidden
            term = dot_nt(hidden, s.wd_all[group].reshape(1024, 384))
            total = term if total is None else total + term
        return total

    s.ring.forward()
    s.gather_down.forward()
    s.gather_down.arrived()
    scatter = ZScatter(links, s.z_send, s.z_far.at[1], s.z_near.at[1])
    ring = s.ring
    s.own_sum[...] = term_of(z)
    ring.near()
    scatter.left(term_of(ring.left[2]))
    scatter.right(term_of(ring.right[2]))
    ring.far()
    scatter.far(term_of(lax.rem(z + 2, 4)))
    scatter.merge()
    mlp = scatter.total(s.own_sum[...])
    into, gain_part = rms_back(mlp, s.gain_mlp_out[...], s.out_grad[...].astype(F32))
    s.d_mlp_all[z] = into.astype(BF16)
    s.ring = ZGather(links, s.d_mlp_all)
    s.gain_rows[3] = gain_part
    s.mixed[...] = (s.h1[...] + mlp * inverse_rms(mlp) * s.gain_mlp_out[...]).astype(BF16)
    ring.done()
    scatter.done()
    s.gather_up.done()
    s.gather_down.done()


def feed_forward_back(s, links):
    x, yh, z, yl, c = here()

    def term_of(block):
        left = s.d_mlp_all[block]
        total = None
        for group in range(2):
            cols = slice(group * 384, group * 384 + 384)
            d_hidden = dot(left, s.wd_all[group].reshape(1024, 384))
            d_gate = (d_hidden * s.up_all[block, :, cols].astype(F32)).astype(BF16)
            d_up = (d_hidden * s.gate_all[block, :, cols].astype(F32)).astype(BF16)
            s.up_all[block, :, cols] = d_gate
            s.gate_all[block, :, cols] = d_up
            term = dot_nt(d_gate, s.wg_all[group].reshape(1024, 384)) + dot_nt(
                d_up, s.wu_all[group].reshape(1024, 384)
            )
            total = term if total is None else total + term
        return total

    scatter = ZScatter(links, s.z_send, s.z_far.at[2], s.z_near.at[2])
    ring = s.ring
    s.own_sum[...] = term_of(z)
    ring.forward()
    ring.near()
    scatter.left(term_of(ring.left[2]))
    scatter.right(term_of(ring.right[2]))
    ring.far()
    scatter.far(term_of(lax.rem(z + 2, 4)))
    d_mlp = s.d_mlp_all[...].reshape(512, 1024)
    hn = s.hn_all[...].reshape(512, 1024)
    for group in range(2):
        cols = slice(group * 384, group * 384 + 384)
        down = dot_tn(d_mlp, s.hidden_all[:, :, cols].reshape(512, 384)).astype(BF16)
        s.terms_a[group, :, :, :, :, 0:384] = down.reshape(4, 2, 2, 64, 384)
    scatter.merge()
    for group in range(2):
        cols = slice(group * 384, group * 384 + 384)
        gate = dot_tn(hn, s.up_all[:, :, cols].reshape(512, 384)).astype(BF16)
        gate = gate.reshape(4, 2, 2, 64, 384)
        s.terms_a[group, :, :, :, :, 384:640] = gate[..., 0:256]
        s.terms_b[group, :, :, :, :, 0:128] = gate[..., 256:384]
    s.shrink[0].start()
    d_hn = scatter.total(s.own_sum[...])
    into, gain_part = rms_back(s.h1[...], s.gain_mlp_in[...], d_hn)
    s.gain_rows[2] = gain_part
    d_h1 = s.out_grad[...].astype(F32) + into
    s.d_h1[...] = d_h1
    into, gain_part = rms_back(s.branch[...], s.gain_attn_out[...], d_h1)
    s.d_branch_all[z] = into.astype(BF16)
    s.ring = ZGather(links, s.d_branch_all)
    s.gain_rows[1] = gain_part
    s.shrink[0].send_first()
    for group in range(2):
        cols = slice(group * 384, group * 384 + 384)
        up = dot_tn(hn, s.gate_all[:, :, cols].reshape(512, 384)).astype(BF16)
        s.terms_b[group, :, :, :, :, 128:512] = up.reshape(4, 2, 2, 64, 384)
    s.shrink[1].start()
    s.ring.forward()
    ring.done()
    scatter.done()


def attend_back(s, links):
    x, yh, z, yl, c = here()
    ring = s.ring
    lane = lax.broadcasted_iota(jnp.int32, (256, 128), 1)

    def cotangent(block):
        for group in range(2):
            cols = slice(group * 256, group * 256 + 256)
            rows = dot(s.d_branch_all[block], s.wo_all[group].reshape(1024, 256))
            rows = rows.astype(BF16).astype(F32)
            rows = jnp.concatenate([rows[:, :128], rows[:, 128:]], axis=0)
            outs = s.attn[block, :, cols].astype(F32)
            outs = jnp.concatenate([outs[:, :128], outs[:, 128:]], axis=0)
            scaled = (rows * s.recip[group, block]).astype(BF16)
            inner = -jnp.sum(scaled.astype(F32) * outs, axis=1, keepdims=True)
            high = inner.astype(BF16)
            low = (inner - high.astype(F32)).astype(BF16)
            extra = jnp.where(
                lane == 0, high.astype(F32), jnp.where(lane == 1, low.astype(F32), 0.0)
            )
            s.d_out[group, block] = jnp.concatenate([scaled, extra.astype(BF16)], axis=1)

    cotangent(z)
    s.d_q[...] = jnp.zeros_like(s.d_q)
    ring.near()
    cotangent(ring.left[2])
    cotangent(ring.right[2])
    s.shrink[1].send_first()
    ring.far()
    cotangent(lax.rem(z + 2, 4))
    d_branch = s.d_branch_all[...].reshape(512, 1024)
    for group in range(2):
        cols = slice(group * 256, group * 256 + 256)
        back = dot_tn(d_branch, s.attn[:, :, cols].reshape(512, 256)).astype(BF16)
        back = back.reshape(4, 2, 2, 64, 256)
        s.terms_a[group, :, :, :, :, 0:128] = back[..., 0:128]
        s.terms_b[group, :, :, :, :, 0:128] = back[..., 128:256]
    s.shrink[2].start()
    s.shrink[3].start()
    start = s.lengths[0, 0]
    ones = jnp.where(lane < 2, 1.0, 0.0).astype(BF16)
    token_row = lax.rem(lax.broadcasted_iota(jnp.int32, (1, 256), 1), 128)
    token_col = lax.broadcasted_iota(jnp.int32, (256, 1), 0)

    def unit_back(group, from_h, from_l, unit, first_block, diagonal):
        both = s.kv_all[group, from_h, from_l, unit].reshape(256, 256)
        key, value = both[:, :128], both[:, 128:]
        count = 4 - first_block
        query = s.q[group, first_block:].reshape(count * 256, 128)
        cot = s.d_out[group, first_block:].reshape(count * 256, 256)
        curved = jnp.tanh(dot_nt(key, query) * (1.0 / CAP))
        weight = jnp.exp2(curved * (CAP * LOG2E))
        token_k = token_col + (from_h * 2048 + unit * 512 + from_l * 256)
        pieces = []
        for block in range(first_block, 4):
            token_q = token_row + (yh * 2048 + block * 512 + yl * 256 + c * 128)
            seen = token_k >= jnp.where(token_q >= start, start, 0)
            if diagonal and block == first_block:
                seen = seen & (token_k <= token_q)
            at = (block - first_block) * 256
            pieces.append(jnp.where(seen, weight[:, at : at + 256], 0.0))
        weight = jnp.concatenate(pieces, axis=1)
        grown = dot_nt(jnp.concatenate([value, ones], axis=1), cot)
        slope = (weight * grown * (1.0 - curved * curved)).astype(BF16)
        d_key = dot(slope, query)
        d_value = dot(weight.astype(BF16), cot[:, :128])
        s.d_kv[group, from_h, from_l, unit] = (
            jnp.concatenate([d_key, d_value], axis=1).astype(BF16).reshape(2, 128, 256)
        )
        s.d_q[group, :, first_block * 256 :] += dot(key.T, slope)

    def same_half(group, from_l):
        for unit in range(4):
            unit_back(group, yh, from_l, unit, unit, True)

    def other_half(from_l):
        @pl.loop(0, 8)
        def _(at):
            unit_back(lax.div(at, 4), 0, from_l, lax.rem(at, 4), 0, False)

    def pair_plan(slot, from_h, from_l):
        return links.plan(
            s.d_kv.at[:, from_h, from_l, :, 1 - c], s.pair_recv.at[slot], sibling()
        )

    def add_pair(slot, from_h, from_l):
        s.d_kv[:, from_h, from_l, :, c] = (
            s.d_kv[:, from_h, from_l, :, c].astype(F32) + s.pair_recv[slot].astype(F32)
        ).astype(BF16)

    def own_part(from_h, from_l):
        return s.d_kv.at[:, from_h, from_l, :, c]

    far_pair = [pair_plan(0, 0, 1 - yl), pair_plan(1, 0, yl)]
    far_send = [
        links.plan(own_part(0, 1 - yl), s.y_recv.at[0], (x, 0, z, 1 - yl, c)),
        links.plan(own_part(0, yl), s.y_recv.at[1], (x, 0, z, yl, c)),
    ]

    @pl.when(yh == 1)
    def _():
        other_half(1 - yl)
        far_pair[0].start()
        s.y_recv[0:2] = jnp.zeros((2, 2, 4, 128, 256), BF16)
        other_half(yl)
        far_pair[1].start()
        far_pair[0].wait()
        add_pair(0, 0, 1 - yl)
        far_send[0].start()

    for i in (0, 1):
        s.shrink[i].send_last()
    for i in (2, 3):
        s.shrink[i].send_first()
    same_half(0, 1 - yl)

    @pl.when(yh == 1)
    def _():
        far_pair[1].wait()
        add_pair(1, 0, yl)
        far_send[1].start()

    same_half(1, 1 - yl)
    near_pair = pair_plan(2, yh, 1 - yl)
    near_pair.start()
    same_half(0, yl)
    near_pair.wait()
    add_pair(2, yh, 1 - yl)
    near_send = links.send(own_part(yh, 1 - yl), s.y_recv.at[2], (x, yh, z, 1 - yl, c))
    same_half(1, yl)
    own_pair = pair_plan(3, yh, yl)
    own_pair.start()

    def rope_back(values, block):
        return values * s.cosd[block] - swap_halves(values) * s.sind[block]

    for group in range(2):
        d_query = s.d_q[group].T
        for block in range(4):
            for head in range(2):
                first = block * 256 + head * 128
                turned = rope_back(d_query[first : first + 128], block) * SCALE
                at = group * 256 + head * 128
                s.grads[block, :, at : at + 128] = turned.astype(BF16)
    xa = s.xn_all[...].reshape(512, 1024)
    for group in range(2):
        back = dot_tn(xa, s.grads[:, :, group * 256 : group * 256 + 256].reshape(512, 256))
        back = back.astype(BF16).reshape(4, 2, 2, 64, 256)
        s.terms_a[group, :, :, :, :, 0:128] = back[..., 0:128]
        s.terms_b[group, :, :, :, :, 0:128] = back[..., 128:256]
    s.shrink[4].start()
    s.shrink[5].start()
    first = s.shrink[0].result()
    s.dwd[...] = first[:, 0:384]
    s.dwg[:, 0:256] = first[:, 384:640]
    second = s.shrink[1].result()
    s.dwg[:, 256:384] = second[:, 0:128]
    s.dwu[...] = second[:, 128:512]
    for i in (2, 3):
        s.shrink[i].send_last()
    for i in (4, 5):
        s.shrink[i].send_first()
    own_pair.wait()
    near_send.wait()

    @pl.when(yh == 0)
    def _():
        for slot in range(2):
            far_send[slot].wait_recv()

    @pl.when(yh == 1)
    def _():
        for slot in range(2):
            far_send[slot].wait_send()

    for group in range(2):
        for block in range(4):
            both = (
                s.d_kv[group, yh, yl, block, c].astype(F32)
                + s.pair_recv[3, group, block].astype(F32)
                + s.y_recv[2, group, block].astype(F32)
                + s.y_recv[0, group, block].astype(F32)
                + s.y_recv[1, group, block].astype(F32)
            )
            d_key = both[:, :128].astype(BF16).astype(F32)
            at = 512 + group * 128
            s.grads[block, :, at : at + 128] = rope_back(d_key, block).astype(BF16)
            at = 768 + group * 128
            s.grads[block, :, at : at + 128] = both[:, 128:].astype(BF16)
    ring.done()


def finish(s, links):
    x, yh, z, yl, c = here()
    s.gain_own[...] = jnp.zeros_like(s.gain_own)

    def term_of(block):
        left = s.grads[block]
        total = dot_nt(left[:, 512:], s.wkv_all[...].reshape(1024, 512))
        for group in range(2):
            total = total + dot_nt(
                left[:, group * 256 : group * 256 + 256], s.wq_all[group].reshape(1024, 256)
            )
        s.gain_own[0:1] += jnp.sum(total * s.xn_all[block].astype(F32), axis=0, keepdims=True)
        return total

    scatter = ZScatter(links, s.z_send, s.z_far.at[3], s.z_near.at[3])
    scatter.far(term_of(lax.rem(z + 2, 4)))
    xa = s.xn_all[...].reshape(512, 1024)
    back = dot_tn(xa, s.grads[:, :, 512:].reshape(512, 512))
    for k in range(4):
        for h in range(2):
            for low in range(2):
                for core in range(2):
                    rows = [k * 256 + h * 128 + low * 16 + core * 8 + 32 * i for i in range(4)]
                    piece = jnp.concatenate([back[row : row + 8] for row in rows], axis=0)
                    piece = piece.astype(BF16)
                    s.terms_k[h, k, low, core] = piece[:, :256]
                    s.terms_v[h, k, low, core] = piece[:, 256:]
    s.shrink[6].start()
    s.shrink[7].start()
    scatter.right(term_of(lax.rem(z + 1, 4)))
    scatter.left(term_of(lax.rem(z + 3, 4)))
    scatter.merge()
    s.shrink[6].send_first()
    s.shrink[7].send_first()
    own = term_of(z)
    s.gain_own[0:1] = s.gain_own[0:1] / s.gain_attn_in[...]
    for i in (1, 2, 3):
        s.gain_own[i : i + 1] = s.gain_rows[i]
    pair = links.send(s.gain_own, s.gain_pair, sibling())
    for i in (4, 5):
        s.shrink[i].send_last()
    pair.wait()
    s.gain_pair[...] += s.gain_own[...]
    sent = [links.send(s.gain_pair, s.gain_y.at[k - 1], y_device(k)) for k in (2, 1, 3)]
    s.shrink[6].send_last()
    s.shrink[7].send_last()
    for copy in sent:
        copy.wait()
    s.gain_own[...] = s.gain_pair[...] + (s.gain_y[0] + s.gain_y[2]) + s.gain_y[1]
    sent = [links.send(s.gain_own, s.gain_x.at[k - 1], x_device(k)) for k in (2, 1, 3)]
    d_xn = scatter.total(own)
    into, _ = rms_back(s.tokens[...].astype(F32), s.gain_attn_in[...], d_xn)
    s.tokens_grad[...] = (s.d_h1[...] + into).astype(BF16)
    s.dwo[:, 0:128] = s.shrink[2].result()
    s.dwo[:, 128:256] = s.shrink[3].result()
    for copy in sent:
        copy.wait()
    s.gain_pair[...] = s.gain_own[...] + (s.gain_x[0] + s.gain_x[2]) + s.gain_x[1]
    sent = [links.send(s.gain_pair, s.gain_z.at[k - 1], z_device(k)) for k in (2, 1, 3)]
    s.kv_send[:, :, 0:256] = s.shrink[6].result().reshape(4, 8, 256)
    s.kv_send[:, :, 256:512] = s.shrink[7].result().reshape(4, 8, 256)
    moved = []
    for step in (2, 1, 3):
        device = z_device(step)
        moved.append(links.send(s.kv_send.at[device[2]], s.kv_recv.at[z], device))
    s.kv_recv[z] = s.kv_send[z]
    s.dwq[:, 0:128] = s.shrink[4].result()
    s.dwq[:, 128:256] = s.shrink[5].result()
    for copy in sent:
        copy.wait()
    s.gains[...] = s.gain_pair[...] + (s.gain_z[0] + s.gain_z[2]) + s.gain_z[1]
    for copy in moved:
        copy.wait()
    for origin in range(4):
        for group in range(2):
            at = group * 512 + origin * 128
            s.dwk[:, at : at + 128] = s.kv_recv[origin, :, group * 128 : group * 128 + 128]
            s.dwv[:, at : at + 128] = s.kv_recv[
                origin, :, 256 + group * 128 : 384 + group * 128
            ]
    scatter.done()


OPERANDS = (
    "tokens", "lengths", "w_query", "w_key", "w_value", "w_output", "w_gate", "w_up", "w_down",
    "gain_attn_in", "gain_attn_out", "gain_mlp_in", "gain_mlp_out", "out_grad",
)
RESULTS = dict(
    mixed=((128, 1024), BF16), tokens_grad=((128, 1024), BF16), dwq=((64, 256), F32),
    dwk=((8, 1024), F32), dwv=((8, 1024), F32), dwo=((64, 256), F32), dwg=((64, 384), F32),
    dwu=((64, 384), F32), dwd=((64, 384), F32), gains=((8, 1024), F32),
)


def layer_kernel(*refs):
    s = Refs()
    names = list(OPERANDS) + list(RESULTS) + list(SCRATCH)
    for name, ref in zip(names, refs):
        setattr(s, name, ref)
    rest = refs[len(names) :]
    links = Links(rest[-2], rest[-1])
    terms = (
        s.terms_a, s.terms_b, s.terms_a.at[..., 0:128], s.terms_b.at[..., 0:128],
        s.terms_a.at[..., 0:128], s.terms_b.at[..., 0:128], s.terms_k, s.terms_v,
    )
    s.shrink = [
        Shrink(links, terms[i], *rest[4 * i : 4 * i + 4], SHRINKS[i][2])
        for i in range(len(SHRINKS))
    ]
    begin(s, links)
    attend(s, links)
    output_projection(s, links)
    feed_forward(s, links)
    feed_forward_back(s, links)
    attend_back(s, links)
    finish(s, links)


def run_layer(*operands):
    scratch = [pltpu.VMEM(shape, kind) for shape, kind in SCRATCH.values()]
    for rows, width, y_first in SHRINKS:
        scratch += shrink_scratch(rows, width, y_first)
    scratch += [pltpu.SemaphoreType.DMA((SEMS,))] * 2
    return pl.pallas_call(
        layer_kernel,
        name="layer",
        out_shape=tuple(jax.ShapeDtypeStruct(shape, kind) for shape, kind in RESULTS.values()),
        in_specs=[VM, SM] + [VM] * 12,
        out_specs=tuple(VM for _ in RESULTS),
        scratch_shapes=scratch,
        compiler_params=pltpu.CompilerParams(
            collective_id=1, has_side_effects=True, vmem_limit_bytes=VMEM_LIMIT
        ),
    )(*operands)


def leave_kernel(*refs):
    count = len(refs) // 2
    for i in range(count):
        refs[count + i][...] = refs[i][...]


def run_leave(results):
    return pl.pallas_call(
        leave_kernel,
        name="leave",
        out_shape=tuple(jax.ShapeDtypeStruct(r.shape, r.dtype) for r in results),
        in_specs=[VM] * len(results),
        out_specs=tuple(VM for _ in results),
    )(*results)


def per_device(
    tokens, lengths, w_query, w_key, w_value, w_output, w_gate, w_up, w_down,
    gain_attn_in, gain_attn_out, gain_mlp_in, gain_mlp_out, out_grad,
):
    gain_rows = [
        gain.reshape(1, -1) for gain in (gain_attn_in, gain_attn_out, gain_mlp_in, gain_mlp_out)
    ]
    *results, gains = run_layer(
        tokens, lengths, w_query, w_key, w_value, w_output, w_gate, w_up, w_down,
        *gain_rows, out_grad,
    )
    x, yh, z, yl, c = here()
    first = ((((x * 2 + yh) * 4 + z) * 2 + yl) * 2 + c) * 8
    own_gains = lax.dynamic_slice(gains, (0, first), (4, 8))
    return tuple(run_leave(results)) + tuple(own_gains[i] for i in range(4))


def solution(mesh):
    grid = Mesh(mesh.devices.reshape(4, 2, 4, 2, 2), AXES)
    tokens = P(AXES, None)
    split = P(("yl", "c"), ("yh", "z"))
    rows = P(("yl", "c"), None)
    grads = P(("x", "yl", "c"), ("yh", "z"))
    gains = P(AXES)
    return jax.shard_map(
        per_device,
        mesh=grid,
        in_specs=(tokens, P("x", None), split, rows, rows, split, split, split, split)
        + (P(),) * 4
        + (tokens,),
        out_specs=(tokens, tokens, grads, tokens, tokens, grads, grads, grads, grads)
        + (gains,) * 4,
        check_vma=False,
    )
```

```python
import math

import jax
import jax.numpy as jnp
from jax import lax
from jax.experimental import pallas as pl
from jax.experimental.pallas import tpu as pltpu
from jax.sharding import Mesh
from jax.sharding import PartitionSpec as P

DH = 128
QEXP_MODEL = 10
QEXP_HIDDEN = 11
CAP = 50.0
EPSILON = 1e-06
THETA = 10000.0
SCALE = DH ** (-0.5)
AXES = ("x", "yh", "z", "yl", "c")
BY_ID = pl.DeviceIdType.MESH
F32 = jnp.float32
BF16 = jnp.bfloat16
VM = pl.BlockSpec(memory_space=pltpu.VMEM)
SM = pl.BlockSpec(memory_space=pltpu.SMEM)
LOG2E = 1.4426950408889634
VMEM_LIMIT = 63 * 2**20


def here():
    return tuple(lax.axis_index(name) for name in AXES)


def z_device(step):
    x, yh, z, yl, c = here()
    return (x, yh, lax.rem(z + step, 4), yl, c)


def y_device(step):
    x, yh, z, yl, c = here()
    y = lax.rem(yh * 2 + yl + step, 4)
    return (x, lax.div(y, 2), z, lax.rem(y, 2), c)


def x_device(step):
    x, yh, z, yl, c = here()
    return (lax.rem(x + step, 4), yh, z, yl, c)


def sibling():
    x, yh, z, yl, c = here()
    return (x, yh, z, yl, 1 - c)


def mate():
    x, yh, z, yl, c = here()
    return (x, 1 - yh, z, 1 - yl, c)


def greet(devices):
    barrier = pltpu.get_barrier_semaphore()
    for device in devices:
        pl.semaphore_signal(barrier, inc=1, device_id=device, device_id_type=BY_ID)
    pl.semaphore_wait(barrier, len(devices))


class Links:
    def __init__(self, send_sems, recv_sems):
        self.send_sems = send_sems
        self.recv_sems = recv_sems
        self.used = 0

    def plan(self, source, target, device):
        at = self.used
        self.used += 1
        return pltpu.make_async_remote_copy(
            src_ref=source,
            dst_ref=target,
            send_sem=self.send_sems.at[at],
            recv_sem=self.recv_sems.at[at],
            device_id=device,
            device_id_type=BY_ID,
        )

    def send(self, source, target, device):
        copy = self.plan(source, target, device)
        copy.start()
        return copy


def dot(left, right):
    return lax.dot_general(left, right, (((1,), (0,)), ((), ())), preferred_element_type=F32)


def dot_nt(left, right):
    return lax.dot_general(left, right, (((1,), (1,)), ((), ())), preferred_element_type=F32)


def dot_tn(left, right):
    return lax.dot_general(left, right, (((0,), (0,)), ((), ())), preferred_element_type=F32)


def quantized(weight, exponent, bits):
    shift = 8 - bits
    code = jnp.clip(jnp.floor(weight.astype(F32) * 2.0**exponent) + 128.0, 0.0, 255.0)
    if shift:
        code = (
            jnp.minimum(jnp.floor((code + 2.0 ** (shift - 1)) * 2.0 ** (-shift)), 2.0**bits - 1.0)
            * 2.0**shift
        )
    return ((code - 128.0) * 2.0 ** (-exponent)).astype(BF16)


def inverse_rms(values):
    return lax.rsqrt(jnp.mean(values * values, axis=-1, keepdims=True) + EPSILON)


def rms_back(values, gain, incoming):
    inverse = inverse_rms(values)
    scaled = incoming * gain
    inner = jnp.mean(scaled * values, axis=-1, keepdims=True)
    into = inverse * (scaled - values * (inverse * inverse) * inner)
    gain_part = jnp.sum(incoming * values * inverse, axis=0, keepdims=True)
    return into, gain_part


def swap_halves(values):
    half = values.shape[-1] // 2
    return jnp.concatenate([values[..., half:], values[..., :half]], axis=-1)


class Gather:
    def __init__(self, links, buffer):
        x, yh, z, yl, c = here()
        self.links = links
        self.buffer = buffer
        quarter = buffer.at[yh, yl, c, x]
        self.ring = {step: links.send(quarter, quarter, y_device(step)) for step in (2, 1, 3)}
        own = buffer.at[yh, yl, c]
        self.pair = links.send(own, own, sibling())
        self.across = {}
        self.passed = []

    def origin(self, step):
        x, yh, z, yl, c = here()
        y = lax.rem(yh * 2 + yl + 4 - step, 4)
        return (lax.div(y, 2), lax.rem(y, 2), c)

    def spread(self):
        x = lax.axis_index("x")
        for step in (1, 3, 2):
            self.ring[step].wait_recv()
            block = self.buffer.at[self.origin(step) + (x,)]
            self.across[step] = [
                self.links.send(block, block, x_device(k)) for k in (2, 1, 3)
            ]

    def forward(self):
        for step in (1, 3, 2):
            for copy in self.across[step]:
                copy.wait_recv()
            block = self.buffer.at[self.origin(step)]
            self.passed.append(self.links.send(block, block, sibling()))

    def arrived(self):
        for copy in [self.pair] + self.passed:
            copy.wait_recv()

    def done(self):
        for copy in [self.pair] + self.passed + list(self.ring.values()):
            copy.wait_send()
        for copies in self.across.values():
            for copy in copies:
                copy.wait_send()


class ZGather:
    def __init__(self, links, buffer):
        x, yh, z, yl, c = here()
        self.links = links
        self.buffer = buffer
        self.right, self.left = z_device(1), z_device(3)
        first, second = buffer.at[z, 0:64], buffer.at[z, 64:128]
        self.right_first = links.send(first, first, self.right)
        self.left_second = links.send(second, second, self.left)
        self.right_second = links.send(second, second, self.right)
        self.left_first = links.send(first, first, self.left)

    def forward(self):
        self.right_first.wait_recv()
        block = self.buffer.at[self.left[2], 0:64]
        self.on_right = self.links.send(block, block, self.right)
        self.left_second.wait_recv()
        block = self.buffer.at[self.right[2], 64:128]
        self.on_left = self.links.send(block, block, self.left)

    def near(self):
        self.right_second.wait_recv()
        self.left_first.wait_recv()

    def far(self):
        self.on_right.wait_recv()
        self.on_left.wait_recv()

    def done(self):
        for copy in (
            self.right_first, self.left_second, self.right_second, self.left_first,
            self.on_right, self.on_left,
        ):
            copy.wait_send()


class ZScatter:
    def __init__(self, links, sends, recv_far, recv_near):
        self.links = links
        self.to_far, self.to_right, self.to_left = (sends.at[i] for i in range(3))
        self.recv_far = recv_far
        self.recv_near = recv_near
        self.right_of, self.left_of = z_device(1), z_device(3)
        self.copies = []
        self.near = []

    def send(self, source, target, device):
        copy = self.links.send(source, target, device)
        self.copies.append(copy)
        return copy

    def far(self, term):
        self.to_far[...] = term.astype(BF16)
        self.far_first = self.send(self.to_far.at[0:64], self.recv_far.at[0], self.right_of)
        self.far_second = self.send(self.to_far.at[64:128], self.recv_far.at[1], self.left_of)

    def right(self, term):
        self.to_right[...] = term.astype(BF16)
        self.near.append(
            self.send(self.to_right.at[64:128], self.recv_near.at[0, 64:128], self.right_of)
        )

    def left(self, term):
        self.to_left[...] = term.astype(BF16)
        self.near.append(
            self.send(self.to_left.at[0:64], self.recv_near.at[1, 0:64], self.left_of)
        )

    def merge(self):
        self.far_first.wait_recv()
        merged = self.to_right[0:64].astype(F32) + self.recv_far[0].astype(F32)
        self.to_right[0:64] = merged.astype(BF16)
        self.near.append(
            self.send(self.to_right.at[0:64], self.recv_near.at[0, 0:64], self.right_of)
        )
        self.far_second.wait_recv()
        merged = self.to_left[64:128].astype(F32) + self.recv_far[1].astype(F32)
        self.to_left[64:128] = merged.astype(BF16)
        self.near.append(
            self.send(self.to_left.at[64:128], self.recv_near.at[1, 64:128], self.left_of)
        )

    def total(self, own):
        for copy in self.near:
            copy.wait_recv()
        return own + self.recv_near[0].astype(F32) + self.recv_near[1].astype(F32)

    def done(self):
        for copy in self.copies:
            copy.wait_send()


class Shrink:
    def __init__(self, links, terms, pair_sum, middle, first_recv, last_recv, y_first):
        self.links = links
        self.terms = terms
        self.pair_sum = pair_sum
        self.middle = middle
        self.first_recv = first_recv
        self.last_recv = last_recv
        self.y_first = y_first
        self.copies = []

    def start(self):
        x, yh, z, yl, c = here()
        self.pair = self.links.send(self.terms.at[:, :, :, 1 - c], self.pair_sum, sibling())

    def send_first(self):
        x, yh, z, yl, c = here()
        self.pair.wait()
        terms, pair_sum = self.terms, self.pair_sum

        @pl.loop(0, 8)
        def _(at):
            h, k = lax.div(at, 4), lax.rem(at, 4)
            for low in range(2):
                pair_sum[h, k, low] = (
                    terms[h, k, low, c].astype(F32) + pair_sum[h, k, low].astype(F32)
                ).astype(BF16)

        self.first = []
        for step in (2, 1, 3):
            if self.y_first:
                device = y_device(step)
                source = pair_sum.at[device[1], :, device[3]]
            else:
                device = x_device(step)
                source = pair_sum.at[:, device[0]]
            self.first.append(self.links.send(source, self.first_recv.at[step - 1], device))

    def send_last(self):
        x, yh, z, yl, c = here()
        for copy in self.first:
            copy.wait()
        got = self.first_recv

        @pl.loop(0, 4)
        def _(at):
            if self.y_first:
                total = self.pair_sum[yh, at, yl].astype(F32)
                for slot in range(3):
                    total = total + got[slot, at].astype(F32)
                self.middle[at] = total.astype(BF16)
            else:
                h, low = lax.div(at, 2), lax.rem(at, 2)
                total = self.pair_sum[h, x, low].astype(F32)
                for slot in range(3):
                    total = total + got[slot, h, low].astype(F32)
                self.middle[h, low] = total.astype(BF16)

        self.second = []
        for step in (2, 1, 3):
            if self.y_first:
                device = x_device(step)
                source = self.middle.at[device[0]]
            else:
                device = y_device(step)
                source = self.middle.at[device[1], device[3]]
            self.second.append(self.links.send(source, self.last_recv.at[step - 1], device))

    def result(self):
        x, yh, z, yl, c = here()
        for copy in self.second:
            copy.wait()
        total = (self.middle[x] if self.y_first else self.middle[yh, yl]).astype(F32)
        for slot in range(3):
            total = total + self.last_recv[slot].astype(F32)
        return total


def shrink_scratch(rows, width, y_first):
    first = (4, rows, width) if y_first else (2, 2, rows, width)
    return [
        pltpu.VMEM((2, 4, 2, rows, width), BF16),
        pltpu.VMEM(first, BF16),
        pltpu.VMEM((3,) + first, BF16),
        pltpu.VMEM((3, rows, width), BF16),
    ]


def everyone():
    return (
        [z_device(s) for s in (1, 2, 3)]
        + [y_device(s) for s in (1, 2, 3)]
        + [x_device(s) for s in (1, 2, 3)]
        + [sibling()]
    )


GELU_A = math.sqrt(2.0 / math.pi)
GELU_B = 0.044715


def gelu_parts(gate):
    square = gate * gate
    curve = jnp.tanh(GELU_A * gate * (1.0 + GELU_B * square))
    half = 0.5 * (1.0 + curve)
    slope = half + 0.5 * gate * (1.0 - curve * curve) * (
        GELU_A * (1.0 + 3.0 * GELU_B * square)
    )
    return gate * half, slope

SCRATCH = dict(
    xn_all=((4, 128, 1024), BF16), wq_all=((2, 2, 2, 4, 64, 256), BF16), wkv_all=((4, 256, 512), BF16),
    q=((2, 4, 2, 128, 128), BF16), cosd=((4, 128, 128), F32), sind=((4, 128, 128), F32),
    kv_all=((2, 2, 2, 4, 2, 128, 256), BF16), attn=((4, 128, 512), BF16),
    recip=((2, 4, 256, 128), F32), wo_all=((2, 2, 2, 4, 64, 256), BF16), acc=((2, 4, 256, 256), F32),
    branch=((128, 1024), F32), h1=((128, 1024), F32), hn_all=((4, 128, 1024), BF16),
    wf_all=((2, 2, 2, 4, 64, 1152), BF16), q_mate=((2, 4, 2, 128, 128), BF16),
    mate_out=((2, 4, 256, 128), BF16), mate_in=((2, 4, 256, 128), BF16),
    sums_out=((2, 4, 1, 256), F32), sums_in=((2, 4, 1, 256), F32),
    inner_out=((2, 4, 1, 256), F32), inner_in=((2, 4, 1, 256), F32),
    d_mate=((2, 4, 256, 256), BF16),
    gate_all=((4, 128, 768), BF16), up_all=((4, 128, 768), BF16), hidden_all=((4, 128, 768), BF16),
    d_mlp_all=((4, 128, 1024), BF16), d_h1=((128, 1024), F32), d_branch_all=((4, 128, 1024), BF16),
    gain_rows=((4, 1, 1024), F32), grads=((4, 128, 1024), BF16),
    d_out=((2, 4, 256, 256), BF16),
    d_kv=((2, 2, 2, 4, 2, 128, 256), BF16), pair_recv=((3, 2, 4, 128, 256), BF16),
    y_recv=((2, 2, 4, 128, 256), BF16),
    kv_send=((4, 8, 512), F32), kv_recv=((4, 8, 512), F32),
    gain_own=((8, 1024), F32), gain_pair=((8, 1024), F32), gain_y=((3, 8, 1024), F32),
    gain_x=((3, 8, 1024), F32), gain_z=((3, 8, 1024), F32),
    own_sum=((128, 1024), F32), z_send=((3, 128, 1024), BF16),
    z_far=((4, 2, 64, 1024), BF16), z_near=((4, 2, 128, 1024), BF16),
    terms_a=((2, 4, 2, 2, 64, 640), BF16), terms_b=((2, 4, 2, 2, 64, 512), BF16),
    terms_k=((2, 4, 2, 2, 32, 256), BF16), terms_v=((2, 4, 2, 2, 32, 256), BF16),
)
SHRINKS = (
    (64, 640, True), (64, 512, False), (64, 128, True), (64, 128, False),
    (64, 128, True), (64, 128, False), (32, 256, True), (32, 256, False),
)
SEMS = 240


class Refs:
    pass


def begin(s, links):
    x, yh, z, yl, c = here()
    xin = s.tokens[...].astype(F32)
    s.xn_all[z] = (xin * inverse_rms(xin) * s.gain_attn_in[...]).astype(BF16)
    for group in range(2):
        first = pl.multiple_of(group * 512 + z * 128, 128)
        s.wkv_all[yl * 2 + c, :, pl.ds(group * 128, 128)] = quantized(
            s.w_key[:, pl.ds(first, 128)], QEXP_MODEL, 8
        )
        s.wkv_all[yl * 2 + c, :, pl.ds(256 + group * 128, 128)] = quantized(
            s.w_value[:, pl.ds(first, 128)], QEXP_MODEL, 8
        )
    s.wq_all[yh, yl, c] = quantized(s.w_query[...], QEXP_MODEL, 8).reshape(4, 64, 256)
    greet(everyone())
    ring = ZGather(links, s.xn_all)
    key_part = s.wkv_all.at[yl * 2 + c, :, 0:256]
    value_part = s.wkv_all.at[yl * 2 + c, :, 256:512]
    from_low = links.send(key_part, key_part, y_device(1))
    from_high = links.send(value_part, value_part, y_device(3))
    own = s.wkv_all.at[yl * 2 + c]
    pair = links.send(own, own, sibling())
    s.gather_q = Gather(links, s.wq_all)
    s.wo_all[yh, yl, c] = quantized(s.w_output[...], QEXP_MODEL, 8).reshape(4, 64, 256)
    s.gather_o = Gather(links, s.wo_all)
    for at, (weight, exponent, bits) in enumerate(
        ((s.w_gate, QEXP_MODEL, 4), (s.w_up, QEXP_MODEL, 4), (s.w_down, QEXP_HIDDEN, 2))
    ):
        s.wf_all[yh, yl, c, :, :, at * 384 : at * 384 + 384] = quantized(
            weight[...], exponent, bits
        ).reshape(4, 64, 384)
    s.gather_f = Gather(links, s.wf_all)
    lane = lax.broadcasted_iota(jnp.int32, (128, 128), 1)
    row = lax.broadcasted_iota(jnp.int32, (128, 128), 0)
    freqs = jnp.exp(lax.rem(lane, 64).astype(F32) * (-2.0 * math.log(THETA) / DH))
    start = s.lengths[0, 0]
    base = yh * 2048 + yl * 256 + c * 128

    def tables(block):
        tok = row + (base + block * 512)
        angle = jnp.where(tok >= start, tok - start, tok).astype(F32) * freqs
        s.cosd[block] = jnp.cos(angle)
        sine = jnp.sin(angle)
        s.sind[block] = jnp.where(lane < 64, -sine, sine)

    tables(0)
    ring.forward()
    tables(1)
    from_low.wait_recv()
    from_high.wait_recv()
    other = s.wkv_all.at[(1 - yl) * 2 + c]
    passed = links.send(other, other, sibling())
    s.gather_q.spread()
    tables(2)
    tables(3)
    pair.wait_recv()
    passed.wait_recv()

    def project_kv(block):
        lin = dot(s.xn_all[block], s.wkv_all[...].reshape(1024, 512))
        cosd, sind = s.cosd[block], s.sind[block]
        for group in range(2):
            key = lin[:, group * 128 : group * 128 + 128]
            key = (key * cosd + swap_halves(key) * sind).astype(BF16)
            value = lin[:, 256 + group * 128 : 384 + group * 128].astype(BF16)
            s.kv_all[group, yh, yl, block, c, :, 0:128] = key
            s.kv_all[group, yh, yl, block, c, :, 128:256] = value

    def project_q(block):
        cosd, sind = s.cosd[block], s.sind[block]
        for group in range(2):
            lin = dot(s.xn_all[block], s.wq_all[group].reshape(1024, 256))
            for head in range(2):
                query = lin[:, head * 128 : head * 128 + 128]
                query = (query * cosd + swap_halves(query) * sind) * SCALE
                s.q[group, block, head] = query.astype(BF16)

    project_kv(z)
    ring.near()
    project_kv(ring.left[2])
    project_kv(ring.right[2])
    ring.far()
    project_kv(lax.rem(z + 2, 4))
    s.kv_pair, s.kv_near, s.kv_far, s.q_send = [], [], [], []
    for group in range(2):
        mine = s.kv_all.at[group, yh, yl, :, c]
        s.kv_pair.append(links.send(mine, mine, sibling()))
        s.kv_near.append(links.send(mine, mine, (x, yh, z, 1 - yl, c)))
        s.kv_far.append(links.plan(mine, mine, mate()))
        s.q_send.append(links.plan(s.q.at[group], s.q_mate.at[group], mate()))

    @pl.when(yh == 0)
    def _():
        for group in range(2):
            s.kv_far[group].start()

    s.gather_o.spread()
    s.gather_q.forward()
    s.gather_q.arrived()
    for block in range(4):
        project_q(block)

    @pl.when(yh == 1)
    def _():
        for group in range(2):
            s.q_send[group].start()

    s.gather_f.spread()
    ring.done()
    for copy in (from_low, from_high, pair, passed):
        copy.wait_send()
    s.gather_q.done()


def attend(s, links):
    x, yh, z, yl, c = here()
    start = s.lengths[0, 0]
    lane = lax.broadcasted_iota(jnp.int32, (1, 256), 1)
    ones = jnp.ones((256, 128), BF16)
    row = lax.rem(lax.broadcasted_iota(jnp.int32, (256, 1), 0), 128)

    def block_sum(query, q_base, group, from_h, from_l, units, diagonal):
        token_q = row + q_base
        floor = jnp.where(token_q >= start, start, 0)
        total = None
        for unit in units:
            both = s.kv_all[group, from_h, from_l, unit].reshape(256, 256)
            token_k = lane + (from_h * 2048 + unit * 512 + from_l * 256)
            curved = jnp.tanh(dot_nt(query, both[:, :128]) * (1.0 / CAP))
            weight = jnp.exp2(curved * (CAP * LOG2E))
            seen = token_k >= floor
            if diagonal and unit == units[-1]:
                seen = seen & (token_k <= token_q)
            weight = jnp.where(seen, weight, 0.0).astype(BF16)
            term = dot(weight, jnp.concatenate([both[:, 128:], ones], axis=1))
            total = term if total is None else total + term
        return total

    own_base = yh * 2048 + yl * 256 + c * 128
    mate_base = 2048 + (1 - yl) * 256 + c * 128

    def same_half(group, from_l, first):
        for block in range(4):
            total = block_sum(
                s.q[group, block].reshape(256, 128), own_base + block * 512, group, yh, from_l,
                list(range(block + 1)), True,
            )
            if first:
                s.acc[group, block] = total
            else:
                s.acc[group, block] += total

    def far_half(group):
        @pl.loop(0, 4)
        def _(block):
            s.acc[group, block] += block_sum(
                s.q[group, block].reshape(256, 128), own_base + block * 512, group, 0, 1 - yl,
                [0, 1, 2, 3], False,
            )

    def for_mate(group):
        @pl.loop(0, 4)
        def _(block):
            total = block_sum(
                s.q_mate[group, block].reshape(256, 128), mate_base + block * 512, group, 0,
                1 - yl, [0, 1, 2, 3], False,
            )
            s.mate_out[group, block] = total[:, :128].astype(BF16)
            s.sums_out[group, block] = total[:, 128:256].T[0:1]

    def pass_plan(group, from_h, from_l):
        block = s.kv_all.at[group, from_h, from_l, :, c]
        return links.plan(block, block, sibling())

    near_pass = [pass_plan(group, yh, 1 - yl) for group in range(2)]
    far_pass = [pass_plan(group, 0, 1 - yl) for group in range(2)]
    back = []
    for group in range(2):
        back.append(links.plan(s.mate_out.at[group], s.mate_in.at[group], mate()))
        back.append(links.plan(s.sums_out.at[group], s.sums_in.at[group], mate()))

    @pl.when(yh == 0)
    def _():
        s.mate_in[...] = jnp.zeros_like(s.mate_in)
        s.sums_in[...] = jnp.zeros_like(s.sums_in)

    for group in range(2):
        s.kv_pair[group].wait_recv()
        same_half(group, yl, True)
    s.gather_o.forward()
    for group in range(2):
        s.kv_near[group].wait_recv()
        near_pass[group].start()

        @pl.when(yh == 1)
        def _():
            s.kv_far[group].wait_recv()
            far_pass[group].start()

        near_pass[group].wait_recv()
        same_half(group, 1 - yl, False)

        @pl.when(yh == 1)
        def _():
            far_pass[group].wait_recv()
            far_half(group)

        @pl.when(yh == 0)
        def _():
            s.q_send[group].wait_recv()
            for_mate(group)
            back[2 * group].start()
            back[2 * group + 1].start()

    s.gather_f.forward()
    for group in range(2):

        @pl.when(yh == 1)
        def _():
            back[2 * group].wait_recv()
            back[2 * group + 1].wait_recv()

        for block in range(4):
            total = s.acc[group, block]
            more = jnp.broadcast_to(s.sums_in[group, block], (128, 256)).T
            inverse = 1.0 / (total[:, 128:256] + more)
            s.recip[group, block] = inverse
            out = total[:, :128] + s.mate_in[group, block].astype(F32)
            out = (out * inverse).astype(BF16)
            for head in range(2):
                first = group * 256 + head * 128
                s.attn[block, :, first : first + 128] = out[head * 128 : head * 128 + 128]
    for group in range(2):
        s.kv_pair[group].wait_send()
        s.kv_near[group].wait_send()
        near_pass[group].wait_send()

    @pl.when(yh == 0)
    def _():
        for group in range(2):
            s.kv_far[group].wait_send()
        for copy in back:
            copy.wait_send()

    @pl.when(yh == 1)
    def _():
        for group in range(2):
            far_pass[group].wait_send()
            s.q_send[group].wait_send()


def all_terms(scatter, term_of):
    x, yh, z, yl, c = here()
    scatter.far(term_of(lax.rem(z + 2, 4)))
    scatter.right(term_of(lax.rem(z + 1, 4)))
    scatter.left(term_of(lax.rem(z + 3, 4)))
    scatter.merge()
    return term_of(z)


def output_projection(s, links):
    x, yh, z, yl, c = here()

    def term_of(block):
        left = s.attn[block]
        return dot_nt(left[:, :256], s.wo_all[0].reshape(1024, 256)) + dot_nt(
            left[:, 256:], s.wo_all[1].reshape(1024, 256)
        )

    s.gather_o.arrived()
    scatter = ZScatter(links, s.z_send, s.z_far.at[0], s.z_near.at[0])
    own = all_terms(scatter, term_of)
    branch = scatter.total(own)
    h1 = s.tokens[...].astype(F32) + branch * inverse_rms(branch) * s.gain_attn_out[...]
    s.hn_all[z] = (h1 * inverse_rms(h1) * s.gain_mlp_in[...]).astype(BF16)
    s.ring = ZGather(links, s.hn_all)
    s.branch[...] = branch
    s.h1[...] = h1
    s.gather_f.arrived()
    scatter.done()
    s.gather_o.done()
    s.gather_f.done()


def feed_forward(s, links):
    x, yh, z, yl, c = here()

    def term_of(block):
        left = s.hn_all[block]
        total = None
        for group in range(2):
            cols = slice(group * 384, group * 384 + 384)
            gate = dot(left, s.wf_all[group, ..., 0:384].reshape(1024, 384))
            up = dot(left, s.wf_all[group, ..., 384:768].reshape(1024, 384))
            value, slope = gelu_parts(gate)
            s.gate_all[block, :, cols] = value.astype(BF16)
            s.up_all[block, :, cols] = (up * slope).astype(BF16)
            hidden = (value * up).astype(BF16)
            s.hidden_all[block, :, cols] = hidden
            term = dot_nt(hidden, s.wf_all[group, ..., 768:1152].reshape(1024, 384))
            total = term if total is None else total + term
        return total

    s.ring.forward()
    scatter = ZScatter(links, s.z_send, s.z_far.at[1], s.z_near.at[1])
    ring = s.ring
    s.own_sum[...] = term_of(z)
    ring.near()
    scatter.left(term_of(ring.left[2]))
    scatter.right(term_of(ring.right[2]))
    ring.far()
    scatter.far(term_of(lax.rem(z + 2, 4)))
    scatter.merge()
    mlp = scatter.total(s.own_sum[...])
    into, gain_part = rms_back(mlp, s.gain_mlp_out[...], s.out_grad[...].astype(F32))
    s.d_mlp_all[z] = into.astype(BF16)
    s.ring = ZGather(links, s.d_mlp_all)
    s.gain_rows[3] = gain_part
    s.mixed[...] = (s.h1[...] + mlp * inverse_rms(mlp) * s.gain_mlp_out[...]).astype(BF16)
    ring.done()
    scatter.done()


def feed_forward_back(s, links):
    x, yh, z, yl, c = here()

    def term_of(block):
        left = s.d_mlp_all[block]
        total = None
        for group in range(2):
            cols = slice(group * 384, group * 384 + 384)
            d_hidden = dot(left, s.wf_all[group, ..., 768:1152].reshape(1024, 384))
            d_gate = (d_hidden * s.up_all[block, :, cols].astype(F32)).astype(BF16)
            d_up = (d_hidden * s.gate_all[block, :, cols].astype(F32)).astype(BF16)
            s.up_all[block, :, cols] = d_gate
            s.gate_all[block, :, cols] = d_up
            term = dot_nt(d_gate, s.wf_all[group, ..., 0:384].reshape(1024, 384)) + dot_nt(
                d_up, s.wf_all[group, ..., 384:768].reshape(1024, 384)
            )
            total = term if total is None else total + term
        return total

    scatter = ZScatter(links, s.z_send, s.z_far.at[2], s.z_near.at[2])
    ring = s.ring
    s.own_sum[...] = term_of(z)
    ring.forward()
    ring.near()
    scatter.left(term_of(ring.left[2]))
    scatter.right(term_of(ring.right[2]))
    ring.far()
    scatter.far(term_of(lax.rem(z + 2, 4)))
    d_mlp = s.d_mlp_all[...].reshape(512, 1024)
    hn = s.hn_all[...].reshape(512, 1024)
    for group in range(2):
        cols = slice(group * 384, group * 384 + 384)
        down = dot_tn(d_mlp, s.hidden_all[:, :, cols].reshape(512, 384)).astype(BF16)
        s.terms_a[group, :, :, :, :, 0:384] = down.reshape(4, 2, 2, 64, 384)
    scatter.merge()
    for group in range(2):
        cols = slice(group * 384, group * 384 + 384)
        gate = dot_tn(hn, s.up_all[:, :, cols].reshape(512, 384)).astype(BF16)
        gate = gate.reshape(4, 2, 2, 64, 384)
        s.terms_a[group, :, :, :, :, 384:640] = gate[..., 0:256]
        s.terms_b[group, :, :, :, :, 0:128] = gate[..., 256:384]
    s.shrink[0].start()
    d_hn = scatter.total(s.own_sum[...])
    into, gain_part = rms_back(s.h1[...], s.gain_mlp_in[...], d_hn)
    s.gain_rows[2] = gain_part
    d_h1 = s.out_grad[...].astype(F32) + into
    s.d_h1[...] = d_h1
    into, gain_part = rms_back(s.branch[...], s.gain_attn_out[...], d_h1)
    s.d_branch_all[z] = into.astype(BF16)
    s.ring = ZGather(links, s.d_branch_all)
    s.gain_rows[1] = gain_part
    s.shrink[0].send_first()
    for group in range(2):
        cols = slice(group * 384, group * 384 + 384)
        up = dot_tn(hn, s.gate_all[:, :, cols].reshape(512, 384)).astype(BF16)
        s.terms_b[group, :, :, :, :, 128:512] = up.reshape(4, 2, 2, 64, 384)
    s.shrink[1].start()
    s.ring.forward()
    ring.done()
    scatter.done()


def attend_back(s, links):
    x, yh, z, yl, c = here()
    ring = s.ring
    lane = lax.broadcasted_iota(jnp.int32, (256, 128), 1)

    def extra_lanes(inner):
        high = inner.astype(BF16).astype(F32)
        low = inner - high
        return jnp.where(lane == 0, high, jnp.where(lane == 1, low, 0.0)).astype(BF16)

    def cotangent(block):
        for group in range(2):
            cols = slice(group * 256, group * 256 + 256)
            rows = dot(s.d_branch_all[block], s.wo_all[group].reshape(1024, 256))
            rows = rows.astype(BF16).astype(F32)
            rows = jnp.concatenate([rows[:, :128], rows[:, 128:]], axis=0)
            outs = s.attn[block, :, cols].astype(F32)
            outs = jnp.concatenate([outs[:, :128], outs[:, 128:]], axis=0)
            scaled = (rows * s.recip[group, block]).astype(BF16)
            inner = -jnp.sum(scaled.astype(F32) * outs, axis=1, keepdims=True)
            inner = jnp.broadcast_to(inner, (256, 128))
            s.inner_out[group, block] = inner.T[0:1]
            s.d_out[group, block] = jnp.concatenate([scaled, extra_lanes(inner)], axis=1)

    cotangent(z)
    s.acc[...] = jnp.zeros_like(s.acc)
    ring.near()
    cotangent(ring.left[2])
    cotangent(ring.right[2])
    s.shrink[1].send_first()
    ring.far()
    cotangent(lax.rem(z + 2, 4))
    lend = []
    for group in range(2):
        lend.append(
            links.plan(
                s.d_out.at[group, :, :, 0:128], s.d_mate.at[group, :, :, 0:128], mate()
            )
        )
        lend.append(links.plan(s.inner_out.at[group], s.inner_in.at[group], mate()))

    @pl.when(yh == 1)
    def _():
        for copy in lend:
            copy.start()

    d_branch = s.d_branch_all[...].reshape(512, 1024)
    for group in range(2):
        cols = slice(group * 256, group * 256 + 256)
        back = dot_tn(d_branch, s.attn[:, :, cols].reshape(512, 256)).astype(BF16)
        back = back.reshape(4, 2, 2, 64, 256)
        s.terms_a[group, :, :, :, :, 0:128] = back[..., 0:128]
        s.terms_b[group, :, :, :, :, 0:128] = back[..., 128:256]
    s.shrink[2].start()
    s.shrink[3].start()
    start = s.lengths[0, 0]
    ones = jnp.where(lane < 2, 1.0, 0.0).astype(BF16)
    token_row = lax.rem(lax.broadcasted_iota(jnp.int32, (1, 256), 1), 128)
    token_col = lax.broadcasted_iota(jnp.int32, (256, 1), 0)

    own_base = yh * 2048 + yl * 256 + c * 128
    mate_base = 2048 + (1 - yl) * 256 + c * 128

    def unit_back(group, from_h, from_l, unit, first_block, diagonal, lent=False):
        both = s.kv_all[group, from_h, from_l, unit].reshape(256, 256)
        key, value = both[:, :128], both[:, 128:]
        count = 4 - first_block
        queries, cots, base, rows = (
            (s.q_mate, s.d_mate, mate_base, slice(128, 256))
            if lent
            else (s.q, s.d_out, own_base, slice(0, 128))
        )
        query = queries[group, first_block:].reshape(count * 256, 128)
        cot = cots[group, first_block:].reshape(count * 256, 256)
        curved = jnp.tanh(dot_nt(key, query) * (1.0 / CAP))
        weight = jnp.exp2(curved * (CAP * LOG2E))
        token_k = token_col + (from_h * 2048 + unit * 512 + from_l * 256)
        pieces = []
        for block in range(first_block, 4):
            token_q = token_row + (base + block * 512)
            seen = token_k >= jnp.where(token_q >= start, start, 0)
            if diagonal and block == first_block:
                seen = seen & (token_k <= token_q)
            at = (block - first_block) * 256
            pieces.append(jnp.where(seen, weight[:, at : at + 256], 0.0))
        weight = jnp.concatenate(pieces, axis=1)
        grown = dot_nt(jnp.concatenate([value, ones], axis=1), cot)
        slope = (weight * grown * (1.0 - curved * curved)).astype(BF16)
        d_key = dot(slope, query)
        d_value = dot(weight.astype(BF16), cot[:, :128])
        both = jnp.concatenate([d_key, d_value], axis=1)
        if lent:
            both = both + s.d_kv[group, from_h, from_l, unit].astype(F32).reshape(256, 256)
        s.d_kv[group, from_h, from_l, unit] = both.astype(BF16).reshape(2, 128, 256)
        d_query = dot(key.T, slope)
        for block in range(first_block, 4):
            at = (block - first_block) * 256
            s.acc[group, block, rows, :] += d_query[:, at : at + 256]

    def same_half(group, from_l):
        for unit in range(4):
            unit_back(group, yh, from_l, unit, unit, True)

    def pair_plan(slot, group, from_h, from_l):
        return links.plan(
            s.d_kv.at[group, from_h, from_l, :, 1 - c], s.pair_recv.at[slot, group], sibling()
        )

    def add_pair(slot, group, from_h, from_l):
        s.d_kv[group, from_h, from_l, :, c] = (
            s.d_kv[group, from_h, from_l, :, c].astype(F32)
            + s.pair_recv[slot, group].astype(F32)
        ).astype(BF16)

    far_pair = [pair_plan(0, group, 0, 1 - yl) for group in range(2)]
    near_pair = [pair_plan(1, group, yh, 1 - yl) for group in range(2)]
    own_pair = [pair_plan(2, group, yh, yl) for group in range(2)]
    far_send = [
        links.plan(s.d_kv.at[group, 0, 1 - yl, :, c], s.y_recv.at[0, group], mate())
        for group in range(2)
    ]
    near_send = [
        links.plan(
            s.d_kv.at[group, yh, 1 - yl, :, c], s.y_recv.at[1, group], (x, yh, z, 1 - yl, c)
        )
        for group in range(2)
    ]
    returned = [
        links.plan(s.mate_out.at[group], s.mate_in.at[group], mate()) for group in range(2)
    ]

    @pl.when(yh == 1)
    def _():
        s.y_recv[0] = jnp.zeros((2, 4, 128, 256), BF16)
        for group in range(2):

            @pl.loop(0, 4)
            def _(unit):
                unit_back(group, 0, 1 - yl, unit, 0, False)

            far_pair[group].start()

    same_half(0, 1 - yl)

    @pl.when(yh == 1)
    def _():
        for group in range(2):
            far_pair[group].wait()
            add_pair(0, group, 0, 1 - yl)
            far_send[group].start()

    same_half(1, 1 - yl)
    for i in (0, 1):
        s.shrink[i].send_last()
    for i in (2, 3):
        s.shrink[i].send_first()

    @pl.when(yh == 0)
    def _():
        for group in range(2):
            lend[2 * group].wait_recv()
            lend[2 * group + 1].wait_recv()
            for block in range(4):
                inner = jnp.broadcast_to(s.inner_in[group, block], (128, 256)).T
                s.d_mate[group, block, :, 128:256] = extra_lanes(inner)

            @pl.loop(0, 4)
            def _(unit):
                unit_back(group, 0, 1 - yl, unit, 0, False, True)

            for block in range(4):
                s.mate_out[group, block] = s.acc[group, block, 128:256, :].T.astype(BF16)
            returned[group].start()

    for group in range(2):
        near_pair[group].start()
    same_half(0, yl)
    own_pair[0].start()
    for group in range(2):
        near_pair[group].wait()
        add_pair(1, group, yh, 1 - yl)
        near_send[group].start()
    same_half(1, yl)
    own_pair[1].start()

    @pl.when(yh == 1)
    def _():
        for copy in returned:
            copy.wait_recv()

    def rope_back(values, block):
        return values * s.cosd[block] - swap_halves(values) * s.sind[block]

    for group in range(2):
        for block in range(4):
            d_query = s.acc[group, block, 0:128, :].T + s.mate_in[group, block].astype(F32)
            for head in range(2):
                turned = rope_back(d_query[head * 128 : head * 128 + 128], block) * SCALE
                at = group * 256 + head * 128
                s.grads[block, :, at : at + 128] = turned.astype(BF16)
    xa = s.xn_all[...].reshape(512, 1024)
    for group in range(2):
        back = dot_tn(xa, s.grads[:, :, group * 256 : group * 256 + 256].reshape(512, 256))
        back = back.astype(BF16).reshape(4, 2, 2, 64, 256)
        s.terms_a[group, :, :, :, :, 0:128] = back[..., 0:128]
        s.terms_b[group, :, :, :, :, 0:128] = back[..., 128:256]
    s.shrink[4].start()
    s.shrink[5].start()
    first = s.shrink[0].result()
    s.dwd[...] = first[:, 0:384]
    s.dwg[:, 0:256] = first[:, 384:640]
    second = s.shrink[1].result()
    s.dwg[:, 256:384] = second[:, 0:128]
    s.dwu[...] = second[:, 128:512]
    for i in (2, 3):
        s.shrink[i].send_last()
    for i in (4, 5):
        s.shrink[i].send_first()
    for group in range(2):
        own_pair[group].wait()
        near_send[group].wait()

    @pl.when(yh == 0)
    def _():
        for copy in far_send:
            copy.wait_recv()
        for copy in returned:
            copy.wait_send()

    @pl.when(yh == 1)
    def _():
        for copy in far_send + lend:
            copy.wait_send()

    for group in range(2):
        for block in range(4):
            both = (
                s.d_kv[group, yh, yl, block, c].astype(F32)
                + s.pair_recv[2, group, block].astype(F32)
                + s.y_recv[0, group, block].astype(F32)
                + s.y_recv[1, group, block].astype(F32)
            )
            d_key = both[:, :128].astype(BF16).astype(F32)
            at = 512 + group * 128
            s.grads[block, :, at : at + 128] = rope_back(d_key, block).astype(BF16)
            at = 768 + group * 128
            s.grads[block, :, at : at + 128] = both[:, 128:].astype(BF16)
    ring.done()


def finish(s, links):
    x, yh, z, yl, c = here()
    s.gain_own[...] = jnp.zeros_like(s.gain_own)

    def term_of(block):
        left = s.grads[block]
        total = dot_nt(left[:, 512:], s.wkv_all[...].reshape(1024, 512))
        for group in range(2):
            total = total + dot_nt(
                left[:, group * 256 : group * 256 + 256], s.wq_all[group].reshape(1024, 256)
            )
        s.gain_own[0:1] += jnp.sum(total * s.xn_all[block].astype(F32), axis=0, keepdims=True)
        return total

    scatter = ZScatter(links, s.z_send, s.z_far.at[3], s.z_near.at[3])
    scatter.far(term_of(lax.rem(z + 2, 4)))
    xa = s.xn_all[...].reshape(512, 1024)
    back = dot_tn(xa, s.grads[:, :, 512:].reshape(512, 512))
    for k in range(4):
        for h in range(2):
            for low in range(2):
                for core in range(2):
                    rows = [k * 256 + h * 128 + low * 16 + core * 8 + 32 * i for i in range(4)]
                    piece = jnp.concatenate([back[row : row + 8] for row in rows], axis=0)
                    piece = piece.astype(BF16)
                    s.terms_k[h, k, low, core] = piece[:, :256]
                    s.terms_v[h, k, low, core] = piece[:, 256:]
    s.shrink[6].start()
    s.shrink[7].start()
    scatter.right(term_of(lax.rem(z + 1, 4)))
    scatter.left(term_of(lax.rem(z + 3, 4)))
    scatter.merge()
    s.shrink[6].send_first()
    s.shrink[7].send_first()
    own = term_of(z)
    s.gain_own[0:1] = s.gain_own[0:1] / s.gain_attn_in[...]
    for i in (1, 2, 3):
        s.gain_own[i : i + 1] = s.gain_rows[i]
    pair = links.send(s.gain_own, s.gain_pair, sibling())
    for i in (4, 5):
        s.shrink[i].send_last()
    pair.wait()
    s.gain_pair[...] += s.gain_own[...]
    sent = [links.send(s.gain_pair, s.gain_y.at[k - 1], y_device(k)) for k in (2, 1, 3)]
    s.shrink[6].send_last()
    s.shrink[7].send_last()
    for copy in sent:
        copy.wait()
    s.gain_own[...] = s.gain_pair[...] + (s.gain_y[0] + s.gain_y[2]) + s.gain_y[1]
    sent = [links.send(s.gain_own, s.gain_x.at[k - 1], x_device(k)) for k in (2, 1, 3)]
    d_xn = scatter.total(own)
    into, _ = rms_back(s.tokens[...].astype(F32), s.gain_attn_in[...], d_xn)
    s.tokens_grad[...] = (s.d_h1[...] + into).astype(BF16)
    s.dwo[:, 0:128] = s.shrink[2].result()
    s.dwo[:, 128:256] = s.shrink[3].result()
    for copy in sent:
        copy.wait()
    s.gain_pair[...] = s.gain_own[...] + (s.gain_x[0] + s.gain_x[2]) + s.gain_x[1]
    sent = [links.send(s.gain_pair, s.gain_z.at[k - 1], z_device(k)) for k in (2, 1, 3)]
    s.kv_send[:, :, 0:256] = s.shrink[6].result().reshape(4, 8, 256)
    s.kv_send[:, :, 256:512] = s.shrink[7].result().reshape(4, 8, 256)
    moved = []
    for step in (2, 1, 3):
        device = z_device(step)
        moved.append(links.send(s.kv_send.at[device[2]], s.kv_recv.at[z], device))
    s.kv_recv[z] = s.kv_send[z]
    s.dwq[:, 0:128] = s.shrink[4].result()
    s.dwq[:, 128:256] = s.shrink[5].result()
    for copy in sent:
        copy.wait()
    s.gains[...] = s.gain_pair[...] + (s.gain_z[0] + s.gain_z[2]) + s.gain_z[1]
    for copy in moved:
        copy.wait()
    for origin in range(4):
        for group in range(2):
            at = group * 512 + origin * 128
            s.dwk[:, at : at + 128] = s.kv_recv[origin, :, group * 128 : group * 128 + 128]
            s.dwv[:, at : at + 128] = s.kv_recv[
                origin, :, 256 + group * 128 : 384 + group * 128
            ]
    scatter.done()


OPERANDS = (
    "tokens", "lengths", "w_query", "w_key", "w_value", "w_output", "w_gate", "w_up", "w_down",
    "gain_attn_in", "gain_attn_out", "gain_mlp_in", "gain_mlp_out", "out_grad",
)
RESULTS = dict(
    mixed=((128, 1024), BF16), tokens_grad=((128, 1024), BF16), dwq=((64, 256), F32),
    dwk=((8, 1024), F32), dwv=((8, 1024), F32), dwo=((64, 256), F32), dwg=((64, 384), F32),
    dwu=((64, 384), F32), dwd=((64, 384), F32), gains=((8, 1024), F32),
)


def layer_kernel(*refs):
    s = Refs()
    names = list(OPERANDS) + list(RESULTS) + list(SCRATCH)
    for name, ref in zip(names, refs):
        setattr(s, name, ref)
    rest = refs[len(names) :]
    links = Links(rest[-2], rest[-1])
    terms = (
        s.terms_a, s.terms_b, s.terms_a.at[..., 0:128], s.terms_b.at[..., 0:128],
        s.terms_a.at[..., 0:128], s.terms_b.at[..., 0:128], s.terms_k, s.terms_v,
    )
    s.shrink = [
        Shrink(links, terms[i], *rest[4 * i : 4 * i + 4], SHRINKS[i][2])
        for i in range(len(SHRINKS))
    ]
    begin(s, links)
    attend(s, links)
    output_projection(s, links)
    feed_forward(s, links)
    feed_forward_back(s, links)
    attend_back(s, links)
    finish(s, links)


def run_layer(*operands):
    scratch = [pltpu.VMEM(shape, kind) for shape, kind in SCRATCH.values()]
    for rows, width, y_first in SHRINKS:
        scratch += shrink_scratch(rows, width, y_first)
    scratch += [pltpu.SemaphoreType.DMA((SEMS,))] * 2
    return pl.pallas_call(
        layer_kernel,
        name="layer",
        out_shape=tuple(jax.ShapeDtypeStruct(shape, kind) for shape, kind in RESULTS.values()),
        in_specs=[VM, SM] + [VM] * 12,
        out_specs=tuple(VM for _ in RESULTS),
        scratch_shapes=scratch,
        compiler_params=pltpu.CompilerParams(
            collective_id=1, has_side_effects=True, vmem_limit_bytes=VMEM_LIMIT
        ),
    )(*operands)


def leave_kernel(*refs):
    count = len(refs) // 2
    for i in range(count):
        refs[count + i][...] = refs[i][...]


def run_leave(results):
    return pl.pallas_call(
        leave_kernel,
        name="leave",
        out_shape=tuple(jax.ShapeDtypeStruct(r.shape, r.dtype) for r in results),
        in_specs=[VM] * len(results),
        out_specs=tuple(VM for _ in results),
    )(*results)


def per_device(
    tokens, lengths, w_query, w_key, w_value, w_output, w_gate, w_up, w_down,
    gain_attn_in, gain_attn_out, gain_mlp_in, gain_mlp_out, out_grad,
):
    gain_rows = [
        gain.reshape(1, -1) for gain in (gain_attn_in, gain_attn_out, gain_mlp_in, gain_mlp_out)
    ]
    *results, gains = run_layer(
        tokens, lengths, w_query, w_key, w_value, w_output, w_gate, w_up, w_down,
        *gain_rows, out_grad,
    )
    x, yh, z, yl, c = here()
    first = ((((x * 2 + yh) * 4 + z) * 2 + yl) * 2 + c) * 8
    own_gains = lax.dynamic_slice(gains, (0, first), (4, 8))
    return tuple(run_leave(results)) + tuple(own_gains[i] for i in range(4))


def solution(mesh):
    grid = Mesh(mesh.devices.reshape(4, 2, 4, 2, 2), AXES)
    tokens = P(AXES, None)
    split = P(("yl", "c"), ("yh", "z"))
    rows = P(("yl", "c"), None)
    grads = P(("x", "yl", "c"), ("yh", "z"))
    gains = P(AXES)
    return jax.shard_map(
        per_device,
        mesh=grid,
        in_specs=(tokens, P("x", None), split, rows, rows, split, split, split, split)
        + (P(),) * 4
        + (tokens,),
        out_specs=(tokens, tokens, grads, tokens, tokens, grads, grads, grads, grads)
        + (gains,) * 4,
        check_vma=False,
    )
```

```python
import math

import jax
import jax.numpy as jnp
from jax import lax
from jax.experimental import pallas as pl
from jax.experimental.pallas import tpu as pltpu
from jax.sharding import Mesh
from jax.sharding import PartitionSpec as P

DH = 128
QEXP_MODEL = 10
QEXP_HIDDEN = 11
CAP = 50.0
EPSILON = 1e-06
THETA = 10000.0
SCALE = DH ** (-0.5)
AXES = ("x", "yh", "z", "yl", "c")
BY_ID = pl.DeviceIdType.MESH
F32 = jnp.float32
BF16 = jnp.bfloat16
VM = pl.BlockSpec(memory_space=pltpu.VMEM)
SM = pl.BlockSpec(memory_space=pltpu.SMEM)
LOG2E = 1.4426950408889634
VMEM_LIMIT = 63 * 2**20


def here():
    return tuple(lax.axis_index(name) for name in AXES)


def z_device(step):
    x, yh, z, yl, c = here()
    return (x, yh, lax.rem(z + step, 4), yl, c)


def y_device(step):
    x, yh, z, yl, c = here()
    y = lax.rem(yh * 2 + yl + step, 4)
    return (x, lax.div(y, 2), z, lax.rem(y, 2), c)


def x_device(step):
    x, yh, z, yl, c = here()
    return (lax.rem(x + step, 4), yh, z, yl, c)


def sibling():
    x, yh, z, yl, c = here()
    return (x, yh, z, yl, 1 - c)


def mate():
    x, yh, z, yl, c = here()
    return (x, 1 - yh, z, 1 - yl, c)


def greet(devices):
    barrier = pltpu.get_barrier_semaphore()
    for device in devices:
        pl.semaphore_signal(barrier, inc=1, device_id=device, device_id_type=BY_ID)
    pl.semaphore_wait(barrier, len(devices))


class Links:
    def __init__(self, send_sems, recv_sems):
        self.send_sems = send_sems
        self.recv_sems = recv_sems
        self.used = 0

    def plan(self, source, target, device):
        at = self.used
        self.used += 1
        return pltpu.make_async_remote_copy(
            src_ref=source,
            dst_ref=target,
            send_sem=self.send_sems.at[at],
            recv_sem=self.recv_sems.at[at],
            device_id=device,
            device_id_type=BY_ID,
        )

    def send(self, source, target, device):
        copy = self.plan(source, target, device)
        copy.start()
        return copy


def dot(left, right):
    return lax.dot_general(left, right, (((1,), (0,)), ((), ())), preferred_element_type=F32)


def dot_nt(left, right):
    return lax.dot_general(left, right, (((1,), (1,)), ((), ())), preferred_element_type=F32)


def dot_tn(left, right):
    return lax.dot_general(left, right, (((0,), (0,)), ((), ())), preferred_element_type=F32)


def quantized(weight, exponent, bits):
    shift = 8 - bits
    code = jnp.clip(jnp.floor(weight.astype(F32) * 2.0**exponent) + 128.0, 0.0, 255.0)
    if shift:
        code = (
            jnp.minimum(jnp.floor((code + 2.0 ** (shift - 1)) * 2.0 ** (-shift)), 2.0**bits - 1.0)
            * 2.0**shift
        )
    return ((code - 128.0) * 2.0 ** (-exponent)).astype(BF16)


def inverse_rms(values):
    return lax.rsqrt(jnp.mean(values * values, axis=-1, keepdims=True) + EPSILON)


def rms_back(values, gain, incoming):
    inverse = inverse_rms(values)
    scaled = incoming * gain
    inner = jnp.mean(scaled * values, axis=-1, keepdims=True)
    into = inverse * (scaled - values * (inverse * inverse) * inner)
    gain_part = jnp.sum(incoming * values * inverse, axis=0, keepdims=True)
    return into, gain_part


def swap_halves(values):
    half = values.shape[-1] // 2
    return jnp.concatenate([values[..., half:], values[..., :half]], axis=-1)


class Gather:
    def __init__(self, links, buffer):
        x, yh, z, yl, c = here()
        self.links = links
        self.buffer = buffer
        quarter = buffer.at[yh, yl, c, x]
        self.ring = {step: links.send(quarter, quarter, y_device(step)) for step in (2, 1, 3)}
        own = buffer.at[yh, yl, c]
        self.pair = links.send(own, own, sibling())
        self.across = {}
        self.passed = []

    def origin(self, step):
        x, yh, z, yl, c = here()
        y = lax.rem(yh * 2 + yl + 4 - step, 4)
        return (lax.div(y, 2), lax.rem(y, 2), c)

    def spread(self):
        x = lax.axis_index("x")
        for step in (1, 3, 2):
            self.ring[step].wait_recv()
            block = self.buffer.at[self.origin(step) + (x,)]
            self.across[step] = [
                self.links.send(block, block, x_device(k)) for k in (2, 1, 3)
            ]

    def forward(self):
        for step in (1, 3, 2):
            for copy in self.across[step]:
                copy.wait_recv()
            block = self.buffer.at[self.origin(step)]
            self.passed.append(self.links.send(block, block, sibling()))

    def arrived(self):
        for copy in [self.pair] + self.passed:
            copy.wait_recv()

    def done(self):
        for copy in [self.pair] + self.passed + list(self.ring.values()):
            copy.wait_send()
        for copies in self.across.values():
            for copy in copies:
                copy.wait_send()


class ZGather:
    def __init__(self, links, buffer):
        x, yh, z, yl, c = here()
        self.links = links
        self.buffer = buffer
        self.right, self.left = z_device(1), z_device(3)
        first, second = buffer.at[z, 0:64], buffer.at[z, 64:128]
        self.right_first = links.send(first, first, self.right)
        self.left_second = links.send(second, second, self.left)
        self.right_second = links.send(second, second, self.right)
        self.left_first = links.send(first, first, self.left)

    def forward(self):
        self.right_first.wait_recv()
        block = self.buffer.at[self.left[2], 0:64]
        self.on_right = self.links.send(block, block, self.right)
        self.left_second.wait_recv()
        block = self.buffer.at[self.right[2], 64:128]
        self.on_left = self.links.send(block, block, self.left)

    def near(self):
        self.right_second.wait_recv()
        self.left_first.wait_recv()

    def far(self):
        self.on_right.wait_recv()
        self.on_left.wait_recv()

    def done(self):
        for copy in (
            self.right_first, self.left_second, self.right_second, self.left_first,
            self.on_right, self.on_left,
        ):
            copy.wait_send()


class ZScatter:
    def __init__(self, links, sends, recv_far, recv_near):
        self.links = links
        self.to_far, self.to_right, self.to_left = (sends.at[i] for i in range(3))
        self.recv_far = recv_far
        self.recv_near = recv_near
        self.right_of, self.left_of = z_device(1), z_device(3)
        self.copies = []
        self.near = []

    def send(self, source, target, device):
        copy = self.links.send(source, target, device)
        self.copies.append(copy)
        return copy

    def far(self, term):
        self.to_far[...] = term.astype(BF16)
        self.far_first = self.send(self.to_far.at[0:64], self.recv_far.at[0], self.right_of)
        self.far_second = self.send(self.to_far.at[64:128], self.recv_far.at[1], self.left_of)

    def right(self, term):
        self.to_right[...] = term.astype(BF16)
        self.near.append(
            self.send(self.to_right.at[64:128], self.recv_near.at[0, 64:128], self.right_of)
        )

    def left(self, term):
        self.to_left[...] = term.astype(BF16)
        self.near.append(
            self.send(self.to_left.at[0:64], self.recv_near.at[1, 0:64], self.left_of)
        )

    def merge(self):
        self.far_first.wait_recv()
        merged = self.to_right[0:64].astype(F32) + self.recv_far[0].astype(F32)
        self.to_right[0:64] = merged.astype(BF16)
        self.near.append(
            self.send(self.to_right.at[0:64], self.recv_near.at[0, 0:64], self.right_of)
        )
        self.far_second.wait_recv()
        merged = self.to_left[64:128].astype(F32) + self.recv_far[1].astype(F32)
        self.to_left[64:128] = merged.astype(BF16)
        self.near.append(
            self.send(self.to_left.at[64:128], self.recv_near.at[1, 64:128], self.left_of)
        )

    def total(self, own):
        for copy in self.near:
            copy.wait_recv()
        return own + self.recv_near[0].astype(F32) + self.recv_near[1].astype(F32)

    def done(self):
        for copy in self.copies:
            copy.wait_send()


class Shrink:
    def __init__(self, links, terms, pair_sum, middle, first_recv, last_recv, y_first):
        self.links = links
        self.terms = terms
        self.pair_sum = pair_sum
        self.middle = middle
        self.first_recv = first_recv
        self.last_recv = last_recv
        self.y_first = y_first
        self.copies = []

    def start(self):
        x, yh, z, yl, c = here()
        self.pair = self.links.send(self.terms.at[:, :, :, 1 - c], self.pair_sum, sibling())

    def send_first(self):
        x, yh, z, yl, c = here()
        self.pair.wait()
        terms, pair_sum = self.terms, self.pair_sum

        @pl.loop(0, 8)
        def _(at):
            h, k = lax.div(at, 4), lax.rem(at, 4)
            for low in range(2):
                pair_sum[h, k, low] = (
                    terms[h, k, low, c].astype(F32) + pair_sum[h, k, low].astype(F32)
                ).astype(BF16)

        self.first = []
        for step in (2, 1, 3):
            if self.y_first:
                device = y_device(step)
                source = pair_sum.at[device[1], :, device[3]]
            else:
                device = x_device(step)
                source = pair_sum.at[:, device[0]]
            self.first.append(self.links.send(source, self.first_recv.at[step - 1], device))

    def send_last(self):
        x, yh, z, yl, c = here()
        for copy in self.first:
            copy.wait()
        got = self.first_recv

        @pl.loop(0, 4)
        def _(at):
            if self.y_first:
                total = self.pair_sum[yh, at, yl].astype(F32)
                for slot in range(3):
                    total = total + got[slot, at].astype(F32)
                self.middle[at] = total.astype(BF16)
            else:
                h, low = lax.div(at, 2), lax.rem(at, 2)
                total = self.pair_sum[h, x, low].astype(F32)
                for slot in range(3):
                    total = total + got[slot, h, low].astype(F32)
                self.middle[h, low] = total.astype(BF16)

        self.second = []
        for step in (2, 1, 3):
            if self.y_first:
                device = x_device(step)
                source = self.middle.at[device[0]]
            else:
                device = y_device(step)
                source = self.middle.at[device[1], device[3]]
            self.second.append(self.links.send(source, self.last_recv.at[step - 1], device))

    def result(self):
        x, yh, z, yl, c = here()
        for copy in self.second:
            copy.wait()
        total = (self.middle[x] if self.y_first else self.middle[yh, yl]).astype(F32)
        for slot in range(3):
            total = total + self.last_recv[slot].astype(F32)
        return total


def shrink_scratch(rows, width, y_first):
    first = (4, rows, width) if y_first else (2, 2, rows, width)
    return [
        pltpu.VMEM((2, 4, 2, rows, width), BF16),
        pltpu.VMEM(first, BF16),
        pltpu.VMEM((3,) + first, BF16),
        pltpu.VMEM((3, rows, width), BF16),
    ]


def everyone():
    return (
        [z_device(s) for s in (1, 2, 3)]
        + [y_device(s) for s in (1, 2, 3)]
        + [x_device(s) for s in (1, 2, 3)]
        + [sibling()]
    )


GELU_A = math.sqrt(2.0 / math.pi)
GELU_B = 0.044715


def gelu_parts(gate):
    square = gate * gate
    curve = jnp.tanh(GELU_A * gate * (1.0 + GELU_B * square))
    half = 0.5 * (1.0 + curve)
    slope = half + 0.5 * gate * (1.0 - curve * curve) * (
        GELU_A * (1.0 + 3.0 * GELU_B * square)
    )
    return gate * half, slope

SCRATCH = dict(
    xn_all=((4, 128, 1024), BF16), wq_all=((2, 2, 2, 4, 64, 256), BF16), wkv_all=((4, 256, 512), BF16),
    q=((2, 4, 2, 128, 128), BF16), cosd=((4, 128, 128), F32), sind=((4, 128, 128), F32),
    kv_all=((2, 2, 2, 4, 2, 128, 256), BF16), attn=((4, 128, 512), BF16),
    recip=((2, 4, 256, 128), F32), wo_all=((2, 2, 2, 4, 64, 256), BF16), acc=((2, 4, 256, 256), F32),
    branch=((128, 1024), F32), h1=((128, 1024), F32), hn_all=((4, 128, 1024), BF16),
    wf_all=((2, 2, 2, 4, 64, 1152), BF16), q_mate=((2, 4, 2, 128, 128), BF16),
    mate_out=((2, 4, 256, 128), BF16), mate_in=((2, 4, 256, 128), BF16),
    sums_out=((2, 4, 1, 256), F32), sums_in=((2, 4, 1, 256), F32),
    inner_out=((2, 4, 1, 256), F32), inner_in=((2, 4, 1, 256), F32),
    d_mate=((2, 4, 256, 256), BF16),
    gate_all=((4, 128, 768), BF16), up_all=((4, 128, 768), BF16), hidden_all=((4, 128, 768), BF16),
    d_mlp_all=((4, 128, 1024), BF16), d_h1=((128, 1024), F32), d_branch_all=((4, 128, 1024), BF16),
    gain_rows=((4, 1, 1024), F32), grads=((4, 128, 1024), BF16),
    d_out=((2, 4, 256, 256), BF16),
    d_kv=((2, 2, 2, 4, 2, 128, 256), BF16), pair_recv=((3, 2, 4, 128, 256), BF16),
    y_recv=((2, 2, 4, 128, 256), BF16),
    kv_send=((4, 8, 512), F32), kv_recv=((4, 8, 512), F32),
    gain_own=((8, 1024), F32), gain_pair=((8, 1024), F32), gain_y=((3, 8, 1024), F32),
    gain_x=((3, 8, 1024), F32), gain_z=((3, 8, 1024), F32),
    own_sum=((128, 1024), F32), z_send=((3, 128, 1024), BF16),
    z_far=((4, 2, 64, 1024), BF16), z_near=((4, 2, 128, 1024), BF16),
    terms_a=((2, 4, 2, 2, 64, 640), BF16), terms_b=((2, 4, 2, 2, 64, 512), BF16),
    terms_k=((2, 4, 2, 2, 32, 256), BF16), terms_v=((2, 4, 2, 2, 32, 256), BF16),
)
SHRINKS = (
    (64, 640, False), (64, 512, False), (64, 128, False), (64, 128, False),
    (64, 128, True), (64, 128, False), (32, 256, True), (32, 256, False),
)
SEMS = 240


class Refs:
    pass


def begin(s, links):
    x, yh, z, yl, c = here()
    xin = s.tokens[...].astype(F32)
    s.xn_all[z] = (xin * inverse_rms(xin) * s.gain_attn_in[...]).astype(BF16)
    greet(everyone())
    ring = ZGather(links, s.xn_all)
    for group in range(2):
        first = pl.multiple_of(group * 512 + z * 128, 128)
        s.wkv_all[yl * 2 + c, :, pl.ds(group * 128, 128)] = quantized(
            s.w_key[:, pl.ds(first, 128)], QEXP_MODEL, 8
        )
        s.wkv_all[yl * 2 + c, :, pl.ds(256 + group * 128, 128)] = quantized(
            s.w_value[:, pl.ds(first, 128)], QEXP_MODEL, 8
        )
    key_part = s.wkv_all.at[yl * 2 + c, :, 0:256]
    value_part = s.wkv_all.at[yl * 2 + c, :, 256:512]
    from_low = links.send(key_part, key_part, y_device(1))
    from_high = links.send(value_part, value_part, y_device(3))
    own = s.wkv_all.at[yl * 2 + c]
    pair = links.send(own, own, sibling())
    s.wq_all[yh, yl, c] = quantized(s.w_query[...], QEXP_MODEL, 8).reshape(4, 64, 256)
    s.gather_q = Gather(links, s.wq_all)
    s.wo_all[yh, yl, c] = quantized(s.w_output[...], QEXP_MODEL, 8).reshape(4, 64, 256)
    s.gather_o = Gather(links, s.wo_all)
    for at, (weight, exponent, bits) in enumerate(
        ((s.w_gate, QEXP_MODEL, 4), (s.w_up, QEXP_MODEL, 4), (s.w_down, QEXP_HIDDEN, 2))
    ):
        s.wf_all[yh, yl, c, :, :, at * 384 : at * 384 + 384] = quantized(
            weight[...], exponent, bits
        ).reshape(4, 64, 384)
    s.gather_f = Gather(links, s.wf_all)
    lane = lax.broadcasted_iota(jnp.int32, (128, 128), 1)
    row = lax.broadcasted_iota(jnp.int32, (128, 128), 0)
    freqs = jnp.exp(lax.rem(lane, 64).astype(F32) * (-2.0 * math.log(THETA) / DH))
    start = s.lengths[0, 0]
    base = yh * 2048 + yl * 256 + c * 128

    def tables(block):
        tok = row + (base + block * 512)
        angle = jnp.where(tok >= start, tok - start, tok).astype(F32) * freqs
        s.cosd[block] = jnp.cos(angle)
        sine = jnp.sin(angle)
        s.sind[block] = jnp.where(lane < 64, -sine, sine)

    tables(0)
    ring.forward()
    tables(1)
    from_low.wait_recv()
    from_high.wait_recv()
    other = s.wkv_all.at[(1 - yl) * 2 + c]
    passed = links.send(other, other, sibling())
    s.gather_q.spread()
    tables(2)
    tables(3)
    pair.wait_recv()
    passed.wait_recv()

    def project_kv(block):
        lin = dot(s.xn_all[block], s.wkv_all[...].reshape(1024, 512))
        cosd, sind = s.cosd[block], s.sind[block]
        for group in range(2):
            key = lin[:, group * 128 : group * 128 + 128]
            key = (key * cosd + swap_halves(key) * sind).astype(BF16)
            value = lin[:, 256 + group * 128 : 384 + group * 128].astype(BF16)
            s.kv_all[group, yh, yl, block, c, :, 0:128] = key
            s.kv_all[group, yh, yl, block, c, :, 128:256] = value

    def project_q(block):
        cosd, sind = s.cosd[block], s.sind[block]
        for group in range(2):
            lin = dot(s.xn_all[block], s.wq_all[group].reshape(1024, 256))
            for head in range(2):
                query = lin[:, head * 128 : head * 128 + 128]
                query = (query * cosd + swap_halves(query) * sind) * (SCALE / CAP)
                s.q[group, block, head] = query.astype(BF16)

    project_kv(z)
    ring.near()
    project_kv(ring.left[2])
    project_kv(ring.right[2])
    ring.far()
    project_kv(lax.rem(z + 2, 4))
    s.kv_pair, s.kv_near, s.kv_far, s.q_send = [], [], [], []
    for group in range(2):
        mine = s.kv_all.at[group, yh, yl, :, c]
        s.kv_pair.append(links.send(mine, mine, sibling()))
        s.kv_near.append(links.send(mine, mine, (x, yh, z, 1 - yl, c)))
        s.kv_far.append(links.plan(mine, mine, mate()))
        s.q_send.append(links.plan(s.q.at[group], s.q_mate.at[group], mate()))

    @pl.when(yh == 0)
    def _():
        for group in range(2):
            s.kv_far[group].start()

    s.gather_o.spread()
    s.gather_q.forward()
    s.gather_q.arrived()
    for block in range(4):
        project_q(block)

    @pl.when(yh == 1)
    def _():
        for group in range(2):
            s.q_send[group].start()

    s.gather_f.spread()
    ring.done()
    for copy in (from_low, from_high, pair, passed):
        copy.wait_send()
    s.gather_q.done()


def attend(s, links):
    x, yh, z, yl, c = here()
    start = s.lengths[0, 0]
    lane = lax.broadcasted_iota(jnp.int32, (1, 256), 1)
    ones = jnp.ones((256, 128), BF16)
    row = lax.rem(lax.broadcasted_iota(jnp.int32, (256, 1), 0), 128)

    def block_sum(query, q_base, group, from_h, from_l, units, diagonal):
        token_q = row + q_base
        floor = jnp.where(token_q >= start, start, 0)
        total = None
        for unit in units:
            both = s.kv_all[group, from_h, from_l, unit].reshape(256, 256)
            token_k = lane + (from_h * 2048 + unit * 512 + from_l * 256)
            curved = jnp.tanh(dot_nt(query, both[:, :128]))
            weight = jnp.exp2(curved * (CAP * LOG2E))
            seen = token_k >= floor
            if diagonal and unit == units[-1]:
                seen = seen & (token_k <= token_q)
            weight = jnp.where(seen, weight, 0.0).astype(BF16)
            term = dot(weight, jnp.concatenate([both[:, 128:], ones], axis=1))
            total = term if total is None else total + term
        return total

    own_base = yh * 2048 + yl * 256 + c * 128
    mate_base = 2048 + (1 - yl) * 256 + c * 128

    def same_half(group, from_l, first):
        for block in range(4):
            total = block_sum(
                s.q[group, block].reshape(256, 128), own_base + block * 512, group, yh, from_l,
                list(range(block + 1)), True,
            )
            if first:
                s.acc[group, block] = total
            else:
                s.acc[group, block] += total

    def far_half(group):
        @pl.loop(0, 4)
        def _(block):
            s.acc[group, block] += block_sum(
                s.q[group, block].reshape(256, 128), own_base + block * 512, group, 0, 1 - yl,
                [0, 1, 2, 3], False,
            )

    def for_mate(group):
        @pl.loop(0, 4)
        def _(block):
            total = block_sum(
                s.q_mate[group, block].reshape(256, 128), mate_base + block * 512, group, 0,
                1 - yl, [0, 1, 2, 3], False,
            )
            s.mate_out[group, block] = total[:, :128].astype(BF16)
            s.sums_out[group, block] = total[:, 128:256].T[0:1]

    def pass_plan(group, from_h, from_l):
        block = s.kv_all.at[group, from_h, from_l, :, c]
        return links.plan(block, block, sibling())

    near_pass = [pass_plan(group, yh, 1 - yl) for group in range(2)]
    far_pass = [pass_plan(group, 0, 1 - yl) for group in range(2)]
    back = []
    for group in range(2):
        back.append(links.plan(s.mate_out.at[group], s.mate_in.at[group], mate()))
        back.append(links.plan(s.sums_out.at[group], s.sums_in.at[group], mate()))

    @pl.when(yh == 0)
    def _():
        s.mate_in[...] = jnp.zeros_like(s.mate_in)
        s.sums_in[...] = jnp.zeros_like(s.sums_in)

    for group in range(2):
        s.kv_pair[group].wait_recv()
        same_half(group, yl, True)
    s.gather_o.forward()
    for group in range(2):
        s.kv_near[group].wait_recv()
        near_pass[group].start()

        @pl.when(yh == 1)
        def _():
            s.kv_far[group].wait_recv()
            far_pass[group].start()

        near_pass[group].wait_recv()
        same_half(group, 1 - yl, False)

        @pl.when(yh == 1)
        def _():
            far_pass[group].wait_recv()
            far_half(group)

        @pl.when(yh == 0)
        def _():
            s.q_send[group].wait_recv()
            for_mate(group)
            back[2 * group].start()
            back[2 * group + 1].start()

    for group in range(2):

        @pl.when(yh == 1)
        def _():
            back[2 * group].wait_recv()
            back[2 * group + 1].wait_recv()

        for block in range(4):
            total = s.acc[group, block]
            more = jnp.broadcast_to(s.sums_in[group, block], (128, 256)).T
            inverse = 1.0 / (total[:, 128:256] + more)
            s.recip[group, block] = inverse
            out = total[:, :128] + s.mate_in[group, block].astype(F32)
            out = (out * inverse).astype(BF16)
            for head in range(2):
                first = group * 256 + head * 128
                s.attn[block, :, first : first + 128] = out[head * 128 : head * 128 + 128]
    for group in range(2):
        s.kv_pair[group].wait_send()
        s.kv_near[group].wait_send()
        near_pass[group].wait_send()

    @pl.when(yh == 0)
    def _():
        for group in range(2):
            s.kv_far[group].wait_send()
        for copy in back:
            copy.wait_send()

    @pl.when(yh == 1)
    def _():
        for group in range(2):
            far_pass[group].wait_send()
            s.q_send[group].wait_send()


def all_terms(scatter, term_of):
    x, yh, z, yl, c = here()
    scatter.far(term_of(lax.rem(z + 2, 4)))
    scatter.right(term_of(lax.rem(z + 1, 4)))
    scatter.left(term_of(lax.rem(z + 3, 4)))
    scatter.merge()
    return term_of(z)


def output_projection(s, links):
    x, yh, z, yl, c = here()

    def term_of(block):
        left = s.attn[block]
        return dot_nt(left[:, :256], s.wo_all[0].reshape(1024, 256)) + dot_nt(
            left[:, 256:], s.wo_all[1].reshape(1024, 256)
        )

    s.gather_o.arrived()
    scatter = ZScatter(links, s.z_send, s.z_far.at[0], s.z_near.at[0])
    own = all_terms(scatter, term_of)
    s.gather_f.forward()
    branch = scatter.total(own)
    h1 = s.tokens[...].astype(F32) + branch * inverse_rms(branch) * s.gain_attn_out[...]
    s.hn_all[z] = (h1 * inverse_rms(h1) * s.gain_mlp_in[...]).astype(BF16)
    s.ring = ZGather(links, s.hn_all)
    s.branch[...] = branch
    s.h1[...] = h1
    s.gather_f.arrived()
    scatter.done()
    s.gather_o.done()
    s.gather_f.done()


def feed_forward(s, links):
    x, yh, z, yl, c = here()

    def term_of(block):
        left = s.hn_all[block]
        total = None
        for group in range(2):
            cols = slice(group * 384, group * 384 + 384)
            gate = dot(left, s.wf_all[group, ..., 0:384].reshape(1024, 384))
            up = dot(left, s.wf_all[group, ..., 384:768].reshape(1024, 384))
            value, slope = gelu_parts(gate)
            s.gate_all[block, :, cols] = value.astype(BF16)
            s.up_all[block, :, cols] = (up * slope).astype(BF16)
            hidden = (value * up).astype(BF16)
            s.hidden_all[block, :, cols] = hidden
            term = dot_nt(hidden, s.wf_all[group, ..., 768:1152].reshape(1024, 384))
            total = term if total is None else total + term
        return total

    s.ring.forward()
    scatter = ZScatter(links, s.z_send, s.z_far.at[1], s.z_near.at[1])
    ring = s.ring
    s.own_sum[...] = term_of(z)
    ring.near()
    scatter.left(term_of(ring.left[2]))
    scatter.right(term_of(ring.right[2]))
    ring.far()
    scatter.far(term_of(lax.rem(z + 2, 4)))
    scatter.merge()
    mlp = scatter.total(s.own_sum[...])
    into, gain_part = rms_back(mlp, s.gain_mlp_out[...], s.out_grad[...].astype(F32))
    s.d_mlp_all[z] = into.astype(BF16)
    s.ring = ZGather(links, s.d_mlp_all)
    s.gain_rows[3] = gain_part
    s.mixed[...] = (s.h1[...] + mlp * inverse_rms(mlp) * s.gain_mlp_out[...]).astype(BF16)
    ring.done()
    scatter.done()


def feed_forward_back(s, links):
    x, yh, z, yl, c = here()

    def term_of(block):
        left = s.d_mlp_all[block]
        total = None
        for group in range(2):
            cols = slice(group * 384, group * 384 + 384)
            d_hidden = dot(left, s.wf_all[group, ..., 768:1152].reshape(1024, 384))
            d_gate = (d_hidden * s.up_all[block, :, cols].astype(F32)).astype(BF16)
            d_up = (d_hidden * s.gate_all[block, :, cols].astype(F32)).astype(BF16)
            s.up_all[block, :, cols] = d_gate
            s.gate_all[block, :, cols] = d_up
            term = dot_nt(d_gate, s.wf_all[group, ..., 0:384].reshape(1024, 384)) + dot_nt(
                d_up, s.wf_all[group, ..., 384:768].reshape(1024, 384)
            )
            total = term if total is None else total + term
        return total

    scatter = ZScatter(links, s.z_send, s.z_far.at[2], s.z_near.at[2])
    ring = s.ring
    s.own_sum[...] = term_of(z)
    ring.forward()
    ring.near()
    scatter.left(term_of(ring.left[2]))
    scatter.right(term_of(ring.right[2]))
    ring.far()
    scatter.far(term_of(lax.rem(z + 2, 4)))
    d_mlp = s.d_mlp_all[...].reshape(512, 1024)
    hn = s.hn_all[...].reshape(512, 1024)
    for group in range(2):
        cols = slice(group * 384, group * 384 + 384)
        down = dot_tn(d_mlp, s.hidden_all[:, :, cols].reshape(512, 384)).astype(BF16)
        s.terms_a[group, :, :, :, :, 0:384] = down.reshape(4, 2, 2, 64, 384)
    scatter.merge()
    for group in range(2):
        cols = slice(group * 384, group * 384 + 384)
        gate = dot_tn(hn, s.up_all[:, :, cols].reshape(512, 384)).astype(BF16)
        gate = gate.reshape(4, 2, 2, 64, 384)
        s.terms_a[group, :, :, :, :, 384:640] = gate[..., 0:256]
        s.terms_b[group, :, :, :, :, 0:128] = gate[..., 256:384]
    d_hn = scatter.total(s.own_sum[...])
    into, gain_part = rms_back(s.h1[...], s.gain_mlp_in[...], d_hn)
    s.gain_rows[2] = gain_part
    d_h1 = s.out_grad[...].astype(F32) + into
    s.d_h1[...] = d_h1
    into, gain_part = rms_back(s.branch[...], s.gain_attn_out[...], d_h1)
    s.d_branch_all[z] = into.astype(BF16)
    s.ring = ZGather(links, s.d_branch_all)
    s.gain_rows[1] = gain_part
    for group in range(2):
        cols = slice(group * 384, group * 384 + 384)
        up = dot_tn(hn, s.gate_all[:, :, cols].reshape(512, 384)).astype(BF16)
        s.terms_b[group, :, :, :, :, 128:512] = up.reshape(4, 2, 2, 64, 384)
    s.ring.forward()
    s.shrink[0].start()
    s.shrink[1].start()
    ring.done()
    scatter.done()


def attend_back(s, links):
    x, yh, z, yl, c = here()
    ring = s.ring
    lane = lax.broadcasted_iota(jnp.int32, (256, 128), 1)

    def extra_lanes(inner):
        high = inner.astype(BF16).astype(F32)
        low = inner - high
        return jnp.where(lane == 0, high, jnp.where(lane == 1, low, 0.0)).astype(BF16)

    def cotangent(block):
        for group in range(2):
            cols = slice(group * 256, group * 256 + 256)
            rows = dot(s.d_branch_all[block], s.wo_all[group].reshape(1024, 256))
            rows = rows.astype(BF16).astype(F32)
            rows = jnp.concatenate([rows[:, :128], rows[:, 128:]], axis=0)
            outs = s.attn[block, :, cols].astype(F32)
            outs = jnp.concatenate([outs[:, :128], outs[:, 128:]], axis=0)
            scaled = (rows * s.recip[group, block]).astype(BF16)
            inner = -jnp.sum(scaled.astype(F32) * outs, axis=1, keepdims=True)
            inner = jnp.broadcast_to(inner, (256, 128))
            s.inner_out[group, block] = inner.T[0:1]
            s.d_out[group, block] = jnp.concatenate([scaled, extra_lanes(inner)], axis=1)

    cotangent(z)
    s.acc[...] = jnp.zeros_like(s.acc)
    ring.near()
    cotangent(ring.left[2])
    cotangent(ring.right[2])
    ring.far()
    cotangent(lax.rem(z + 2, 4))
    lend = []
    for group in range(2):
        lend.append(
            links.plan(
                s.d_out.at[group, :, :, 0:128], s.d_mate.at[group, :, :, 0:128], mate()
            )
        )
        lend.append(links.plan(s.inner_out.at[group], s.inner_in.at[group], mate()))

    @pl.when(yh == 1)
    def _():
        for copy in lend:
            copy.start()

    s.shrink[0].send_first()
    s.shrink[1].send_first()
    d_branch = s.d_branch_all[...].reshape(512, 1024)
    for group in range(2):
        cols = slice(group * 256, group * 256 + 256)
        back = dot_tn(d_branch, s.attn[:, :, cols].reshape(512, 256)).astype(BF16)
        back = back.reshape(4, 2, 2, 64, 256)
        s.terms_a[group, :, :, :, :, 0:128] = back[..., 0:128]
        s.terms_b[group, :, :, :, :, 0:128] = back[..., 128:256]
    s.shrink[2].start()
    s.shrink[3].start()
    start = s.lengths[0, 0]
    ones = jnp.where(lane < 2, 1.0, 0.0).astype(BF16)
    token_row = lax.rem(lax.broadcasted_iota(jnp.int32, (1, 256), 1), 128)
    token_col = lax.broadcasted_iota(jnp.int32, (256, 1), 0)

    own_base = yh * 2048 + yl * 256 + c * 128
    mate_base = 2048 + (1 - yl) * 256 + c * 128

    def unit_back(group, from_h, from_l, unit, first_block, diagonal, lent=False):
        both = s.kv_all[group, from_h, from_l, unit].reshape(256, 256)
        key, value = both[:, :128], both[:, 128:]
        count = 4 - first_block
        queries, cots, base, rows = (
            (s.q_mate, s.d_mate, mate_base, slice(128, 256))
            if lent
            else (s.q, s.d_out, own_base, slice(0, 128))
        )
        query = queries[group, first_block:].reshape(count * 256, 128)
        cot = cots[group, first_block:].reshape(count * 256, 256)
        curved = jnp.tanh(dot_nt(key, query))
        weight = jnp.exp2(curved * (CAP * LOG2E))
        token_k = token_col + (from_h * 2048 + unit * 512 + from_l * 256)
        pieces = []
        for block in range(first_block, 4):
            token_q = token_row + (base + block * 512)
            seen = token_k >= jnp.where(token_q >= start, start, 0)
            if diagonal and block == first_block:
                seen = seen & (token_k <= token_q)
            at = (block - first_block) * 256
            pieces.append(jnp.where(seen, weight[:, at : at + 256], 0.0))
        weight = jnp.concatenate(pieces, axis=1)
        grown = dot_nt(jnp.concatenate([value, ones], axis=1), cot)
        slope = (weight * grown * (1.0 - curved * curved)).astype(BF16)
        d_key = dot(slope, query) * CAP
        d_value = dot(weight.astype(BF16), cot[:, :128])
        both = jnp.concatenate([d_key, d_value], axis=1)
        if lent:
            both = both + s.d_kv[group, from_h, from_l, unit].astype(F32).reshape(256, 256)
        s.d_kv[group, from_h, from_l, unit] = both.astype(BF16).reshape(2, 128, 256)
        d_query = dot(key.T, slope)
        for block in range(first_block, 4):
            at = (block - first_block) * 256
            s.acc[group, block, rows, :] += d_query[:, at : at + 256]

    def same_half(group, from_l):
        for unit in range(4):
            unit_back(group, yh, from_l, unit, unit, True)

    def pair_plan(slot, group, from_h, from_l):
        return links.plan(
            s.d_kv.at[group, from_h, from_l, :, 1 - c], s.pair_recv.at[slot, group], sibling()
        )

    def add_pair(slot, group, from_h, from_l):
        s.d_kv[group, from_h, from_l, :, c] = (
            s.d_kv[group, from_h, from_l, :, c].astype(F32)
            + s.pair_recv[slot, group].astype(F32)
        ).astype(BF16)

    far_pair = [pair_plan(0, group, 0, 1 - yl) for group in range(2)]
    near_pair = [pair_plan(1, group, yh, 1 - yl) for group in range(2)]
    own_pair = [pair_plan(2, group, yh, yl) for group in range(2)]
    far_send = [
        links.plan(s.d_kv.at[group, 0, 1 - yl, :, c], s.y_recv.at[0, group], mate())
        for group in range(2)
    ]
    near_send = [
        links.plan(
            s.d_kv.at[group, yh, 1 - yl, :, c], s.y_recv.at[1, group], (x, yh, z, 1 - yl, c)
        )
        for group in range(2)
    ]
    returned = [
        links.plan(s.mate_out.at[group], s.mate_in.at[group], mate()) for group in range(2)
    ]

    @pl.when(yh == 1)
    def _():
        s.y_recv[0] = jnp.zeros((2, 4, 128, 256), BF16)
        for group in range(2):

            @pl.loop(0, 4)
            def _(unit):
                unit_back(group, 0, 1 - yl, unit, 0, False)

            far_pair[group].start()

    same_half(0, 1 - yl)

    @pl.when(yh == 1)
    def _():
        for group in range(2):
            far_pair[group].wait()
            add_pair(0, group, 0, 1 - yl)
            far_send[group].start()

    same_half(1, 1 - yl)
    for i in (2, 3):
        s.shrink[i].send_first()

    @pl.when(yh == 0)
    def _():
        for group in range(2):
            lend[2 * group].wait_recv()
            lend[2 * group + 1].wait_recv()
            for block in range(4):
                inner = jnp.broadcast_to(s.inner_in[group, block], (128, 256)).T
                s.d_mate[group, block, :, 128:256] = extra_lanes(inner)

            @pl.loop(0, 4)
            def _(unit):
                unit_back(group, 0, 1 - yl, unit, 0, False, True)

            for block in range(4):
                s.mate_out[group, block] = s.acc[group, block, 128:256, :].T.astype(BF16)
            returned[group].start()

    for group in range(2):
        near_pair[group].start()
    same_half(0, yl)
    own_pair[0].start()
    for group in range(2):
        near_pair[group].wait()
        add_pair(1, group, yh, 1 - yl)
        near_send[group].start()
    same_half(1, yl)
    own_pair[1].start()

    @pl.when(yh == 1)
    def _():
        for copy in returned:
            copy.wait_recv()

    def rope_back(values, block):
        return values * s.cosd[block] - swap_halves(values) * s.sind[block]

    for group in range(2):
        for block in range(4):
            d_query = s.acc[group, block, 0:128, :].T + s.mate_in[group, block].astype(F32)
            for head in range(2):
                turned = rope_back(d_query[head * 128 : head * 128 + 128], block) * SCALE
                at = group * 256 + head * 128
                s.grads[block, :, at : at + 128] = turned.astype(BF16)
    xa = s.xn_all[...].reshape(512, 1024)
    for group in range(2):
        back = dot_tn(xa, s.grads[:, :, group * 256 : group * 256 + 256].reshape(512, 256))
        back = back.astype(BF16).reshape(4, 2, 2, 64, 256)
        s.terms_a[group, :, :, :, :, 0:128] = back[..., 0:128]
        s.terms_b[group, :, :, :, :, 0:128] = back[..., 128:256]
    s.shrink[4].start()
    s.shrink[5].start()
    for i in (0, 1, 2, 3):
        s.shrink[i].send_last()
    for i in (4, 5):
        s.shrink[i].send_first()
    for group in range(2):
        own_pair[group].wait()
        near_send[group].wait()

    @pl.when(yh == 0)
    def _():
        for copy in far_send:
            copy.wait_recv()
        for copy in returned:
            copy.wait_send()

    @pl.when(yh == 1)
    def _():
        for copy in far_send + lend:
            copy.wait_send()

    for group in range(2):
        for block in range(4):
            both = (
                s.d_kv[group, yh, yl, block, c].astype(F32)
                + s.pair_recv[2, group, block].astype(F32)
                + s.y_recv[0, group, block].astype(F32)
                + s.y_recv[1, group, block].astype(F32)
            )
            d_key = both[:, :128].astype(BF16).astype(F32)
            at = 512 + group * 128
            s.grads[block, :, at : at + 128] = rope_back(d_key, block).astype(BF16)
            at = 768 + group * 128
            s.grads[block, :, at : at + 128] = both[:, 128:].astype(BF16)
    ring.done()


def finish(s, links):
    x, yh, z, yl, c = here()
    s.gain_own[...] = jnp.zeros_like(s.gain_own)

    def term_of(block):
        left = s.grads[block]
        total = dot_nt(left[:, 512:], s.wkv_all[...].reshape(1024, 512))
        for group in range(2):
            total = total + dot_nt(
                left[:, group * 256 : group * 256 + 256], s.wq_all[group].reshape(1024, 256)
            )
        s.gain_own[0:1] += jnp.sum(total * s.xn_all[block].astype(F32), axis=0, keepdims=True)
        return total

    scatter = ZScatter(links, s.z_send, s.z_far.at[3], s.z_near.at[3])
    xa = s.xn_all[...].reshape(512, 1024)
    back = dot_tn(xa, s.grads[:, :, 512:].reshape(512, 512))
    for k in range(4):
        for h in range(2):
            for low in range(2):
                for core in range(2):
                    rows = [k * 256 + h * 128 + low * 16 + core * 8 + 32 * i for i in range(4)]
                    piece = jnp.concatenate([back[row : row + 8] for row in rows], axis=0)
                    piece = piece.astype(BF16)
                    s.terms_k[h, k, low, core] = piece[:, :256]
                    s.terms_v[h, k, low, core] = piece[:, 256:]
    s.shrink[6].start()
    s.shrink[7].start()
    scatter.far(term_of(lax.rem(z + 2, 4)))
    scatter.right(term_of(lax.rem(z + 1, 4)))
    scatter.left(term_of(lax.rem(z + 3, 4)))
    s.shrink[6].send_first()
    s.shrink[7].send_first()
    scatter.merge()
    own = term_of(z)
    s.gain_own[0:1] = s.gain_own[0:1] / s.gain_attn_in[...]
    for i in (1, 2, 3):
        s.gain_own[i : i + 1] = s.gain_rows[i]
    pair = links.send(s.gain_own, s.gain_pair, sibling())
    for i in (4, 5):
        s.shrink[i].send_last()
    pair.wait()
    s.gain_pair[...] += s.gain_own[...]
    sent = [links.send(s.gain_pair, s.gain_y.at[k - 1], y_device(k)) for k in (2, 1, 3)]
    s.shrink[6].send_last()
    s.shrink[7].send_last()
    for copy in sent:
        copy.wait()
    s.gain_own[...] = s.gain_pair[...] + (s.gain_y[0] + s.gain_y[2]) + s.gain_y[1]
    sent = [links.send(s.gain_own, s.gain_x.at[k - 1], x_device(k)) for k in (2, 1, 3)]
    d_xn = scatter.total(own)
    into, _ = rms_back(s.tokens[...].astype(F32), s.gain_attn_in[...], d_xn)
    s.tokens_grad[...] = (s.d_h1[...] + into).astype(BF16)
    first = s.shrink[0].result()
    s.dwd[...] = first[:, 0:384]
    s.dwg[:, 0:256] = first[:, 384:640]
    second = s.shrink[1].result()
    s.dwg[:, 256:384] = second[:, 0:128]
    s.dwu[...] = second[:, 128:512]
    s.dwo[:, 0:128] = s.shrink[2].result()
    s.dwo[:, 128:256] = s.shrink[3].result()
    for copy in sent:
        copy.wait()
    s.gain_pair[...] = s.gain_own[...] + (s.gain_x[0] + s.gain_x[2]) + s.gain_x[1]
    sent = [links.send(s.gain_pair, s.gain_z.at[k - 1], z_device(k)) for k in (2, 1, 3)]
    s.kv_send[:, :, 0:256] = s.shrink[6].result().reshape(4, 8, 256)
    s.kv_send[:, :, 256:512] = s.shrink[7].result().reshape(4, 8, 256)
    moved = []
    for step in (2, 1, 3):
        device = z_device(step)
        moved.append(links.send(s.kv_send.at[device[2]], s.kv_recv.at[z], device))
    s.kv_recv[z] = s.kv_send[z]
    s.dwq[:, 0:128] = s.shrink[4].result()
    s.dwq[:, 128:256] = s.shrink[5].result()
    for copy in sent:
        copy.wait()
    s.gains[...] = s.gain_pair[...] + (s.gain_z[0] + s.gain_z[2]) + s.gain_z[1]
    for copy in moved:
        copy.wait()
    for origin in range(4):
        for group in range(2):
            at = group * 512 + origin * 128
            s.dwk[:, at : at + 128] = s.kv_recv[origin, :, group * 128 : group * 128 + 128]
            s.dwv[:, at : at + 128] = s.kv_recv[
                origin, :, 256 + group * 128 : 384 + group * 128
            ]
    scatter.done()


OPERANDS = (
    "tokens", "lengths", "w_query", "w_key", "w_value", "w_output", "w_gate", "w_up", "w_down",
    "gain_attn_in", "gain_attn_out", "gain_mlp_in", "gain_mlp_out", "out_grad",
)
RESULTS = dict(
    mixed=((128, 1024), BF16), tokens_grad=((128, 1024), BF16), dwq=((64, 256), F32),
    dwk=((8, 1024), F32), dwv=((8, 1024), F32), dwo=((64, 256), F32), dwg=((64, 384), F32),
    dwu=((64, 384), F32), dwd=((64, 384), F32), gains=((8, 1024), F32),
)


def layer_kernel(*refs):
    s = Refs()
    names = list(OPERANDS) + list(RESULTS) + list(SCRATCH)
    for name, ref in zip(names, refs):
        setattr(s, name, ref)
    rest = refs[len(names) :]
    links = Links(rest[-2], rest[-1])
    terms = (
        s.terms_a, s.terms_b, s.terms_a.at[..., 0:128], s.terms_b.at[..., 0:128],
        s.terms_a.at[..., 0:128], s.terms_b.at[..., 0:128], s.terms_k, s.terms_v,
    )
    s.shrink = [
        Shrink(links, terms[i], *rest[4 * i : 4 * i + 4], SHRINKS[i][2])
        for i in range(len(SHRINKS))
    ]
    begin(s, links)
    attend(s, links)
    output_projection(s, links)
    feed_forward(s, links)
    feed_forward_back(s, links)
    attend_back(s, links)
    finish(s, links)


def run_layer(*operands):
    scratch = [pltpu.VMEM(shape, kind) for shape, kind in SCRATCH.values()]
    for rows, width, y_first in SHRINKS:
        scratch += shrink_scratch(rows, width, y_first)
    scratch += [pltpu.SemaphoreType.DMA((SEMS,))] * 2
    return pl.pallas_call(
        layer_kernel,
        name="layer",
        out_shape=tuple(jax.ShapeDtypeStruct(shape, kind) for shape, kind in RESULTS.values()),
        in_specs=[VM, SM] + [VM] * 12,
        out_specs=tuple(VM for _ in RESULTS),
        scratch_shapes=scratch,
        compiler_params=pltpu.CompilerParams(
            collective_id=1, has_side_effects=True, vmem_limit_bytes=VMEM_LIMIT
        ),
    )(*operands)


def leave_kernel(*refs):
    count = len(refs) // 2
    for i in range(count):
        refs[count + i][...] = refs[i][...]


def run_leave(results):
    return pl.pallas_call(
        leave_kernel,
        name="leave",
        out_shape=tuple(jax.ShapeDtypeStruct(r.shape, r.dtype) for r in results),
        in_specs=[VM] * len(results),
        out_specs=tuple(VM for _ in results),
    )(*results)


def per_device(
    tokens, lengths, w_query, w_key, w_value, w_output, w_gate, w_up, w_down,
    gain_attn_in, gain_attn_out, gain_mlp_in, gain_mlp_out, out_grad,
):
    gain_rows = [
        gain.reshape(1, -1) for gain in (gain_attn_in, gain_attn_out, gain_mlp_in, gain_mlp_out)
    ]
    *results, gains = run_layer(
        tokens, lengths, w_query, w_key, w_value, w_output, w_gate, w_up, w_down,
        *gain_rows, out_grad,
    )
    x, yh, z, yl, c = here()
    first = ((((x * 2 + yh) * 4 + z) * 2 + yl) * 2 + c) * 8
    own_gains = lax.dynamic_slice(gains, (0, first), (4, 8))
    return tuple(run_leave(results)) + tuple(own_gains[i] for i in range(4))


def solution(mesh):
    grid = Mesh(mesh.devices.reshape(4, 2, 4, 2, 2), AXES)
    tokens = P(AXES, None)
    split = P(("yl", "c"), ("yh", "z"))
    rows = P(("yl", "c"), None)
    grads = P(("x", "yl", "c"), ("yh", "z"))
    gains = P(AXES)
    return jax.shard_map(
        per_device,
        mesh=grid,
        in_specs=(tokens, P("x", None), split, rows, rows, split, split, split, split)
        + (P(),) * 4
        + (tokens,),
        out_specs=(tokens, tokens, grads, tokens, tokens, grads, grads, grads, grads)
        + (gains,) * 4,
        check_vma=False,
    )
```

```python
import math

import jax
import jax.numpy as jnp
from jax import lax
from jax.experimental import pallas as pl
from jax.experimental.pallas import tpu as pltpu
from jax.sharding import Mesh
from jax.sharding import PartitionSpec as P

DH = 128
QEXP_MODEL = 10
QEXP_HIDDEN = 11
CAP = 50.0
EPSILON = 1e-06
THETA = 10000.0
SCALE = DH ** (-0.5)
AXES = ("x", "yh", "z", "yl", "c")
BY_ID = pl.DeviceIdType.MESH
F32 = jnp.float32
BF16 = jnp.bfloat16
VM = pl.BlockSpec(memory_space=pltpu.VMEM)
SM = pl.BlockSpec(memory_space=pltpu.SMEM)
LOG2E = 1.4426950408889634
VMEM_LIMIT = 63 * 2**20


def here():
    return tuple(lax.axis_index(name) for name in AXES)


def z_device(step):
    x, yh, z, yl, c = here()
    return (x, yh, lax.rem(z + step, 4), yl, c)


def y_device(step):
    x, yh, z, yl, c = here()
    y = lax.rem(yh * 2 + yl + step, 4)
    return (x, lax.div(y, 2), z, lax.rem(y, 2), c)


def x_device(step):
    x, yh, z, yl, c = here()
    return (lax.rem(x + step, 4), yh, z, yl, c)


def sibling():
    x, yh, z, yl, c = here()
    return (x, yh, z, yl, 1 - c)


def mate():
    x, yh, z, yl, c = here()
    return (x, 1 - yh, z, 1 - yl, c)


def greet(devices):
    barrier = pltpu.get_barrier_semaphore()
    for device in devices:
        pl.semaphore_signal(barrier, inc=1, device_id=device, device_id_type=BY_ID)
    pl.semaphore_wait(barrier, len(devices))


class Links:
    def __init__(self, send_sems, recv_sems):
        self.send_sems = send_sems
        self.recv_sems = recv_sems
        self.used = 0

    def plan(self, source, target, device):
        at = self.used
        self.used += 1
        return pltpu.make_async_remote_copy(
            src_ref=source,
            dst_ref=target,
            send_sem=self.send_sems.at[at],
            recv_sem=self.recv_sems.at[at],
            device_id=device,
            device_id_type=BY_ID,
        )

    def send(self, source, target, device):
        copy = self.plan(source, target, device)
        copy.start()
        return copy


def dot(left, right):
    return lax.dot_general(left, right, (((1,), (0,)), ((), ())), preferred_element_type=F32)


def dot_nt(left, right):
    return lax.dot_general(left, right, (((1,), (1,)), ((), ())), preferred_element_type=F32)


def dot_tn(left, right):
    return lax.dot_general(left, right, (((0,), (0,)), ((), ())), preferred_element_type=F32)


def quantized(weight, exponent, bits):
    shift = 8 - bits
    code = jnp.clip(jnp.floor(weight.astype(F32) * 2.0**exponent) + 128.0, 0.0, 255.0)
    if shift:
        code = (
            jnp.minimum(jnp.floor((code + 2.0 ** (shift - 1)) * 2.0 ** (-shift)), 2.0**bits - 1.0)
            * 2.0**shift
        )
    return ((code - 128.0) * 2.0 ** (-exponent)).astype(BF16)


def inverse_rms(values):
    return lax.rsqrt(jnp.mean(values * values, axis=-1, keepdims=True) + EPSILON)


def rms_back(values, gain, incoming):
    inverse = inverse_rms(values)
    scaled = incoming * gain
    inner = jnp.mean(scaled * values, axis=-1, keepdims=True)
    into = inverse * (scaled - values * (inverse * inverse) * inner)
    gain_part = jnp.sum(incoming * values * inverse, axis=0, keepdims=True)
    return into, gain_part


def swap_halves(values):
    half = values.shape[-1] // 2
    return jnp.concatenate([values[..., half:], values[..., :half]], axis=-1)


class Gather:
    def __init__(self, links, buffer):
        x, yh, z, yl, c = here()
        self.links = links
        self.buffer = buffer
        quarter = buffer.at[yh, yl, c, x]
        self.ring = {step: links.send(quarter, quarter, y_device(step)) for step in (2, 1, 3)}
        own = buffer.at[yh, yl, c]
        self.pair = links.send(own, own, sibling())
        self.across = {}
        self.passed = []

    def origin(self, step):
        x, yh, z, yl, c = here()
        y = lax.rem(yh * 2 + yl + 4 - step, 4)
        return (lax.div(y, 2), lax.rem(y, 2), c)

    def spread(self):
        x = lax.axis_index("x")
        for step in (1, 3, 2):
            self.ring[step].wait_recv()
            block = self.buffer.at[self.origin(step) + (x,)]
            self.across[step] = [
                self.links.send(block, block, x_device(k)) for k in (2, 1, 3)
            ]

    def forward(self):
        for step in (1, 3, 2):
            for copy in self.across[step]:
                copy.wait_recv()
            block = self.buffer.at[self.origin(step)]
            self.passed.append(self.links.send(block, block, sibling()))

    def arrived(self):
        for copy in [self.pair] + self.passed:
            copy.wait_recv()

    def done(self):
        for copy in [self.pair] + self.passed + list(self.ring.values()):
            copy.wait_send()
        for copies in self.across.values():
            for copy in copies:
                copy.wait_send()


class ZGather:
    def __init__(self, links, buffer):
        x, yh, z, yl, c = here()
        self.links = links
        self.buffer = buffer
        self.right, self.left = z_device(1), z_device(3)
        first, second = buffer.at[z, 0:64], buffer.at[z, 64:128]
        self.right_first = links.send(first, first, self.right)
        self.left_second = links.send(second, second, self.left)
        self.right_second = links.send(second, second, self.right)
        self.left_first = links.send(first, first, self.left)

    def forward(self):
        self.right_first.wait_recv()
        block = self.buffer.at[self.left[2], 0:64]
        self.on_right = self.links.send(block, block, self.right)
        self.left_second.wait_recv()
        block = self.buffer.at[self.right[2], 64:128]
        self.on_left = self.links.send(block, block, self.left)

    def near(self):
        self.right_second.wait_recv()
        self.left_first.wait_recv()

    def far(self):
        self.on_right.wait_recv()
        self.on_left.wait_recv()

    def done(self):
        for copy in (
            self.right_first, self.left_second, self.right_second, self.left_first,
            self.on_right, self.on_left,
        ):
            copy.wait_send()


class ZScatter:
    def __init__(self, links, sends, recv_far, recv_near):
        self.links = links
        self.to_far, self.to_right, self.to_left = (sends.at[i] for i in range(3))
        self.recv_far = recv_far
        self.recv_near = recv_near
        self.right_of, self.left_of = z_device(1), z_device(3)
        self.copies = []
        self.near = []

    def send(self, source, target, device):
        copy = self.links.send(source, target, device)
        self.copies.append(copy)
        return copy

    def far(self, term):
        self.to_far[...] = term.astype(BF16)
        self.far_first = self.send(self.to_far.at[0:64], self.recv_far.at[0], self.right_of)
        self.far_second = self.send(self.to_far.at[64:128], self.recv_far.at[1], self.left_of)

    def right(self, term):
        self.to_right[...] = term.astype(BF16)
        self.near.append(
            self.send(self.to_right.at[64:128], self.recv_near.at[0, 64:128], self.right_of)
        )

    def left(self, term):
        self.to_left[...] = term.astype(BF16)
        self.near.append(
            self.send(self.to_left.at[0:64], self.recv_near.at[1, 0:64], self.left_of)
        )

    def merge(self):
        self.far_first.wait_recv()
        merged = self.to_right[0:64].astype(F32) + self.recv_far[0].astype(F32)
        self.to_right[0:64] = merged.astype(BF16)
        self.near.append(
            self.send(self.to_right.at[0:64], self.recv_near.at[0, 0:64], self.right_of)
        )
        self.far_second.wait_recv()
        merged = self.to_left[64:128].astype(F32) + self.recv_far[1].astype(F32)
        self.to_left[64:128] = merged.astype(BF16)
        self.near.append(
            self.send(self.to_left.at[64:128], self.recv_near.at[1, 64:128], self.left_of)
        )

    def total(self, own):
        for copy in self.near:
            copy.wait_recv()
        return own + self.recv_near[0].astype(F32) + self.recv_near[1].astype(F32)

    def done(self):
        for copy in self.copies:
            copy.wait_send()


class Shrink:
    def __init__(self, links, terms, pair_sum, middle, first_recv, last_recv, y_first):
        self.links = links
        self.terms = terms
        self.pair_sum = pair_sum
        self.middle = middle
        self.first_recv = first_recv
        self.last_recv = last_recv
        self.y_first = y_first
        self.copies = []

    def start(self):
        x, yh, z, yl, c = here()
        self.pair = self.links.send(self.terms.at[:, :, :, 1 - c], self.pair_sum, sibling())

    def send_first(self):
        x, yh, z, yl, c = here()
        self.pair.wait()
        terms, pair_sum = self.terms, self.pair_sum

        @pl.loop(0, 8)
        def _(at):
            h, k = lax.div(at, 4), lax.rem(at, 4)
            for low in range(2):
                pair_sum[h, k, low] = (
                    terms[h, k, low, c].astype(F32) + pair_sum[h, k, low].astype(F32)
                ).astype(BF16)

        self.first = []
        for step in (2, 1, 3):
            if self.y_first:
                device = y_device(step)
                source = pair_sum.at[device[1], :, device[3]]
            else:
                device = x_device(step)
                source = pair_sum.at[:, device[0]]
            self.first.append(self.links.send(source, self.first_recv.at[step - 1], device))

    def send_last(self):
        x, yh, z, yl, c = here()
        for copy in self.first:
            copy.wait()
        got = self.first_recv

        @pl.loop(0, 4)
        def _(at):
            if self.y_first:
                total = self.pair_sum[yh, at, yl].astype(F32)
                for slot in range(3):
                    total = total + got[slot, at].astype(F32)
                self.middle[at] = total.astype(BF16)
            else:
                h, low = lax.div(at, 2), lax.rem(at, 2)
                total = self.pair_sum[h, x, low].astype(F32)
                for slot in range(3):
                    total = total + got[slot, h, low].astype(F32)
                self.middle[h, low] = total.astype(BF16)

        self.second = []
        for step in (2, 1, 3):
            if self.y_first:
                device = x_device(step)
                source = self.middle.at[device[0]]
            else:
                device = y_device(step)
                source = self.middle.at[device[1], device[3]]
            self.second.append(self.links.send(source, self.last_recv.at[step - 1], device))

    def result(self):
        x, yh, z, yl, c = here()
        for copy in self.second:
            copy.wait()
        total = (self.middle[x] if self.y_first else self.middle[yh, yl]).astype(F32)
        for slot in range(3):
            total = total + self.last_recv[slot].astype(F32)
        return total


def shrink_scratch(rows, width, y_first):
    first = (4, rows, width) if y_first else (2, 2, rows, width)
    return [
        pltpu.VMEM((2, 4, 2, rows, width), BF16),
        pltpu.VMEM(first, BF16),
        pltpu.VMEM((3,) + first, BF16),
        pltpu.VMEM((3, rows, width), BF16),
    ]


def everyone():
    return (
        [z_device(s) for s in (1, 2, 3)]
        + [y_device(s) for s in (1, 2, 3)]
        + [x_device(s) for s in (1, 2, 3)]
        + [sibling()]
    )


GELU_A = math.sqrt(2.0 / math.pi)
GELU_B = 0.044715


def gelu_parts(gate):
    square = gate * gate
    curve = jnp.tanh(GELU_A * gate * (1.0 + GELU_B * square))
    half = 0.5 * (1.0 + curve)
    slope = half + 0.5 * gate * (1.0 - curve * curve) * (
        GELU_A * (1.0 + 3.0 * GELU_B * square)
    )
    return gate * half, slope

SCRATCH = dict(
    xn_all=((4, 128, 1024), BF16), wq_all=((2, 2, 2, 4, 64, 256), BF16), wkv_all=((4, 256, 512), BF16),
    q=((2, 4, 2, 128, 128), BF16), cosd=((4, 128, 128), F32), sind=((4, 128, 128), F32),
    kv_all=((2, 2, 2, 4, 2, 128, 256), BF16), attn=((4, 128, 512), BF16),
    recip=((2, 4, 256, 128), F32), wo_all=((2, 2, 2, 4, 64, 256), BF16), acc=((2, 4, 256, 256), F32),
    branch=((128, 1024), F32), h1=((128, 1024), F32), hn_all=((4, 128, 1024), BF16),
    wf_all=((2, 2, 2, 4, 64, 1152), BF16), q_mate=((2, 4, 2, 128, 128), BF16),
    mate_out=((2, 4, 256, 128), BF16), mate_in=((2, 4, 256, 128), BF16),
    sums_out=((2, 4, 1, 256), F32), sums_in=((2, 4, 1, 256), F32),
    inner_out=((2, 4, 1, 256), F32), inner_in=((2, 4, 1, 256), F32),
    d_mate=((2, 4, 256, 256), BF16),
    gate_all=((4, 128, 768), BF16), up_all=((4, 128, 768), BF16), hidden_all=((4, 128, 768), BF16),
    d_mlp_all=((4, 128, 1024), BF16), d_h1=((128, 1024), F32), d_branch_all=((4, 128, 1024), BF16),
    gain_rows=((4, 1, 1024), F32), grads=((4, 128, 1024), BF16),
    d_out=((2, 4, 256, 256), BF16),
    d_kv=((2, 2, 2, 4, 2, 128, 256), BF16), pair_recv=((3, 2, 4, 128, 256), BF16),
    y_recv=((2, 2, 4, 128, 256), BF16),
    kv_send=((4, 8, 512), F32), kv_recv=((4, 8, 512), F32),
    gain_own=((8, 1024), F32), gain_pair=((8, 1024), F32), gain_y=((3, 8, 1024), F32),
    gain_x=((3, 8, 1024), F32), gain_z=((3, 8, 1024), F32),
    own_sum=((128, 1024), F32), z_send=((3, 128, 1024), BF16),
    z_far=((4, 2, 64, 1024), BF16), z_near=((4, 2, 128, 1024), BF16),
    terms_a=((2, 4, 2, 2, 64, 640), BF16), terms_b=((2, 4, 2, 2, 64, 512), BF16),
    terms_k=((2, 4, 2, 2, 32, 256), BF16), terms_v=((2, 4, 2, 2, 32, 256), BF16),
)
SHRINKS = (
    (64, 640, False), (64, 512, False), (64, 128, False), (64, 128, False),
    (64, 128, True), (64, 128, False), (32, 256, True), (32, 256, False),
)
SEMS = 240


class Refs:
    pass


def begin(s, links):
    x, yh, z, yl, c = here()
    xin = s.tokens[...].astype(F32)
    s.xn_all[z] = (xin * inverse_rms(xin) * s.gain_attn_in[...]).astype(BF16)
    greet(everyone())
    ring = ZGather(links, s.xn_all)
    for group in range(2):
        first = pl.multiple_of(group * 512 + z * 128, 128)
        s.wkv_all[yl * 2 + c, :, pl.ds(group * 128, 128)] = quantized(
            s.w_key[:, pl.ds(first, 128)], QEXP_MODEL, 8
        )
        s.wkv_all[yl * 2 + c, :, pl.ds(256 + group * 128, 128)] = quantized(
            s.w_value[:, pl.ds(first, 128)], QEXP_MODEL, 8
        )
    key_part = s.wkv_all.at[yl * 2 + c, :, 0:256]
    value_part = s.wkv_all.at[yl * 2 + c, :, 256:512]
    from_low = links.send(key_part, key_part, y_device(1))
    from_high = links.send(value_part, value_part, y_device(3))
    own = s.wkv_all.at[yl * 2 + c]
    pair = links.send(own, own, sibling())
    s.wq_all[yh, yl, c] = quantized(s.w_query[...], QEXP_MODEL, 8).reshape(4, 64, 256)
    s.gather_q = Gather(links, s.wq_all)
    s.wo_all[yh, yl, c] = quantized(s.w_output[...], QEXP_MODEL, 8).reshape(4, 64, 256)
    s.gather_o = Gather(links, s.wo_all)
    for at, (weight, exponent, bits) in enumerate(
        ((s.w_gate, QEXP_MODEL, 4), (s.w_up, QEXP_MODEL, 4), (s.w_down, QEXP_HIDDEN, 2))
    ):
        s.wf_all[yh, yl, c, :, :, at * 384 : at * 384 + 384] = quantized(
            weight[...], exponent, bits
        ).reshape(4, 64, 384)
    s.gather_f = Gather(links, s.wf_all)
    lane = lax.broadcasted_iota(jnp.int32, (128, 128), 1)
    row = lax.broadcasted_iota(jnp.int32, (128, 128), 0)
    freqs = jnp.exp(lax.rem(lane, 64).astype(F32) * (-2.0 * math.log(THETA) / DH))
    start = s.lengths[0, 0]
    base = yh * 2048 + yl * 256 + c * 128

    def tables(block):
        tok = row + (base + block * 512)
        angle = jnp.where(tok >= start, tok - start, tok).astype(F32) * freqs
        s.cosd[block] = jnp.cos(angle)
        sine = jnp.sin(angle)
        s.sind[block] = jnp.where(lane < 64, -sine, sine)

    tables(0)
    ring.forward()
    tables(1)
    from_low.wait_recv()
    from_high.wait_recv()
    other = s.wkv_all.at[(1 - yl) * 2 + c]
    passed = links.send(other, other, sibling())
    s.gather_q.spread()
    tables(2)
    tables(3)
    pair.wait_recv()
    passed.wait_recv()

    def project_kv(block):
        lin = dot(s.xn_all[block], s.wkv_all[...].reshape(1024, 512))
        cosd, sind = s.cosd[block], s.sind[block]
        for group in range(2):
            key = lin[:, group * 128 : group * 128 + 128]
            key = (key * cosd + swap_halves(key) * sind).astype(BF16)
            value = lin[:, 256 + group * 128 : 384 + group * 128].astype(BF16)
            s.kv_all[group, yh, yl, block, c, :, 0:128] = key
            s.kv_all[group, yh, yl, block, c, :, 128:256] = value

    def project_q(block):
        cosd, sind = s.cosd[block], s.sind[block]
        for group in range(2):
            lin = dot(s.xn_all[block], s.wq_all[group].reshape(1024, 256))
            for head in range(2):
                query = lin[:, head * 128 : head * 128 + 128]
                query = (query * cosd + swap_halves(query) * sind) * (SCALE / CAP)
                s.q[group, block, head] = query.astype(BF16)

    project_kv(z)
    ring.near()
    project_kv(ring.left[2])
    project_kv(ring.right[2])
    ring.far()
    project_kv(lax.rem(z + 2, 4))
    s.kv_pair, s.kv_near, s.kv_far, s.q_send = [], [], [], []
    for group in range(2):
        mine = s.kv_all.at[group, yh, yl, :, c]
        s.kv_pair.append(links.send(mine, mine, sibling()))
        s.kv_near.append(links.send(mine, mine, (x, yh, z, 1 - yl, c)))
        s.kv_far.append(links.plan(mine, mine, mate()))
        s.q_send.append(links.plan(s.q.at[group], s.q_mate.at[group], mate()))

    @pl.when(yh == 0)
    def _():
        for group in range(2):
            s.kv_far[group].start()

    s.gather_o.spread()
    s.gather_q.forward()
    s.gather_q.arrived()
    for block in range(4):
        project_q(block)

    @pl.when(yh == 1)
    def _():
        for group in range(2):
            s.q_send[group].start()

    s.gather_f.spread()
    ring.done()
    for copy in (from_low, from_high, pair, passed):
        copy.wait_send()
    s.gather_q.done()


def attend(s, links):
    x, yh, z, yl, c = here()
    start = s.lengths[0, 0]
    lane = lax.broadcasted_iota(jnp.int32, (1, 256), 1)
    ones = jnp.ones((256, 128), BF16)
    row = lax.rem(lax.broadcasted_iota(jnp.int32, (256, 1), 0), 128)

    def block_sum(query, q_base, group, from_h, from_l, units, diagonal):
        token_q = row + q_base
        floor = jnp.where(token_q >= start, start, 0)
        total = None
        for unit in units:
            both = s.kv_all[group, from_h, from_l, unit].reshape(256, 256)
            token_k = lane + (from_h * 2048 + unit * 512 + from_l * 256)
            curved = jnp.tanh(dot_nt(query, both[:, :128]))
            weight = jnp.exp2(curved * (CAP * LOG2E))
            seen = token_k >= floor
            if diagonal and unit == units[-1]:
                seen = seen & (token_k <= token_q)
            weight = jnp.where(seen, weight, 0.0).astype(BF16)
            term = dot(weight, jnp.concatenate([both[:, 128:], ones], axis=1))
            total = term if total is None else total + term
        return total

    own_base = yh * 2048 + yl * 256 + c * 128
    mate_base = 2048 + (1 - yl) * 256 + c * 128

    def same_half(group, from_l, first):
        for block in range(4):
            total = block_sum(
                s.q[group, block].reshape(256, 128), own_base + block * 512, group, yh, from_l,
                list(range(block + 1)), True,
            )
            if first:
                s.acc[group, block] = total
            else:
                s.acc[group, block] += total

    def far_half(group):
        @pl.loop(0, 4)
        def _(block):
            s.acc[group, block] += block_sum(
                s.q[group, block].reshape(256, 128), own_base + block * 512, group, 0, 1 - yl,
                [0, 1, 2, 3], False,
            )

    def for_mate(group, half):
        @pl.loop(2 * half, 2 * half + 2)
        def _(block):
            total = block_sum(
                s.q_mate[group, block].reshape(256, 128), mate_base + block * 512, group, 0,
                1 - yl, [0, 1, 2, 3], False,
            )
            s.mate_out[group, block] = total[:, :128].astype(BF16)
            s.sums_out[group, block] = total[:, 128:256].T[0:1]

    def pass_plan(group, from_h, from_l):
        block = s.kv_all.at[group, from_h, from_l, :, c]
        return links.plan(block, block, sibling())

    near_pass = [pass_plan(group, yh, 1 - yl) for group in range(2)]
    far_pass = [pass_plan(group, 0, 1 - yl) for group in range(2)]
    back = []
    for group in range(2):
        for half in range(2):
            part = slice(2 * half, 2 * half + 2)
            back.append(
                links.plan(s.mate_out.at[group, part], s.mate_in.at[group, part], mate())
            )
        back.append(links.plan(s.sums_out.at[group], s.sums_in.at[group], mate()))

    @pl.when(yh == 0)
    def _():
        s.mate_in[...] = jnp.zeros_like(s.mate_in)
        s.sums_in[...] = jnp.zeros_like(s.sums_in)

    for group in range(2):
        s.kv_pair[group].wait_recv()
        same_half(group, yl, True)
    s.gather_o.forward()
    for group in range(2):
        s.kv_near[group].wait_recv()
        near_pass[group].start()

        @pl.when(yh == 1)
        def _():
            s.kv_far[group].wait_recv()
            far_pass[group].start()

        near_pass[group].wait_recv()
        same_half(group, 1 - yl, False)

        @pl.when(yh == 1)
        def _():
            far_pass[group].wait_recv()
            far_half(group)

        @pl.when(yh == 0)
        def _():
            s.q_send[group].wait_recv()
            for_mate(group, 0)
            back[3 * group].start()
            for_mate(group, 1)
            back[3 * group + 1].start()
            back[3 * group + 2].start()

    for group in range(2):

        @pl.when(yh == 1)
        def _():
            for copy in back[3 * group : 3 * group + 3]:
                copy.wait_recv()

        for block in range(4):
            total = s.acc[group, block]
            more = jnp.broadcast_to(s.sums_in[group, block], (128, 256)).T
            inverse = 1.0 / (total[:, 128:256] + more)
            s.recip[group, block] = inverse
            out = total[:, :128] + s.mate_in[group, block].astype(F32)
            out = (out * inverse).astype(BF16)
            for head in range(2):
                first = group * 256 + head * 128
                s.attn[block, :, first : first + 128] = out[head * 128 : head * 128 + 128]
    for group in range(2):
        s.kv_pair[group].wait_send()
        s.kv_near[group].wait_send()
        near_pass[group].wait_send()

    @pl.when(yh == 0)
    def _():
        for group in range(2):
            s.kv_far[group].wait_send()
        for copy in back:
            copy.wait_send()

    @pl.when(yh == 1)
    def _():
        for group in range(2):
            far_pass[group].wait_send()
            s.q_send[group].wait_send()


def all_terms(scatter, term_of):
    x, yh, z, yl, c = here()
    scatter.far(term_of(lax.rem(z + 2, 4)))
    scatter.right(term_of(lax.rem(z + 1, 4)))
    scatter.left(term_of(lax.rem(z + 3, 4)))
    own = term_of(z)
    scatter.merge()
    return own


def output_projection(s, links):
    x, yh, z, yl, c = here()

    def term_of(block):
        left = s.attn[block]
        return dot_nt(left[:, :256], s.wo_all[0].reshape(1024, 256)) + dot_nt(
            left[:, 256:], s.wo_all[1].reshape(1024, 256)
        )

    s.gather_o.arrived()
    scatter = ZScatter(links, s.z_send, s.z_far.at[0], s.z_near.at[0])
    own = all_terms(scatter, term_of)
    s.gather_f.forward()
    branch = scatter.total(own)
    h1 = s.tokens[...].astype(F32) + branch * inverse_rms(branch) * s.gain_attn_out[...]
    s.hn_all[z] = (h1 * inverse_rms(h1) * s.gain_mlp_in[...]).astype(BF16)
    s.ring = ZGather(links, s.hn_all)
    s.branch[...] = branch
    s.h1[...] = h1
    s.gather_f.arrived()
    scatter.done()
    s.gather_o.done()
    s.gather_f.done()


def feed_forward(s, links):
    x, yh, z, yl, c = here()

    def term_of(block):
        left = s.hn_all[block]
        total = None
        for group in range(2):
            cols = slice(group * 384, group * 384 + 384)
            gate = dot(left, s.wf_all[group, ..., 0:384].reshape(1024, 384))
            up = dot(left, s.wf_all[group, ..., 384:768].reshape(1024, 384))
            value, slope = gelu_parts(gate)
            s.gate_all[block, :, cols] = value.astype(BF16)
            s.up_all[block, :, cols] = (up * slope).astype(BF16)
            hidden = (value * up).astype(BF16)
            s.hidden_all[block, :, cols] = hidden
            term = dot_nt(hidden, s.wf_all[group, ..., 768:1152].reshape(1024, 384))
            total = term if total is None else total + term
        return total

    s.ring.forward()
    scatter = ZScatter(links, s.z_send, s.z_far.at[1], s.z_near.at[1])
    ring = s.ring
    s.own_sum[...] = term_of(z)
    ring.near()
    scatter.left(term_of(ring.left[2]))
    scatter.right(term_of(ring.right[2]))
    ring.far()
    scatter.far(term_of(lax.rem(z + 2, 4)))
    scatter.merge()
    mlp = scatter.total(s.own_sum[...])
    into, gain_part = rms_back(mlp, s.gain_mlp_out[...], s.out_grad[...].astype(F32))
    s.d_mlp_all[z] = into.astype(BF16)
    s.ring = ZGather(links, s.d_mlp_all)
    s.gain_rows[3] = gain_part
    s.mixed[...] = (s.h1[...] + mlp * inverse_rms(mlp) * s.gain_mlp_out[...]).astype(BF16)
    ring.done()
    scatter.done()


def feed_forward_back(s, links):
    x, yh, z, yl, c = here()

    def term_of(block):
        left = s.d_mlp_all[block]
        total = None
        for group in range(2):
            cols = slice(group * 384, group * 384 + 384)
            d_hidden = dot(left, s.wf_all[group, ..., 768:1152].reshape(1024, 384))
            d_gate = (d_hidden * s.up_all[block, :, cols].astype(F32)).astype(BF16)
            d_up = (d_hidden * s.gate_all[block, :, cols].astype(F32)).astype(BF16)
            s.up_all[block, :, cols] = d_gate
            s.gate_all[block, :, cols] = d_up
            term = dot_nt(d_gate, s.wf_all[group, ..., 0:384].reshape(1024, 384)) + dot_nt(
                d_up, s.wf_all[group, ..., 384:768].reshape(1024, 384)
            )
            total = term if total is None else total + term
        return total

    scatter = ZScatter(links, s.z_send, s.z_far.at[2], s.z_near.at[2])
    ring = s.ring
    s.own_sum[...] = term_of(z)
    ring.forward()
    ring.near()
    scatter.left(term_of(ring.left[2]))
    scatter.right(term_of(ring.right[2]))
    ring.far()
    scatter.far(term_of(lax.rem(z + 2, 4)))
    d_mlp = s.d_mlp_all[...].reshape(512, 1024)
    hn = s.hn_all[...].reshape(512, 1024)
    for group in range(2):
        cols = slice(group * 384, group * 384 + 384)
        down = dot_tn(d_mlp, s.hidden_all[:, :, cols].reshape(512, 384)).astype(BF16)
        s.terms_a[group, :, :, :, :, 0:384] = down.reshape(4, 2, 2, 64, 384)
    scatter.merge()
    for group in range(2):
        cols = slice(group * 384, group * 384 + 384)
        gate = dot_tn(hn, s.up_all[:, :, cols].reshape(512, 384)).astype(BF16)
        gate = gate.reshape(4, 2, 2, 64, 384)
        s.terms_a[group, :, :, :, :, 384:640] = gate[..., 0:256]
        s.terms_b[group, :, :, :, :, 0:128] = gate[..., 256:384]
    d_hn = scatter.total(s.own_sum[...])
    into, gain_part = rms_back(s.h1[...], s.gain_mlp_in[...], d_hn)
    s.gain_rows[2] = gain_part
    d_h1 = s.out_grad[...].astype(F32) + into
    s.d_h1[...] = d_h1
    into, gain_part = rms_back(s.branch[...], s.gain_attn_out[...], d_h1)
    s.d_branch_all[z] = into.astype(BF16)
    s.ring = ZGather(links, s.d_branch_all)
    s.gain_rows[1] = gain_part
    for group in range(2):
        cols = slice(group * 384, group * 384 + 384)
        up = dot_tn(hn, s.gate_all[:, :, cols].reshape(512, 384)).astype(BF16)
        s.terms_b[group, :, :, :, :, 128:512] = up.reshape(4, 2, 2, 64, 384)
    s.ring.forward()
    s.shrink[0].start()
    s.shrink[1].start()
    ring.done()
    scatter.done()


def attend_back(s, links):
    x, yh, z, yl, c = here()
    ring = s.ring
    lane = lax.broadcasted_iota(jnp.int32, (256, 128), 1)

    def extra_lanes(inner):
        high = inner.astype(BF16).astype(F32)
        low = inner - high
        return jnp.where(lane == 0, high, jnp.where(lane == 1, low, 0.0)).astype(BF16)

    def cotangent(block):
        for group in range(2):
            cols = slice(group * 256, group * 256 + 256)
            rows = dot(s.d_branch_all[block], s.wo_all[group].reshape(1024, 256))
            rows = rows.astype(BF16).astype(F32)
            rows = jnp.concatenate([rows[:, :128], rows[:, 128:]], axis=0)
            outs = s.attn[block, :, cols].astype(F32)
            outs = jnp.concatenate([outs[:, :128], outs[:, 128:]], axis=0)
            scaled = (rows * s.recip[group, block]).astype(BF16)
            inner = -jnp.sum(scaled.astype(F32) * outs, axis=1, keepdims=True)
            inner = jnp.broadcast_to(inner, (256, 128))
            s.inner_out[group, block] = inner.T[0:1]
            s.d_out[group, block] = jnp.concatenate([scaled, extra_lanes(inner)], axis=1)

    cotangent(z)
    s.acc[...] = jnp.zeros_like(s.acc)
    ring.near()
    cotangent(ring.left[2])
    cotangent(ring.right[2])
    ring.far()
    cotangent(lax.rem(z + 2, 4))
    lend = []
    for group in range(2):
        lend.append(
            links.plan(
                s.d_out.at[group, :, :, 0:128], s.d_mate.at[group, :, :, 0:128], mate()
            )
        )
        lend.append(links.plan(s.inner_out.at[group], s.inner_in.at[group], mate()))

    @pl.when(yh == 1)
    def _():
        for copy in lend:
            copy.start()

    s.shrink[0].send_first()
    s.shrink[1].send_first()
    d_branch = s.d_branch_all[...].reshape(512, 1024)
    for group in range(2):
        cols = slice(group * 256, group * 256 + 256)
        back = dot_tn(d_branch, s.attn[:, :, cols].reshape(512, 256)).astype(BF16)
        back = back.reshape(4, 2, 2, 64, 256)
        s.terms_a[group, :, :, :, :, 0:128] = back[..., 0:128]
        s.terms_b[group, :, :, :, :, 0:128] = back[..., 128:256]
    s.shrink[2].start()
    s.shrink[3].start()
    start = s.lengths[0, 0]
    ones = jnp.where(lane < 2, 1.0, 0.0).astype(BF16)
    token_row = lax.rem(lax.broadcasted_iota(jnp.int32, (1, 256), 1), 128)
    token_col = lax.broadcasted_iota(jnp.int32, (256, 1), 0)

    own_base = yh * 2048 + yl * 256 + c * 128
    mate_base = 2048 + (1 - yl) * 256 + c * 128

    def unit_back(group, from_h, from_l, unit, first_block, diagonal, lent=False):
        both = s.kv_all[group, from_h, from_l, unit].reshape(256, 256)
        key, value = both[:, :128], both[:, 128:]
        count = 4 - first_block
        queries, cots, base, rows = (
            (s.q_mate, s.d_mate, mate_base, slice(128, 256))
            if lent
            else (s.q, s.d_out, own_base, slice(0, 128))
        )
        query = queries[group, first_block:].reshape(count * 256, 128)
        cot = cots[group, first_block:].reshape(count * 256, 256)
        curved = jnp.tanh(dot_nt(key, query))
        weight = jnp.exp2(curved * (CAP * LOG2E))
        token_k = token_col + (from_h * 2048 + unit * 512 + from_l * 256)
        pieces = []
        for block in range(first_block, 4):
            token_q = token_row + (base + block * 512)
            seen = token_k >= jnp.where(token_q >= start, start, 0)
            if diagonal and block == first_block:
                seen = seen & (token_k <= token_q)
            at = (block - first_block) * 256
            pieces.append(jnp.where(seen, weight[:, at : at + 256], 0.0))
        weight = jnp.concatenate(pieces, axis=1)
        grown = dot_nt(jnp.concatenate([value, ones], axis=1), cot)
        slope = (weight * grown * (1.0 - curved * curved)).astype(BF16)
        d_key = dot(slope, query) * CAP
        d_value = dot(weight.astype(BF16), cot[:, :128])
        both = jnp.concatenate([d_key, d_value], axis=1)
        if lent:
            both = both + s.d_kv[group, from_h, from_l, unit].astype(F32).reshape(256, 256)
        s.d_kv[group, from_h, from_l, unit] = both.astype(BF16).reshape(2, 128, 256)
        d_query = dot(key.T, slope)
        for block in range(first_block, 4):
            at = (block - first_block) * 256
            s.acc[group, block, rows, :] += d_query[:, at : at + 256]

    def same_half(group, from_l):
        for unit in range(4):
            unit_back(group, yh, from_l, unit, unit, True)

    def pair_plan(slot, group, from_h, from_l):
        return links.plan(
            s.d_kv.at[group, from_h, from_l, :, 1 - c], s.pair_recv.at[slot, group], sibling()
        )

    def add_pair(slot, group, from_h, from_l):
        s.d_kv[group, from_h, from_l, :, c] = (
            s.d_kv[group, from_h, from_l, :, c].astype(F32)
            + s.pair_recv[slot, group].astype(F32)
        ).astype(BF16)

    far_pair = [pair_plan(0, group, 0, 1 - yl) for group in range(2)]
    near_pair = [pair_plan(1, group, yh, 1 - yl) for group in range(2)]
    own_pair = [pair_plan(2, group, yh, yl) for group in range(2)]
    far_send = [
        links.plan(s.d_kv.at[group, 0, 1 - yl, :, c], s.y_recv.at[0, group], mate())
        for group in range(2)
    ]
    near_send = [
        links.plan(
            s.d_kv.at[group, yh, 1 - yl, :, c], s.y_recv.at[1, group], (x, yh, z, 1 - yl, c)
        )
        for group in range(2)
    ]
    returned = [
        links.plan(s.mate_out.at[group], s.mate_in.at[group], mate()) for group in range(2)
    ]

    @pl.when(yh == 1)
    def _():
        s.y_recv[0] = jnp.zeros((2, 4, 128, 256), BF16)
        for group in range(2):

            @pl.loop(0, 4)
            def _(unit):
                unit_back(group, 0, 1 - yl, unit, 0, False)

            far_pair[group].start()

    same_half(0, 1 - yl)

    @pl.when(yh == 1)
    def _():
        for group in range(2):
            far_pair[group].wait()
            add_pair(0, group, 0, 1 - yl)
            far_send[group].start()

    same_half(1, 1 - yl)
    for i in (2, 3):
        s.shrink[i].send_first()

    @pl.when(yh == 0)
    def _():
        for group in range(2):
            lend[2 * group].wait_recv()
            lend[2 * group + 1].wait_recv()
            for block in range(4):
                inner = jnp.broadcast_to(s.inner_in[group, block], (128, 256)).T
                s.d_mate[group, block, :, 128:256] = extra_lanes(inner)

            @pl.loop(0, 4)
            def _(unit):
                unit_back(group, 0, 1 - yl, unit, 0, False, True)

            for block in range(4):
                s.mate_out[group, block] = s.acc[group, block, 128:256, :].T.astype(BF16)
            returned[group].start()

    for group in range(2):
        near_pair[group].start()
    same_half(0, yl)
    own_pair[0].start()
    for group in range(2):
        near_pair[group].wait()
        add_pair(1, group, yh, 1 - yl)
        near_send[group].start()
    same_half(1, yl)
    own_pair[1].start()

    @pl.when(yh == 1)
    def _():
        for copy in returned:
            copy.wait_recv()

    def rope_back(values, block):
        return values * s.cosd[block] - swap_halves(values) * s.sind[block]

    for group in range(2):
        for block in range(4):
            d_query = s.acc[group, block, 0:128, :].T + s.mate_in[group, block].astype(F32)
            for head in range(2):
                turned = rope_back(d_query[head * 128 : head * 128 + 128], block) * SCALE
                at = group * 256 + head * 128
                s.grads[block, :, at : at + 128] = turned.astype(BF16)
    xa = s.xn_all[...].reshape(512, 1024)
    for group in range(2):
        back = dot_tn(xa, s.grads[:, :, group * 256 : group * 256 + 256].reshape(512, 256))
        back = back.astype(BF16).reshape(4, 2, 2, 64, 256)
        s.terms_a[group, :, :, :, :, 0:128] = back[..., 0:128]
        s.terms_b[group, :, :, :, :, 0:128] = back[..., 128:256]
    s.shrink[4].start()
    s.shrink[5].start()
    for i in (0, 1, 2, 3):
        s.shrink[i].send_last()
    for i in (4, 5):
        s.shrink[i].send_first()
    for group in range(2):
        own_pair[group].wait()
        near_send[group].wait()

    @pl.when(yh == 0)
    def _():
        for copy in far_send:
            copy.wait_recv()
        for copy in returned:
            copy.wait_send()

    @pl.when(yh == 1)
    def _():
        for copy in far_send + lend:
            copy.wait_send()

    for group in range(2):
        for block in range(4):
            both = (
                s.d_kv[group, yh, yl, block, c].astype(F32)
                + s.pair_recv[2, group, block].astype(F32)
                + s.y_recv[0, group, block].astype(F32)
                + s.y_recv[1, group, block].astype(F32)
            )
            d_key = both[:, :128].astype(BF16).astype(F32)
            at = 512 + group * 128
            s.grads[block, :, at : at + 128] = rope_back(d_key, block).astype(BF16)
            at = 768 + group * 128
            s.grads[block, :, at : at + 128] = both[:, 128:].astype(BF16)
    ring.done()


def finish(s, links):
    x, yh, z, yl, c = here()
    s.gain_own[...] = jnp.zeros_like(s.gain_own)

    def term_of(block):
        left = s.grads[block]
        total = dot_nt(left[:, 512:], s.wkv_all[...].reshape(1024, 512))
        for group in range(2):
            total = total + dot_nt(
                left[:, group * 256 : group * 256 + 256], s.wq_all[group].reshape(1024, 256)
            )
        s.gain_own[0:1] += jnp.sum(total * s.xn_all[block].astype(F32), axis=0, keepdims=True)
        return total

    scatter = ZScatter(links, s.z_send, s.z_far.at[3], s.z_near.at[3])
    xa = s.xn_all[...].reshape(512, 1024)
    back = dot_tn(xa, s.grads[:, :, 512:].reshape(512, 512))
    for k in range(4):
        for h in range(2):
            for low in range(2):
                for core in range(2):
                    rows = [k * 256 + h * 128 + low * 16 + core * 8 + 32 * i for i in range(4)]
                    piece = jnp.concatenate([back[row : row + 8] for row in rows], axis=0)
                    piece = piece.astype(BF16)
                    s.terms_k[h, k, low, core] = piece[:, :256]
                    s.terms_v[h, k, low, core] = piece[:, 256:]
    s.shrink[6].start()
    s.shrink[7].start()
    scatter.far(term_of(lax.rem(z + 2, 4)))
    scatter.right(term_of(lax.rem(z + 1, 4)))
    scatter.left(term_of(lax.rem(z + 3, 4)))
    s.shrink[6].send_first()
    s.shrink[7].send_first()
    scatter.merge()
    own = term_of(z)
    s.gain_own[0:1] = s.gain_own[0:1] / s.gain_attn_in[...]
    for i in (1, 2, 3):
        s.gain_own[i : i + 1] = s.gain_rows[i]
    pair = links.send(s.gain_own, s.gain_pair, sibling())
    for i in (4, 5):
        s.shrink[i].send_last()
    pair.wait()
    s.gain_pair[...] += s.gain_own[...]
    sent = [links.send(s.gain_pair, s.gain_y.at[k - 1], y_device(k)) for k in (2, 1, 3)]
    s.shrink[6].send_last()
    s.shrink[7].send_last()
    for copy in sent:
        copy.wait()
    s.gain_own[...] = s.gain_pair[...] + (s.gain_y[0] + s.gain_y[2]) + s.gain_y[1]
    sent = [links.send(s.gain_own, s.gain_x.at[k - 1], x_device(k)) for k in (2, 1, 3)]
    d_xn = scatter.total(own)
    into, _ = rms_back(s.tokens[...].astype(F32), s.gain_attn_in[...], d_xn)
    s.tokens_grad[...] = (s.d_h1[...] + into).astype(BF16)
    first = s.shrink[0].result()
    s.dwd[...] = first[:, 0:384]
    s.dwg[:, 0:256] = first[:, 384:640]
    second = s.shrink[1].result()
    s.dwg[:, 256:384] = second[:, 0:128]
    s.dwu[...] = second[:, 128:512]
    s.dwo[:, 0:128] = s.shrink[2].result()
    s.dwo[:, 128:256] = s.shrink[3].result()
    for copy in sent:
        copy.wait()
    s.gain_pair[...] = s.gain_own[...] + (s.gain_x[0] + s.gain_x[2]) + s.gain_x[1]
    sent = [links.send(s.gain_pair, s.gain_z.at[k - 1], z_device(k)) for k in (2, 1, 3)]
    s.kv_send[:, :, 0:256] = s.shrink[6].result().reshape(4, 8, 256)
    s.kv_send[:, :, 256:512] = s.shrink[7].result().reshape(4, 8, 256)
    moved = []
    for step in (2, 1, 3):
        device = z_device(step)
        moved.append(links.send(s.kv_send.at[device[2]], s.kv_recv.at[z], device))
    s.kv_recv[z] = s.kv_send[z]
    s.dwq[:, 0:128] = s.shrink[4].result()
    s.dwq[:, 128:256] = s.shrink[5].result()
    for copy in sent:
        copy.wait()
    s.gains[...] = s.gain_pair[...] + (s.gain_z[0] + s.gain_z[2]) + s.gain_z[1]
    for copy in moved:
        copy.wait()
    for origin in range(4):
        for group in range(2):
            at = group * 512 + origin * 128
            s.dwk[:, at : at + 128] = s.kv_recv[origin, :, group * 128 : group * 128 + 128]
            s.dwv[:, at : at + 128] = s.kv_recv[
                origin, :, 256 + group * 128 : 384 + group * 128
            ]
    scatter.done()


OPERANDS = (
    "tokens", "lengths", "w_query", "w_key", "w_value", "w_output", "w_gate", "w_up", "w_down",
    "gain_attn_in", "gain_attn_out", "gain_mlp_in", "gain_mlp_out", "out_grad",
)
RESULTS = dict(
    mixed=((128, 1024), BF16), tokens_grad=((128, 1024), BF16), dwq=((64, 256), F32),
    dwk=((8, 1024), F32), dwv=((8, 1024), F32), dwo=((64, 256), F32), dwg=((64, 384), F32),
    dwu=((64, 384), F32), dwd=((64, 384), F32), gains=((8, 1024), F32),
)


def layer_kernel(*refs):
    s = Refs()
    names = list(OPERANDS) + list(RESULTS) + list(SCRATCH)
    for name, ref in zip(names, refs):
        setattr(s, name, ref)
    rest = refs[len(names) :]
    links = Links(rest[-2], rest[-1])
    terms = (
        s.terms_a, s.terms_b, s.terms_a.at[..., 0:128], s.terms_b.at[..., 0:128],
        s.terms_a.at[..., 0:128], s.terms_b.at[..., 0:128], s.terms_k, s.terms_v,
    )
    s.shrink = [
        Shrink(links, terms[i], *rest[4 * i : 4 * i + 4], SHRINKS[i][2])
        for i in range(len(SHRINKS))
    ]
    begin(s, links)
    attend(s, links)
    output_projection(s, links)
    feed_forward(s, links)
    feed_forward_back(s, links)
    attend_back(s, links)
    finish(s, links)


def run_layer(*operands):
    scratch = [pltpu.VMEM(shape, kind) for shape, kind in SCRATCH.values()]
    for rows, width, y_first in SHRINKS:
        scratch += shrink_scratch(rows, width, y_first)
    scratch += [pltpu.SemaphoreType.DMA((SEMS,))] * 2
    return pl.pallas_call(
        layer_kernel,
        name="layer",
        out_shape=tuple(jax.ShapeDtypeStruct(shape, kind) for shape, kind in RESULTS.values()),
        in_specs=[VM, SM] + [VM] * 12,
        out_specs=tuple(VM for _ in RESULTS),
        scratch_shapes=scratch,
        compiler_params=pltpu.CompilerParams(
            collective_id=1, has_side_effects=True, vmem_limit_bytes=VMEM_LIMIT
        ),
    )(*operands)


def leave_kernel(*refs):
    count = len(refs) // 2
    for i in range(count):
        refs[count + i][...] = refs[i][...]


def run_leave(results):
    return pl.pallas_call(
        leave_kernel,
        name="leave",
        out_shape=tuple(jax.ShapeDtypeStruct(r.shape, r.dtype) for r in results),
        in_specs=[VM] * len(results),
        out_specs=tuple(VM for _ in results),
    )(*results)


def per_device(
    tokens, lengths, w_query, w_key, w_value, w_output, w_gate, w_up, w_down,
    gain_attn_in, gain_attn_out, gain_mlp_in, gain_mlp_out, out_grad,
):
    gain_rows = [
        gain.reshape(1, -1) for gain in (gain_attn_in, gain_attn_out, gain_mlp_in, gain_mlp_out)
    ]
    *results, gains = run_layer(
        tokens, lengths, w_query, w_key, w_value, w_output, w_gate, w_up, w_down,
        *gain_rows, out_grad,
    )
    x, yh, z, yl, c = here()
    first = ((((x * 2 + yh) * 4 + z) * 2 + yl) * 2 + c) * 8
    own_gains = lax.dynamic_slice(gains, (0, first), (4, 8))
    return tuple(run_leave(results)) + tuple(own_gains[i] for i in range(4))


def solution(mesh):
    grid = Mesh(mesh.devices.reshape(4, 2, 4, 2, 2), AXES)
    tokens = P(AXES, None)
    split = P(("yl", "c"), ("yh", "z"))
    rows = P(("yl", "c"), None)
    grads = P(("x", "yl", "c"), ("yh", "z"))
    gains = P(AXES)
    return jax.shard_map(
        per_device,
        mesh=grid,
        in_specs=(tokens, P("x", None), split, rows, rows, split, split, split, split)
        + (P(),) * 4
        + (tokens,),
        out_specs=(tokens, tokens, grads, tokens, tokens, grads, grads, grads, grads)
        + (gains,) * 4,
        check_vma=False,
    )
```
